32 devices in a mesh: dp: 2 (over x), row: 4 (over y, core), col: 4 (over z).
Axes of the slice: x: 2, y: 2, z: 4, core: 2. Of those that a mesh axis runs over, the one named last changes fastest.
Arguments:
- tokens: bfloat16 [8192, 1024], P(('dp', 'col'), 'row'), may hold values from -6 to 6
- segments: int32 [16, 512], P(('dp', 'row')), may hold values from 0 to 7, never falling along the last dimension, each value on 1 to 256 neighbouring positions
- qkv_weight: bfloat16 [1024, 3, 1024], P('row', None, 'col'), may hold values from -0.1875 to 0.1875
- qv_bias: float32 [2, 1024], P(None, 'col'), may hold values from -3 to 3
- out_weight: bfloat16 [1024, 1024], P('col', 'row'), may hold values from -0.75 to 0.75
- out_bias: float32 [1024], replicated, may hold values from -3 to 3
- norm1_gain: float32 [1024], replicated, may hold values from 0.5 to 1.5
- norm1_bias: float32 [1024], replicated, may hold values from -3 to 3
- up_weight: bfloat16 [1024, 4096], P('row', 'col'), may hold values from -0.1875 to 0.1875
- up_bias: float32 [4096], P('col'), may hold values from -3 to 3
- down_weight: bfloat16 [4096, 1024], P('col', 'row'), may hold values from -0.09375 to 0.09375
- down_bias: float32 [1024], replicated, may hold values from -3 to 3
- norm2_gain: float32 [1024], replicated, may hold values from 0.5 to 1.5
- norm2_bias: float32 [1024], replicated, may hold values from -3 to 3
- out_grad: bfloat16 [8192, 1024], P(('dp', 'col'), 'row'), may hold values from -6 to 6
Outputs:
- layer_out: bfloat16 [8192, 1024], P(('dp', 'col'), 'row')
- tokens_grad: float32 [8192, 1024], P(('dp', 'col'), 'row')
- qkv_weight_grad: float32 [1024, 3, 1024], P('row', None, 'col')
- qv_bias_grad: float32 [2, 1024], P(None, 'col')
- out_weight_grad: float32 [1024, 1024], P('col', 'row')
- out_bias_grad: float32 [1024], P('row')
- norm1_gain_grad: float32 [1024], P('row')
- norm1_bias_grad: float32 [1024], P('row')
- up_weight_grad: float32 [1024, 4096], P('row', 'col')
- up_bias_grad: float32 [4096], P('col')
- down_weight_grad: float32 [4096, 1024], P('col', 'row')
- down_bias_grad: float32 [1024], P('row')
- norm2_gain_grad: float32 [1024], P('row')
- norm2_bias_grad: float32 [1024], P('row')
The draws below stay inside these ranges and needn't reach their ends.
Inputs may be any that keep to these rules, and one draw needn't show every extreme that they name: `segments`: within each sequence the document numbers never fall; each document covers 1 to 256 tokens, and one of each draw covers exactly 256.
All inputs are finite; a program needn't handle non-finite values.
Results may differ from the reference program's by a relative error of at most 0.014.
Values may be sent and summed in bfloat16 or wider, within the bound.
A program may use at most 128 MiB of HBM per device.

```python
import math
import jax
import jax.numpy as jnp
import numpy as np
from jax import lax

D = 1024
FF = 4096
HEADS = 16
HEAD = 64
SEQ = 512
DOCS = 8
NSEQ = 16
TOKENS = 8192


def block_scale(rng, dims, pieces, least, largest):
    def one(dim, blocks):
        heights = jax.random.uniform(jax.random.fold_in(jax.random.fold_in(rng, 6), dim), (blocks,), jnp.float32, least / len(pieces), largest / len(pieces))
        return jnp.repeat(jnp.exp(heights), dims[dim] // blocks).reshape((-1,) + (1,) * (len(dims) - dim - 1))

    level = one(*pieces[0])
    for cut in pieces[1:]:
        level = level * one(*cut)
    return level


def profile(count, total, bound, skew):
    portions = [(1 << 20) // math.isqrt(rank ** skew) + 1 for rank in range(2, count + 1)]
    rest, holding = total - bound - (count - 1), [1] * (count - 1)
    while rest > 0:
        movable = [i for i in range(count - 1) if holding[i] < bound]
        whole, left = sum([portions[i] for i in movable]), rest
        for i in movable:
            more = min(bound - holding[i], max(1, left * portions[i] // whole), rest)
            holding[i] = holding[i] + more
            rest = rest - more
    return np.array([bound] + holding)


def uneven_parts(own_key, number_of, total, limit, slope):
    if number_of == 2:
        one = jax.random.randint(own_key, (), max(1, total - limit), min(limit, total - 1) + 1)
        return jnp.stack([one, total - one])
    tallies = jnp.asarray(profile(number_of, total, limit, slope), jnp.int32)
    pairs = (number_of - 1) // 2
    source_of, receiver = tallies[1:1 + 2 * pairs:2], tallies[2:2 + 2 * pairs:2]
    slack = jnp.minimum(source_of - 1, limit - receiver)
    shifted = jax.random.randint(jax.random.fold_in(own_key, 1), (pairs,), 0, 1 << 20) % (slack + 1)
    tallies = tallies.at[1:1 + 2 * pairs:2].set(source_of - shifted).at[2:2 + 2 * pairs:2].set(receiver + shifted)
    return tallies[jax.random.permutation(jax.random.fold_in(own_key, 2), number_of)]


def normal_values(key, shape, deviation, bound, pieces=(), held_as=jnp.bfloat16):
    factor_of = block_scale(key, shape, pieces, -0.22, 0.18) if pieces else 1.0
    values = jax.random.normal(key, shape, jnp.float32) * deviation * factor_of
    return jnp.minimum(jnp.maximum(values, -bound), bound).astype(held_as)


def setup_inputs(seed: int = 0) -> dict:
    key_of = jax.random.split(jax.random.key(seed), 16)
    return {
        "tokens": normal_values(key_of[0], (TOKENS, D), 1.0, 6.0, ((0, 8), (1, 4))),
        "segments": jax.vmap(lambda own: jnp.searchsorted(jnp.cumsum(uneven_parts(own, DOCS, SEQ, SEQ // 2, 2)), jnp.arange(SEQ), side="right"))(jax.random.split(key_of[1], NSEQ)).reshape((NSEQ, SEQ)).astype(jnp.int32),
        "qkv_weight": normal_values(key_of[2], (D, 3, D), D ** -0.5, 0.1875, ((0, 4), (2, 4))),
        "qv_bias": normal_values(key_of[3], (2, D), 0.5, 3.0, ((1, 4),), jnp.float32),
        "out_weight": normal_values(key_of[4], (D, D), (D // 16) ** -0.5, 0.75, ((0, 4), (1, 4))),
        "out_bias": normal_values(key_of[5], (D,), 0.5, 3.0, (), jnp.float32),
        "norm1_gain": jnp.clip(1.0 + 0.1 * jax.random.normal(key_of[6], (D,), jnp.float32), 0.5, 1.5),
        "norm1_bias": normal_values(key_of[7], (D,), 0.5, 3.0, (), jnp.float32),
        "up_weight": normal_values(key_of[8], (D, FF), D ** -0.5, 0.1875, ((0, 4), (1, 4))),
        "up_bias": normal_values(key_of[9], (FF,), 0.5, 3.0, ((0, 4),), jnp.float32),
        "down_weight": normal_values(key_of[10], (FF, D), FF ** -0.5, 0.09375, ((0, 4), (1, 4))),
        "down_bias": normal_values(key_of[11], (D,), 0.5, 3.0, (), jnp.float32),
        "norm2_gain": jnp.clip(1.0 + 0.1 * jax.random.normal(key_of[12], (D,), jnp.float32), 0.5, 1.5),
        "norm2_bias": normal_values(key_of[13], (D,), 0.5, 3.0, (), jnp.float32),
        "out_grad": normal_values(key_of[14], (TOKENS, D), 1.0, 6.0, ((0, 8), (1, 4))),
    }


EPS = 1e-05
HIGHEST_PRECISION = lax.Precision.HIGHEST

@jax.custom_vjp
def low(v):
    return lax.optimization_barrier(v.astype(jnp.bfloat16)).astype(jnp.float32)

@jax.custom_vjp
def low_back(v):
    return v

def low_keep(v):
    return (low(v), None)

def low_pass(kept, grad):
    return (grad,)

def back_keep(v):
    return (v, None)

def back_low(kept, grad):
    return (low(grad),)
low.defvjp(low_keep, low_pass)
low_back.defvjp(back_keep, back_low)

def product(left, right):
    return jnp.dot(left, right, precision=HIGHEST_PRECISION, preferred_element_type=jnp.float32)

def layer_norm(summed, gain, offset):
    center = lax.optimization_barrier(jnp.mean(summed, axis=-1, keepdims=True))
    spread = lax.optimization_barrier(jnp.mean(summed * summed, axis=-1, keepdims=True)) - center * center
    return (summed - center) * lax.rsqrt(spread + EPS) * gain + offset

def attend(packed):
    queries, keys_in, values_in, labels = packed
    scale_factor = float(HEAD) ** (-0.5)
    scores = jnp.einsum('qhe,khe->hqk', queries, keys_in, precision=HIGHEST_PRECISION) * scale_factor
    scores = low_back(scores)
    same_doc = labels[:, None] == labels[None, :]
    scores = jnp.where(same_doc[None], scores, -1e+30)
    probs = jax.nn.softmax(scores, axis=-1)
    return jnp.einsum('hqk,khe->qhe', low(probs), values_in, precision=HIGHEST_PRECISION)

def forward(weights_all, inputs, labels):
    qkv_weight, qv_bias, out_weight, out_bias, norm1_gain, norm1_bias, up_weight, up_bias, down_weight, down_bias, norm2_gain, norm2_bias = weights_all
    row_total = inputs.shape[0]
    projected = product(inputs, qkv_weight.reshape(D, 3 * D))
    bias_rows = jnp.stack([qv_bias[0], jnp.zeros_like(qv_bias[0]), qv_bias[1]]).reshape(1, 3 * D)
    projected = low(low_back(projected + bias_rows))
    projected = projected.reshape(row_total // SEQ, SEQ, 3, HEADS, HEAD)
    context = lax.map(jax.checkpoint(attend), (projected[:, :, 0], projected[:, :, 1], projected[:, :, 2], labels))
    context = low(low_back(context.reshape(row_total, D)))
    attended = low_back(product(context, out_weight) + out_bias)
    hidden = layer_norm(inputs + attended, norm1_gain, norm1_bias)
    upward = low_back(product(low(hidden), up_weight) + up_bias)
    activated = low(jax.nn.gelu(upward, approximate=False))
    downward = low_back(product(activated, down_weight) + down_bias)
    return layer_norm(hidden + downward, norm2_gain, norm2_bias)

def reference(tokens, segments, qkv_weight, qv_bias, out_weight, out_bias, norm1_gain, norm1_bias, up_weight, up_bias, down_weight, down_bias, norm2_gain, norm2_bias, out_grad):
    weights_all = (qkv_weight.astype(jnp.float32), qv_bias.astype(jnp.float32), out_weight.astype(jnp.float32), out_bias.astype(jnp.float32), norm1_gain.astype(jnp.float32), norm1_bias.astype(jnp.float32), up_weight.astype(jnp.float32), up_bias.astype(jnp.float32), down_weight.astype(jnp.float32), down_bias.astype(jnp.float32), norm2_gain.astype(jnp.float32), norm2_bias.astype(jnp.float32))
    block_seqs = 8
    block_count = NSEQ // block_seqs
    inputs = tokens.astype(jnp.float32).reshape(block_count, block_seqs * SEQ, D)
    labels = segments.reshape(block_count, block_seqs, SEQ)
    cotangents = out_grad.astype(jnp.float32).reshape(block_count, block_seqs * SEQ, D)

    def accumulate(totals, packed):
        block_in, block_labels, block_cot = packed

        def local_forward(weights_now, inputs_now):
            return forward(weights_now, inputs_now, block_labels)
        result, pullback = jax.vjp(local_forward, weights_all, block_in)
        grad_weights, grad_inputs = pullback(block_cot)
        return (jax.tree.map(jnp.add, totals, grad_weights), (result, grad_inputs))
    zeros_all = jax.tree.map(jnp.zeros_like, weights_all)
    totals, (results, grads_in) = lax.scan(accumulate, zeros_all, (inputs, labels, cotangents))
    return (results.reshape(TOKENS, D).astype(jnp.bfloat16), grads_in.reshape(TOKENS, D), totals[0], totals[1], totals[2], totals[3], totals[4], totals[5], totals[6], totals[7], totals[8], totals[9], totals[10], totals[11])
```

```python
import functools

import jax
import jax.numpy as jnp
from jax import lax
from jax.experimental import pallas as pl
from jax.experimental.pallas import tpu as pltpu
from jax.sharding import PartitionSpec as P

D = 1024
HEAD = 64
SEQ = 512
EPS = 1e-05
MESH = pl.DeviceIdType.MESH
BF = jnp.bfloat16
F32 = jnp.float32
ROWS = 128


def dot(left, right, left_dim, right_dim):
    return lax.dot_general(
        left, right, (((left_dim,), (right_dim,)), ((), ())), preferred_element_type=F32
    )


def al(index, step):
    return pl.multiple_of(index * step, step)


def col_sum(values):
    return jnp.sum(values, 0, keepdims=True)


def layer_kernel(
    seg_in,
    x_in,
    og_in,
    wq_in,
    wo_in,
    wu_in,
    wd_in,
    bias_in,
    vecs,
    lo_out,
    tg_out,
    fin_q,
    fin_o,
    fin_u,
    fin_d,
    vec_out,
    seg,
    biases,
    xf,
    wq,
    wo,
    wu,
    wd,
    proj,
    probs,
    ctx,
    mask,
    part,
    rsc,
    rsy,
    ysend,
    normed1,
    inv1,
    hf,
    act,
    gelup,
    og,
    lo,
    gsec,
    gdf,
    gu,
    gaf,
    gctx,
    gproj,
    partf,
    rscf,
    rsyf,
    ysendf,
    tg,
    gq,
    go,
    gup,
    gd,
    xq,
    xo,
    xu,
    xd,
    zq,
    zo,
    zu,
    zd,
    ss,
    rs,
    ls,
):
    d = lax.axis_index("dp")
    r = lax.axis_index("row")
    c = lax.axis_index("col")
    y = r // 2
    k = r % 2
    p = d % 2
    r1 = r + 1 - 2 * k
    r2 = (r + 2) % 4
    r3 = (r1 + 2) % 4
    kc = c // 2
    ic = c % 2
    is_agg = k == kc
    core_dev = (d, r1, c)
    y_dev = (d, r2, c)
    x_dev = (d + 1 - 2 * p, r, c)

    counts = {"s": 0, "r": 0, "l": 0}

    def new(kind, n=1):
        at = counts[kind]
        counts[kind] += n
        return at

    def remote(si, ri, src, dst, dev):
        return pltpu.make_async_remote_copy(
            src_ref=src,
            dst_ref=dst,
            send_sem=ss.at[si],
            recv_sem=rs.at[ri],
            device_id=dev,
            device_id_type=MESH,
        )

    late = []

    def later(copy, condition=None):
        late.append((condition, copy))

    barrier = pltpu.get_barrier_semaphore()
    for j in (1, 2, 3):
        pl.semaphore_signal(barrier, inc=1, device_id=(d, (r + j) % 4, c), device_id_type=MESH)
        pl.semaphore_signal(barrier, inc=1, device_id=(d, r, (c + j) % 4), device_id_type=MESH)
    pl.semaphore_signal(barrier, inc=1, device_id=x_dev, device_id_type=MESH)

    @pl.when(r != c)
    def _():
        pl.semaphore_signal(barrier, inc=1, device_id=(d, c, r), device_id_type=MESH)
        pl.semaphore_wait(barrier, 8)

    @pl.when(r == c)
    def _():
        pl.semaphore_wait(barrier, 7)

    def qkv_piece(yp):
        return wq_in.at[:, :, pl.ds(al(yp, 384), 384)]

    def out_piece(yp):
        return wo_in.at[yp]

    def up_piece(yp):
        return wu_in.at[:, :, pl.ds(al(yp, 512), 512)]

    def down_piece(yp):
        return wd_in.at[yp]

    def qkv_place(row):
        return wq.at[row, :, :, pl.ds(al(ic, 384), 384)]

    def out_place(row):
        return wo.at[ic, :, :, pl.ds(al(row, 256), 256)]

    def up_place(row):
        return wu.at[row, :, :, pl.ds(al(ic, 512), 512)]

    def down_place(row):
        return wd.at[ic, :, :, pl.ds(al(row, 256), 256)]

    def qkv_half(ref, half, ci):
        return ref.at[:, half, :, pl.ds(al(ci, 384), 384)]

    def out_half(ref, half, ci):
        return ref.at[ci, half]

    def up_half(ref, half, ci):
        return ref.at[:, half, :, pl.ds(al(ci, 512), 512)]

    def down_half(ref, half, ci):
        return ref.at[ci, half]

    class Weight:
        def __init__(self, buffer, piece, place, half):
            self.buffer, self.piece, self.place, self.half = buffer, piece, place, half
            self.s1, self.r1, self.l1 = new("s", 2), new("r", 4), new("l")
            self.s2, self.r2 = new("s", 3), new("r", 4)
            self.s3, self.r3 = new("s", 2), new("r", 2)

        def spread_rows(self):
            other = remote(
                self.s1, self.r1 + r, self.piece(1 - y), self.place(r), (d, 2 * (1 - y) + kc, c)
            )
            other.start()
            later(other)
            near = remote(self.s1 + 1, self.r1 + r, self.piece(y), self.place(r), core_dev)
            own = pltpu.make_async_copy(self.piece(y), self.place(r), ls.at[self.l1])

            @pl.when(jnp.logical_not(is_agg))
            def _():
                near.start()

            later(near, jnp.logical_not(is_agg))

            @pl.when(is_agg)
            def _():
                own.start()

            self.own = own

        def spread_cols(self):
            copies = []
            for j in (1, 2, 3):
                region = self.half(self.buffer, p, ic)
                copies.append(
                    remote(self.s2 + j - 1, self.r2 + c, region, region, (d, r, (c + j) % 4))
                )

            @pl.when(is_agg)
            def _():
                self.own.wait()
                for j in (1, 2, 3):
                    row = (r + j) % 4
                    remote(
                        self.s1, self.r1 + row, self.place(row), self.place(row), core_dev
                    ).wait_recv()
                for copy in copies:
                    copy.start()

            for copy in copies:
                later(copy, is_agg)

        def spread_pair(self):
            for ci in (0, 1):
                source = 2 * k + ci
                region = self.half(self.buffer, p, ci)
                copy = remote(self.s3 + ci, self.r3 + ci, region, region, x_dev)

                @pl.when(source != c)
                def _():
                    remote(self.s2, self.r2 + source, region, region, x_dev).wait_recv()
                    copy.start()

                later(copy, source != c)

        def ready(self):
            for ci in (0, 1):
                region = self.half(self.buffer, 1 - p, ci)

                @pl.when(2 * k + ci != c)
                def _():
                    remote(self.s3 + ci, self.r3 + ci, region, region, x_dev).wait_recv()

    w_qkv = Weight(wq, qkv_piece, qkv_place, qkv_half)
    w_out = Weight(wo, out_piece, out_place, out_half)
    w_up = Weight(wu, up_piece, up_place, up_half)
    w_down = Weight(wd, down_piece, down_place, down_half)

    def rows_of(ref, s, row):
        return ref.at[s, pl.ds(al(row, ROWS), ROWS), :]

    def slab_of(ref, s, row):
        return ref.at[s, :, pl.ds(al(row, 256), 256)]

    class Gather:
        def __init__(self, full, at, s, source=None):
            self.full, self.at, self.s = full, at, s
            self.source = source
            self.si, self.ri = new("s", 3), new("r", 3)

        def send(self):
            mine = self.source if self.source is not None else self.at(self.full, self.s, r)
            place = self.at(self.full, self.s, r)
            for n, dev in ((0, y_dev), (1, core_dev)):
                copy = remote(self.si + n, self.ri + n, mine, place, dev)
                copy.start()
                later(copy)

        def forward(self):
            place = self.at(self.full, self.s, r2)
            remote(self.si, self.ri, place, place, y_dev).wait_recv()
            copy = remote(self.si + 2, self.ri + 2, place, place, core_dev)
            copy.start()
            later(copy)

        def wait(self):
            near = self.at(self.full, self.s, r1)
            remote(self.si, self.ri + 1, near, near, core_dev).wait_recv()
            far = self.at(self.full, self.s, r3)
            remote(self.si, self.ri + 2, far, far, core_dev).wait_recv()

    class Scatter:
        def __init__(self, source, at, core_recv, y_send, y_recv, s):
            self.source, self.at = source, at
            self.core_recv, self.y_send, self.y_recv, self.s = core_recv, y_send, y_recv, s
            si, ri = new("s", 3), new("r", 3)
            self.far = remote(si, ri, at(source, s, r3), core_recv.at[s, 1], core_dev)
            self.near = remote(si + 1, ri + 1, at(source, s, r1), core_recv.at[s, 0], core_dev)
            self.cross = remote(si + 2, ri + 2, y_send.at[s], y_recv.at[s], y_dev)

        def to_core(self):
            self.far.start()
            self.near.start()

        def to_y(self):
            self.far.wait_recv()
            total = self.at(self.source, self.s, r2)[...].astype(F32)
            self.y_send[self.s] = (total + self.core_recv[self.s, 1].astype(F32)).astype(BF)
            self.cross.start()

        def result(self):
            self.near.wait_recv()
            total = self.at(self.source, self.s, r)[...].astype(F32)
            total = total + self.core_recv[self.s, 0].astype(F32)
            self.cross.wait_recv()
            return total + self.y_recv[self.s].astype(F32)

        def sent(self):
            self.far.wait_send()
            self.near.wait_send()
            self.cross.wait_send()

    w_qkv.spread_rows()
    x_gather = [Gather(xf, slab_of, s, x_in.at[s]) for s in (0, 1)]
    x_own = [
        pltpu.make_async_copy(x_in.at[s], slab_of(xf, s, r), ls.at[new("l")]) for s in (0, 1)
    ]
    seg_s, seg_r, seg_l = new("s"), new("r"), new("l")
    seg_copy = remote(seg_s, seg_r, seg_in, seg, (d, c, r))
    seg_own = pltpu.make_async_copy(seg_in, seg, ls.at[seg_l])

    @pl.when(r != c)
    def _():
        seg_copy.start()

    @pl.when(r == c)
    def _():
        seg_own.start()

    bias_s, bias_r = new("s", 3), new("r", 4)
    for j in (1, 2, 3):
        copy = remote(
            bias_s + j - 1, bias_r + c, bias_in, biases.at[c], (d, r, (c + j) % 4)
        )
        copy.start()
        later(copy)
    biases[c] = bias_in[...]
    for s in (0, 1):
        x_gather[s].send()
        x_own[s].start()

    w_qkv.spread_cols()
    w_out.spread_rows()
    w_up.spread_rows()
    x_gather[0].forward()
    w_qkv.spread_pair()
    x_gather[1].forward()
    w_out.spread_cols()
    w_up.spread_cols()
    w_down.spread_rows()

    og_s, og_r, og_l = new("s", 3), new("r", 4), new("l")

    def og_place(row):
        return og.at[:, :, pl.ds(al(row, 256), 256)]

    og_own = pltpu.make_async_copy(og_in.at[:, pl.ds(al(r, ROWS), ROWS), :], og_place(r), ls.at[og_l])
    og_own.start()
    for j in (1, 2, 3):
        row = (r + j) % 4
        copy = remote(
            og_s + j - 1,
            og_r + r,
            og_in.at[:, pl.ds(al(row, ROWS), ROWS), :],
            og_place(r),
            (d, row, c),
        )
        copy.start()
        later(copy)

    for j in (1, 2, 3):
        source = (c + j) % 4
        remote(bias_s, bias_r + source, biases.at[source], biases.at[source], core_dev).wait_recv()

    @pl.when(r != c)
    def _():
        seg_copy.wait_recv()

    @pl.when(r == c)
    def _():
        seg_own.wait()

    later(seg_copy, r != c)
    w_qkv.ready()

    vec_out[...] = jnp.zeros_like(vec_out)

    def project(s):
        rows = xf[s]

        def half(ci, carry):
            weight = wq[:, :, :, pl.ds(al(ci, 384), 384)].reshape(D, 384)
            q_bias = biases[2 * k + ci, 1:2, pl.ds(al(y, 128), 128)]
            v_bias = biases[2 * k + ci, 1:2, pl.ds(pl.multiple_of(256 + y * 128, 128), 128)]
            bias = jnp.concatenate([q_bias, jnp.zeros_like(q_bias), v_bias], 1)
            proj[s, :, pl.ds(al(ci, 384), 384)] = (dot(rows, weight, 1, 0) + bias).astype(BF)
            return carry

        lax.fori_loop(0, 2, half, 0)

    def columns(ci, n):
        return pl.ds(pl.multiple_of(ci * 384 + n * 128, 128), 128)

    def attend(s):
        labels = seg[s : s + 1, :]
        down = jnp.transpose(jnp.broadcast_to(labels, (128, SEQ)))[:, 0:1]
        mask[...] = jnp.where(down == labels, 0.0, -1e30)
        lane = lax.broadcasted_iota(jnp.int32, (SEQ, 128), 1)
        row = lax.broadcasted_iota(jnp.int32, (128, SEQ), 0)

        def pair(ci, carry):
            queries = proj[s, :, columns(ci, 0)]
            keys_in = proj[s, :, columns(ci, 1)]
            values_in = proj[s, :, columns(ci, 2)]
            parts = []
            for h in (0, 1):
                chosen = (lane < HEAD) if h == 0 else (lane >= HEAD)
                masked = jnp.where(chosen, queries, jnp.zeros_like(queries))
                scores = dot(keys_in, masked, 1, 1) * (float(HEAD) ** (-0.5)) + mask[...]
                weights = jnp.exp(scores - jnp.max(scores, 0, keepdims=True))
                totals = jnp.sum(weights, 0, keepdims=True)
                share = (weights * (1.0 / totals)).astype(BF)
                probs[s, ci * 2 + h] = share
                parts.append(dot(values_in, share, 0, 0))
            both = jnp.where(row < HEAD, parts[0], parts[1])
            ctx[s, :, pl.ds(al(ci, 128), 128)] = jnp.transpose(both).astype(BF)
            return carry

        lax.fori_loop(0, 2, pair, 0)

    def out_partial(s):
        part[s] = dot(ctx[s], wo[...].reshape(256, D), 1, 0).astype(BF)

    def norm_stats(summed):
        center = jnp.sum(summed, 1, keepdims=True) * (1.0 / D)
        spread = jnp.sum(summed * summed, 1, keepdims=True) * (1.0 / D) - center * center
        inverse = lax.rsqrt(spread + EPS)
        return (summed - center) * inverse, inverse

    def norm_pull(grad, normed, inverse, gain):
        scaled = grad * gain
        first = jnp.sum(scaled, 1, keepdims=True) * (1.0 / D)
        second = jnp.sum(scaled * normed, 1, keepdims=True) * (1.0 / D)
        return inverse * (scaled - first - normed * second)

    out_bias, gain1, offset1 = vecs[0:1, :], vecs[1:2, :], vecs[2:3, :]
    down_bias, gain2, offset2 = vecs[3:4, :], vecs[4:5, :], vecs[5:6, :]
    own_rows = pl.ds(al(r, ROWS), ROWS)

    def scatters():
        return [Scatter(part, rows_of, rsc, ysend, rsy, s) for s in (0, 1)]

    rs1 = scatters()
    ag1 = [Gather(hf, rows_of, s) for s in (0, 1)]

    def first_norm(s):
        first_sum = rs1[s].result() + out_bias + xf[s, own_rows, :].astype(F32)
        normed, inverse = norm_stats(first_sum)
        normed1[s] = normed
        inv1[s] = jnp.broadcast_to(inverse, (ROWS, 128))
        hf[s, own_rows, :] = (normed * gain1 + offset1).astype(BF)
        ag1[s].send()

    for s in (0, 1):
        if s == 0:
            x_own[0].wait()
            x_gather[0].wait()
        else:
            x_own[1].wait()
            x_gather[1].wait()
        project(s)
        if s == 0:
            w_out.spread_pair()
            w_down.spread_cols()
        attend(s)
        if s == 0:
            w_out.ready()
        else:
            w_up.spread_pair()
        out_partial(s)
        rs1[s].to_core()
        rs1[s].to_y()
    first_norm(0)
    ag1[0].forward()
    first_norm(1)
    w_down.spread_pair()
    w_up.ready()
    ag1[0].wait()

    def up_bias_of(ci):
        return biases[2 * k + ci, 0:1, pl.ds(al(y, 512), 512)]

    def mlp_up(s):
        rows = hf[s]

        def tile(n, carry):
            cols = pl.ds(al(n, 256), 256)
            weight = wu[:, :, :, cols].reshape(D, 256)
            ci = n // 2
            bias = biases[2 * k + ci, 0:1, pl.ds(pl.multiple_of(y * 512 + (n % 2) * 256, 256), 256)]
            upward = dot(rows, weight, 1, 0) + bias
            share = 0.5 + 0.5 * lax.erf(upward * 0.7071067811865476)
            act[s, :, cols] = (upward * share).astype(BF)
            density = jnp.exp(-0.5 * upward * upward) * 0.3989422804014327
            gelup[s, :, cols] = (share + upward * density).astype(BF)
            return carry

        lax.fori_loop(0, 4, tile, 0)

    def mlp_down(s):
        rows = act[s]

        def tile(n, carry):
            cols = pl.ds(al(n, 256), 256)
            weight = wd[:, :, :, cols].reshape(D, 256)
            part[s, :, cols] = dot(rows, weight, 1, 0).astype(BF)
            return carry

        lax.fori_loop(0, 4, tile, 0)

    rs2 = scatters()
    ag2 = [Gather(gdf, rows_of, s) for s in (0, 1)]
    lo_s, lo_r, lo_l = new("s", 6), new("r", 8), new("l", 2)

    og_own.wait()
    for j in (1, 2, 3):
        source = (r + j) % 4
        remote(og_s, og_r + source, og_place(source), og_place(source), core_dev).wait_recv()

    def second_norm(s):
        hidden = normed1[s] * gain1 + offset1
        second_sum = rs2[s].result() + down_bias + hidden
        normed, inverse = norm_stats(second_sum)
        lo[s] = (normed * gain2 + offset2).astype(BF)
        grad = og[s].astype(F32)
        vec_out[0:1, :] += col_sum(grad * normed)
        vec_out[1:2, :] += col_sum(grad)
        grad_second = norm_pull(grad, normed, inverse, gain2)
        gsec[s] = grad_second
        rounded = grad_second.astype(BF)
        vec_out[4:5, :] += col_sum(rounded.astype(F32))
        gdf[s, own_rows, :] = rounded
        ag2[s].send()

    def lo_place(s, row):
        return lo_out.at[s, pl.ds(al(row, ROWS), ROWS), :]

    def lo_part(s, row):
        return lo.at[s, :, pl.ds(al(row, 256), 256)]

    lo_own = [
        pltpu.make_async_copy(lo_part(s, r), lo_place(s, r), ls.at[lo_l + s]) for s in (0, 1)
    ]

    def send_lo(s):
        lo_own[s].start()
        for j in (1, 2, 3):
            row = (r + j) % 4
            copy = remote(
                lo_s + 3 * s + j - 1, lo_r + 4 * s + r, lo_part(s, row), lo_place(s, r), (d, row, c)
            )
            copy.start()
            later(copy)

    for s in (0, 1):
        if s == 1:
            ag1[1].wait()
        mlp_up(s)
        if s == 0:
            ag1[1].forward()
            w_down.ready()
        rs1[s].sent()
        mlp_down(s)
        rs2[s].to_core()
        rs2[s].to_y()
    second_norm(0)
    ag2[0].forward()
    second_norm(1)
    ag2[0].wait()

    def pull_act(s):
        rows = gdf[s]

        def tile(n, carry):
            cols = pl.ds(al(n, 256), 256)
            grad = dot(rows, wd[n // 2, n % 2], 1, 1) * gelup[s, :, cols].astype(F32)
            rounded = grad.astype(BF)
            gu[s, :, cols] = rounded
            vec_out[6:7, cols] += col_sum(rounded.astype(F32))
            return carry

        lax.fori_loop(0, 4, tile, 0)

    def pull_hidden(s):
        rows = gu[s]

        def tile(n, carry):
            weight = wu[n].reshape(256, D)
            part[s, :, pl.ds(al(n, 256), 256)] = dot(rows, weight, 1, 1).astype(BF)
            return carry

        lax.fori_loop(0, 4, tile, 0)

    rs3 = scatters()
    ag3 = [Gather(gaf, rows_of, s) for s in (0, 1)]

    def first_norm_pull(s):
        grad = gsec[s] + rs3[s].result()
        normed = normed1[s]
        vec_out[2:3, :] += col_sum(grad * normed)
        vec_out[3:4, :] += col_sum(grad)
        rounded = norm_pull(grad, normed, inv1[s][:, 0:1], gain1).astype(BF)
        vec_out[5:6, :] += col_sum(rounded.astype(F32))
        gaf[s, own_rows, :] = rounded
        ag3[s].send()

    for s in (0, 1):
        if s == 1:
            ag2[1].wait()
        pull_act(s)
        if s == 0:
            ag2[1].forward()
        rs2[s].sent()
        pull_hidden(s)
        rs3[s].to_core()
        rs3[s].to_y()
        send_lo(s)

    class Grad:
        def __init__(self, buffer, half, pair_half, pair_recv, col_recv, piece, place, fin_half):
            self.buffer, self.half, self.pair_half = buffer, half, pair_half
            self.pair_recv, self.col_recv = pair_recv, col_recv
            self.piece, self.place, self.fin_half = piece, place, fin_half
            self.s1, self.r1 = new("s"), new("r")
            self.s2, self.r2 = new("s", 2), new("r", 3)
            self.s3, self.r3, self.l3 = new("s", 3), new("r", 2), new("l")
            self.s4, self.r4 = new("s"), new("r")
            self.pair = remote(
                self.s1, self.r1, self.pair_half(self.buffer, 1 - p), self.pair_recv, x_dev
            )

        def to_pair(self):
            self.pair.start()
            later(self.pair)

        def to_cols(self):
            self.pair.wait_recv()
            mine = self.pair_half(self.buffer, p)
            mine[...] = (mine[...].astype(F32) + self.pair_recv[...].astype(F32)).astype(BF)
            for ci in (0, 1):
                owner = 2 * k + ci
                slot = (c - owner + 3) % 4
                copy = remote(
                    self.s2 + ci,
                    self.r2 + slot,
                    self.half(self.buffer, p, ci),
                    self.col_recv.at[slot],
                    (d, r, owner),
                )

                @pl.when(owner != c)
                def _():
                    copy.start()

                later(copy, owner != c)

        def to_rows(self):
            own = pltpu.make_async_copy(self.piece(r), self.place(y), ls.at[self.l3])
            self.own = own
            copies = []
            for j in (1, 2, 3):
                row = (r + j) % 4
                copies.append(
                    remote(self.s3 + j - 1, self.r3 + y, self.piece(row), self.place(y), (d, row, c))
                )

            @pl.when(is_agg)
            def _():
                for slot in (0, 1, 2):
                    dst = self.col_recv.at[slot]
                    remote(self.s2, self.r2 + slot, dst, dst, core_dev).wait_recv()
                mine = self.half(self.buffer, p, ic)
                total = mine[...].astype(F32)
                for slot in (0, 1, 2):
                    total = total + self.col_recv[slot].astype(F32)
                mine[...] = total.astype(BF)
                own.start()
                for copy in copies:
                    copy.start()

            for copy in copies:
                later(copy, is_agg)

        def to_pair_again(self):
            @pl.when(is_agg)
            def _():
                self.own.wait()
                place = self.place(1 - y)
                remote(self.s3, self.r3 + 1 - y, place, place, core_dev).wait_recv()

            @pl.when(jnp.logical_not(is_agg))
            def _():
                for yp in (0, 1):
                    place = self.place(yp)
                    remote(self.s3, self.r3 + yp, place, place, core_dev).wait_recv()

            self.last = remote(self.s4, self.r4, self.fin_half(p), self.fin_half(p), x_dev)
            self.last.start()
            later(self.last)

        def done(self):
            dst = self.fin_half(1 - p)
            remote(self.s4, self.r4, dst, dst, x_dev).wait_recv()

    def lead_half(ref, half):
        return ref.at[:, half]

    g_qkv = Grad(
        gq,
        qkv_half,
        lead_half,
        xq,
        zq,
        lambda row: gq.at[row, p, :, pl.ds(al(ic, 384), 384)],
        lambda yp: fin_q.at[p, :, pl.ds(al(yp, 384), 384)],
        lambda half: fin_q.at[half],
    )
    g_out = Grad(
        go,
        out_half,
        lead_half,
        xo,
        zo,
        lambda row: go.at[ic, p, :, pl.ds(al(row, 256), 256)],
        lambda yp: fin_o.at[yp, p],
        lambda half: fin_o.at[:, half],
    )
    g_up = Grad(
        gup,
        up_half,
        lead_half,
        xu,
        zu,
        lambda row: gup.at[row, p, :, pl.ds(al(ic, 512), 512)],
        lambda yp: fin_u.at[p, :, pl.ds(al(yp, 512), 512)],
        lambda half: fin_u.at[half],
    )
    g_down = Grad(
        gd,
        down_half,
        lead_half,
        xd,
        zd,
        lambda row: gd.at[ic, p, :, pl.ds(al(row, 256), 256)],
        lambda yp: fin_d.at[yp, p],
        lambda half: fin_d.at[:, half],
    )

    def tokens_by(ref, cols):
        return ref[:, :, cols].reshape(2 * SEQ, cols.size)

    def down_grad():
        def tile(n, carry):
            left = tokens_by(act, pl.ds(al(n, 256), 256))
            gd[n // 2, n % 2] = dot(left, gdf[...].reshape(2 * SEQ, D), 0, 0).astype(BF)
            return carry

        lax.fori_loop(0, 4, tile, 0)

    def up_grad():
        def tile(n, carry):
            left = tokens_by(hf, pl.ds(al(n, 256), 256))
            gup[n] = (
                dot(left, gu[...].reshape(2 * SEQ, D), 0, 0).astype(BF).reshape(2, 128, D)
            )
            return carry

        lax.fori_loop(0, 4, tile, 0)

    def out_grad():
        left = ctx[...].reshape(2 * SEQ, 256)
        go[...] = dot(left, gaf[...].reshape(2 * SEQ, D), 0, 0).astype(BF).reshape(2, 2, 64, D)

    def qkv_grad():
        def tile(n, carry):
            left = tokens_by(xf, pl.ds(al(n, 256), 256))
            gq[n] = (
                dot(left, gproj[...].reshape(2 * SEQ, 768), 0, 0).astype(BF).reshape(2, 128, 768)
            )
            return carry

        lax.fori_loop(0, 4, tile, 0)

    down_grad()
    g_down.to_pair()
    first_norm_pull(0)
    ag3[0].forward()
    first_norm_pull(1)
    up_grad()
    g_up.to_pair()
    ag3[0].wait()

    def pull_attend(s):
        gctx[...] = dot(gaf[s], wo[...].reshape(256, D), 1, 1).astype(BF)
        lane = lax.broadcasted_iota(jnp.int32, (SEQ, 128), 1)
        row = lax.broadcasted_iota(jnp.int32, (128, SEQ), 0)
        scale_factor = float(HEAD) ** (-0.5)

        def pair(ci, carry):
            queries = proj[s, :, columns(ci, 0)]
            keys_in = proj[s, :, columns(ci, 1)]
            values_in = proj[s, :, columns(ci, 2)]
            grad = gctx[:, pl.ds(al(ci, 128), 128)]
            grads_q, grads_k, grads_v = [], [], []
            for h in (0, 1):
                chosen = (lane < HEAD) if h == 0 else (lane >= HEAD)
                masked = jnp.where(chosen, grad, jnp.zeros_like(grad))
                share = probs[s, ci * 2 + h]
                wide = share.astype(F32)
                weighted = wide * dot(values_in, masked, 1, 1)
                total = jnp.sum(weighted, 0, keepdims=True)
                grad_scores = (weighted - wide * total).astype(BF)
                grads_v.append(dot(share, grad, 1, 0))
                grads_k.append(dot(grad_scores, queries, 1, 0))
                grads_q.append(dot(keys_in, grad_scores, 0, 0))
            both_q = jnp.transpose(jnp.where(row < HEAD, grads_q[0], grads_q[1]) * scale_factor)
            both_q = both_q.astype(BF)
            both_v = jnp.where(lane < HEAD, grads_v[0], grads_v[1]).astype(BF)
            both_k = jnp.where(lane < HEAD, grads_k[0], grads_k[1]) * scale_factor
            gproj[s, :, columns(ci, 0)] = both_q
            gproj[s, :, columns(ci, 1)] = both_k.astype(BF)
            gproj[s, :, columns(ci, 2)] = both_v
            at = pl.ds(al(ci, 128), 128)
            vec_out[7:8, at] += col_sum(both_q.astype(F32))
            at = pl.ds(pl.multiple_of(256 + ci * 128, 128), 128)
            vec_out[7:8, at] += col_sum(both_v.astype(F32))
            return carry

        lax.fori_loop(0, 2, pair, 0)

    def pull_tokens(s):
        rows = gproj[s]

        def tile(n, carry):
            partf[s, n] = dot(rows, wq[n].reshape(256, 768), 1, 1).astype(BF)
            return carry

        lax.fori_loop(0, 4, tile, 0)

    rs4 = [Scatter(partf, lambda ref, s, row: ref.at[s, row], rscf, ysendf, rsyf, s) for s in (0, 1)]
    tg_l = new("l", 2)
    tg_copy = [pltpu.make_async_copy(tg.at[s], tg_out.at[s], ls.at[tg_l + s]) for s in (0, 1)]

    def tokens_done(s):
        tg[s] = rs4[s].result() + slab_of(gaf, s, r)[...].astype(F32)
        tg_copy[s].start()

    for s in (0, 1):
        if s == 1:
            ag3[1].wait()
        pull_attend(s)
        if s == 0:
            ag3[1].forward()
            g_down.to_cols()
        else:
            g_up.to_cols()
        pull_tokens(s)
        rs4[s].to_core()
        rs4[s].to_y()
    qkv_grad()
    g_qkv.to_pair()
    out_grad()
    g_out.to_pair()
    g_down.to_rows()
    tokens_done(0)
    g_up.to_rows()
    g_qkv.to_cols()
    g_out.to_cols()
    tokens_done(1)
    g_down.to_pair_again()
    g_up.to_pair_again()
    g_qkv.to_rows()
    g_out.to_rows()
    g_qkv.to_pair_again()
    g_out.to_pair_again()
    for grad in (g_down, g_up, g_qkv, g_out):
        grad.done()

    for s in (0, 1):
        rs3[s].sent()
        rs4[s].sent()
        tg_copy[s].wait()
        lo_own[s].wait()
        for j in (1, 2, 3):
            source = (r + j) % 4
            place = lo_place(s, source)
            remote(lo_s, lo_r + 4 * s + source, place, place, core_dev).wait_recv()
    for condition, copy in late:
        if condition is None:
            copy.wait_send()
        else:
            pl.when(condition)(copy.wait_send)


S_SEMS = 160
R_SEMS = 160
L_SEMS = 32


def run_layer(seg, x, og, wq, wo, wu, wd, bias, vecs):
    any_spec = pl.BlockSpec(memory_space=pl.ANY)
    vmem = pl.BlockSpec(memory_space=pltpu.VMEM)
    out = jax.ShapeDtypeStruct
    outs = [
        (out((2, SEQ, 256), BF), any_spec),
        (out((2, SEQ, 256), F32), any_spec),
        (out((2, 128, 768), BF), any_spec),
        (out((2, 2, 64, 256), BF), any_spec),
        (out((2, 128, D), BF), any_spec),
        (out((2, 2, 256, 256), BF), any_spec),
        (out((8, D), F32), vmem),
    ]
    full = ((2, SEQ, D), BF)
    scratch = [
        ((8, SEQ), F32),
        ((4, 8, D), F32),
        full,
        ((4, 2, 128, 768), BF),
        ((2, 2, 64, D), BF),
        ((4, 2, 128, D), BF),
        ((2, 2, 256, D), BF),
        ((2, SEQ, 768), BF),
        ((2, 4, SEQ, SEQ), BF),
        ((2, SEQ, 256), BF),
        ((SEQ, SEQ), F32),
        full,
        ((2, 2, ROWS, D), BF),
        ((2, ROWS, D), BF),
        ((2, ROWS, D), BF),
        ((2, ROWS, D), F32),
        ((2, ROWS, 128), F32),
        full,
        full,
        full,
        ((2, ROWS, D), BF),
        ((2, ROWS, D), BF),
        ((2, ROWS, D), F32),
        full,
        full,
        full,
        ((SEQ, 256), BF),
        ((2, SEQ, 768), BF),
        ((2, 4, SEQ, 256), BF),
        ((2, 2, SEQ, 256), BF),
        ((2, SEQ, 256), BF),
        ((2, SEQ, 256), BF),
        ((2, SEQ, 256), F32),
        ((4, 2, 128, 768), BF),
        ((2, 2, 64, D), BF),
        ((4, 2, 128, D), BF),
        ((2, 2, 256, D), BF),
        ((4, 128, 768), BF),
        ((2, 64, D), BF),
        ((4, 128, D), BF),
        ((2, 256, D), BF),
        ((3, 4, 128, 384), BF),
        ((3, 64, D), BF),
        ((3, 4, 128, 512), BF),
        ((3, 256, D), BF),
    ]
    return pl.pallas_call(
        layer_kernel,
        out_shape=[o[0] for o in outs],
        in_specs=[any_spec] * 7 + [vmem] * 2,
        out_specs=[o[1] for o in outs],
        scratch_shapes=[pltpu.VMEM(shape, dtype) for shape, dtype in scratch]
        + [
            pltpu.SemaphoreType.DMA((S_SEMS,)),
            pltpu.SemaphoreType.DMA((R_SEMS,)),
            pltpu.SemaphoreType.DMA((L_SEMS,)),
        ],
        compiler_params=pltpu.CompilerParams(
            collective_id=0, has_side_effects=True, vmem_limit_bytes=62 * 1024 * 1024
        ),
        name="layer",
    )(seg, x, og, wq, wo, wu, wd, bias, vecs)


def shards(
    pairs,
    tokens,
    segments,
    qkv_weight,
    qv_bias,
    out_weight,
    out_bias,
    norm1_gain,
    norm1_bias,
    up_weight,
    up_bias,
    down_weight,
    down_bias,
    norm2_gain,
    norm2_bias,
    out_grad,
):
    row = lax.axis_index("row")
    col = lax.axis_index("col")
    y, k = row // 2, row % 2
    labels = jnp.pad(segments.astype(F32), ((0, 6), (0, 0)))
    wq = qkv_weight.reshape(256, 3, 2, 128).transpose(0, 2, 1, 3).reshape(2, 128, 768)
    bias = jnp.zeros((8, D), F32)
    bias = bias.at[0].set(up_bias).at[1, :512].set(qv_bias.reshape(512))
    vecs = jnp.stack(
        [out_bias, norm1_gain, norm1_bias, down_bias, norm2_gain, norm2_bias, out_bias, out_bias]
    )
    lo, tg, fin_q, fin_o, fin_u, fin_d, vec = run_layer(
        labels,
        tokens.reshape(2, SEQ, 256),
        out_grad.reshape(2, SEQ, 256),
        wq,
        out_weight.reshape(2, 2, 64, 256),
        up_weight.reshape(2, 128, D),
        down_weight.reshape(2, 2, 256, 256),
        bias,
        vecs,
    )
    up_part = lax.dynamic_update_slice(
        jnp.zeros((4, 2, 512), F32), vec[6].reshape(2, 1, 512), (2 * k, y, 0)
    )
    qv_part = lax.dynamic_update_slice(
        jnp.zeros((2, 4, 2, 128), F32), vec[7, :512].reshape(2, 2, 1, 128), (0, 2 * k, y, 0)
    )
    joined = jnp.concatenate([vec[:6].reshape(-1), up_part.reshape(-1), qv_part.reshape(-1)])
    joined = lax.psum(joined, ("dp", "row", "col"))
    features = lax.dynamic_slice_in_dim(joined[: 6 * D].reshape(6, D), row * 256, 256, 1)
    up_bias_grad = lax.dynamic_slice_in_dim(joined[6 * D : 10 * D], col * D, D)
    qv_bias_grad = lax.dynamic_slice_in_dim(joined[10 * D :].reshape(2, D), col * 256, 256, 1)
    grads = (fin_q, fin_o, fin_u, fin_d)
    if pairs is not None:
        grads = lax.psum(grads, "dp", axis_index_groups=pairs)
    fin_q, fin_o, fin_u, fin_d = grads
    fin_q = fin_q.reshape(256, 2, 3, 128).transpose(0, 2, 1, 3).reshape(256, 3, 256)
    return (
        lo.reshape(2 * SEQ, 256),
        tg.reshape(2 * SEQ, 256),
        fin_q.astype(F32),
        qv_bias_grad,
        fin_o.reshape(256, 256).astype(F32),
        features[5],
        features[2],
        features[3],
        fin_u.reshape(256, D).astype(F32),
        up_bias_grad,
        fin_d.reshape(D, 256).astype(F32),
        features[4],
        features[0],
        features[1],
    )


def solution(mesh):
    placed = (
        P(("dp", "col"), "row"),
        P(("dp", "row"), None),
        P("row", None, "col"),
        P(None, "col"),
        P("col", "row"),
        P(),
        P(),
        P(),
        P("row", "col"),
        P("col"),
        P("col", "row"),
        P(),
        P(),
        P(),
        P(("dp", "col"), "row"),
    )
    dp = mesh.shape["dp"]
    pairs = None
    if dp > 2:
        pairs = [list(range(0, dp, 2)), list(range(1, dp, 2))]
    return jax.shard_map(
        functools.partial(shards, pairs),
        mesh=mesh,
        in_specs=placed,
        out_specs=(
            P(("dp", "col"), "row"),
            P(("dp", "col"), "row"),
            P("row", None, "col"),
            P(None, "col"),
            P("col", "row"),
            P("row"),
            P("row"),
            P("row"),
            P("row", "col"),
            P("col"),
            P("col", "row"),
            P("row"),
            P("row"),
            P("row"),
        ),
        check_vma=False,
    )
```

```python
import functools

import jax
import jax.numpy as jnp
from jax import lax
from jax.experimental import pallas as pl
from jax.experimental.pallas import tpu as pltpu
from jax.sharding import PartitionSpec as P

D = 1024
HEAD = 64
SEQ = 512
EPS = 1e-05
MESH = pl.DeviceIdType.MESH
BF = jnp.bfloat16
F32 = jnp.float32
ROWS = 128


def dot(left, right, left_dim, right_dim):
    return lax.dot_general(
        left, right, (((left_dim,), (right_dim,)), ((), ())), preferred_element_type=F32
    )


def al(index, step):
    return pl.multiple_of(index * step, step)


def col_sum(values):
    return jnp.sum(values, 0, keepdims=True)


def layer_kernel(
    seg_in,
    x_in,
    og_in,
    wq_in,
    wo_in,
    wu_in,
    wd_in,
    bias_in,
    vecs,
    lo_out,
    tg_out,
    fin_q,
    fin_o,
    fin_u,
    fin_d,
    vec_out,
    seg,
    biases,
    xf,
    wq,
    wo,
    wu,
    wd,
    stage_q,
    stage_o,
    stage_u,
    stage_d,
    proj,
    probs,
    ctx,
    mask,
    part,
    rsc,
    rsy,
    ysend,
    normed1,
    inv1,
    hf,
    act,
    gelup,
    og,
    lo,
    gsec,
    gdf,
    gu,
    gaf,
    gctx,
    gproj,
    partf,
    rscf,
    rsyf,
    ysendf,
    tg,
    gq,
    go,
    gup,
    gd,
    xq,
    xq1,
    xo,
    xu,
    xd,
    xd1,
    zq,
    zq1,
    zo,
    zu,
    zd,
    zd1,
    vec_sum,
    vec_rows,
    vec_out_parts,
    vec_cols,
    vec_part,
    vec_pair,
    ss,
    rs,
    ls,
):
    d = lax.axis_index("dp")
    r = lax.axis_index("row")
    c = lax.axis_index("col")
    y = r // 2
    k = r % 2
    p = d % 2
    r1 = r + 1 - 2 * k
    r2 = (r + 2) % 4
    r3 = (r1 + 2) % 4
    kc = c // 2
    ic = c % 2
    is_agg = k == kc
    core_dev = (d, r1, c)
    y_dev = (d, r2, c)
    x_dev = (d + 1 - 2 * p, r, c)

    counts = {"s": 0, "r": 0, "l": 0}

    def new(kind, n=1):
        at = counts[kind]
        counts[kind] += n
        return at

    def remote(si, ri, src, dst, dev):
        return pltpu.make_async_remote_copy(
            src_ref=src,
            dst_ref=dst,
            send_sem=ss.at[si],
            recv_sem=rs.at[ri],
            device_id=dev,
            device_id_type=MESH,
        )

    late = []

    def later(copy, condition=None):
        late.append((condition, copy))

    barrier = pltpu.get_barrier_semaphore()
    for j in (1, 2, 3):
        pl.semaphore_signal(barrier, inc=1, device_id=(d, (r + j) % 4, c), device_id_type=MESH)
        pl.semaphore_signal(barrier, inc=1, device_id=(d, r, (c + j) % 4), device_id_type=MESH)
    pl.semaphore_signal(barrier, inc=1, device_id=x_dev, device_id_type=MESH)

    @pl.when(r != c)
    def _():
        pl.semaphore_signal(barrier, inc=1, device_id=(d, c, r), device_id_type=MESH)
        pl.semaphore_wait(barrier, 8)

    @pl.when(r == c)
    def _():
        pl.semaphore_wait(barrier, 7)

    def qkv_piece(yp):
        return wq_in.at[:, :, pl.ds(al(yp, 384), 384)]

    def out_piece(yp):
        return wo_in.at[yp]

    def up_piece(yp):
        return wu_in.at[:, :, pl.ds(al(yp, 512), 512)]

    def down_piece(yp):
        return wd_in.at[yp]

    def qkv_place(row):
        return wq.at[row, :, :, pl.ds(al(ic, 384), 384)]

    def out_place(row):
        return wo.at[ic, :, :, pl.ds(al(row, 256), 256)]

    def up_place(row):
        return wu.at[row, :, :, pl.ds(al(ic, 512), 512)]

    def down_place(row):
        return wd.at[ic, :, :, pl.ds(al(row, 256), 256)]

    def qkv_half(ref, half, ci):
        return ref.at[:, half, :, pl.ds(al(ci, 384), 384)]

    def out_half(ref, half, ci):
        return ref.at[ci, half]

    def up_half(ref, half, ci):
        return ref.at[:, half, :, pl.ds(al(ci, 512), 512)]

    def down_half(ref, half, ci):
        return ref.at[ci, half]

    def qkv_chunk(ref, half, ci, chip):
        return ref.at[pl.ds(2 * chip, 2), half, :, pl.ds(al(ci, 384), 384)]

    def out_chunk(ref, half, ci, chip):
        return ref.at[ci, half, :, pl.ds(al(chip, 512), 512)]

    def up_chunk(ref, half, ci, chip):
        return ref.at[pl.ds(2 * chip, 2), half, :, pl.ds(al(ci, 512), 512)]

    down_chunk = out_chunk
    far_dev = (d, r, (c + 2) % 4)
    near_dev = (d, r, c + 1 - 2 * ic)

    class Weight:
        def __init__(self, buffer, piece, place, chunk, stage):
            self.buffer, self.piece, self.place, self.stage = buffer, piece, place, stage
            self.s1, self.r1, self.l1 = new("s", 2), new("r", 4), new("l")
            self.relay_copy = remote(new("s"), self.r1 + r2, stage, place(r2), core_dev)
            self.staged = remote(self.s1, self.r1 + r2, stage, stage, y_dev)
            self.ready_waits = []
            self.far_copy, self.near_copy, self.pair_far, self.pair_near = {}, {}, {}, {}
            for n in (0, 1):
                chip = y if n == 0 else 1 - y
                held = chunk(buffer, p, ic, chip)
                wanted = chunk(buffer, p, 1 - ic, chip)
                self.far_copy[n] = remote(new("s"), new("r"), held, held, far_dev)
                si, ri = new("s"), new("r")
                self.near_copy[n] = (
                    remote(si, ri, held, held, near_dev),
                    remote(si, ri, wanted, wanted, near_dev),
                )
                si, ri = new("s"), new("r")
                missing = chunk(buffer, 1 - p, ic, chip)
                self.pair_far[n] = (
                    remote(si, ri, held, held, x_dev),
                    remote(si, ri, missing, missing, x_dev),
                )
                si, ri = new("s"), new("r")
                missing = chunk(buffer, 1 - p, 1 - ic, chip)
                self.pair_near[n] = (
                    remote(si, ri, wanted, wanted, x_dev),
                    remote(si, ri, missing, missing, x_dev),
                )

        def spread_rows(self):
            near = remote(self.s1 + 1, self.r1 + r, self.piece(y), self.place(r), core_dev)
            own = pltpu.make_async_copy(self.piece(y), self.place(r), ls.at[self.l1])

            @pl.when(jnp.logical_not(is_agg))
            def _():
                near.start()

            later(near, jnp.logical_not(is_agg))

            @pl.when(is_agg)
            def _():
                own.start()

            direct = remote(self.s1, self.r1 + r, self.piece(1 - y), self.place(r), y_dev)
            staged = remote(self.s1, self.r1 + r, self.piece(1 - y), self.stage, y_dev)

            @pl.when(is_agg)
            def _():
                direct.start()

            @pl.when(jnp.logical_not(is_agg))
            def _():
                staged.start()

            later(direct)
            self.own = own

        def relay(self):
            @pl.when(jnp.logical_not(is_agg))
            def _():
                self.staged.wait_recv()
                self.relay_copy.start()

            later(self.relay_copy, jnp.logical_not(is_agg))

        def lead(self, n):
            copies = (self.far_copy[n], self.near_copy[n][0])

            @pl.when(is_agg)
            def _():
                rows = [r1] if n == 0 else [r2, r3]
                if n == 0:
                    self.own.wait()
                for row in rows:
                    place = self.place(row)
                    remote(self.s1 + 1, self.r1 + row, place, place, core_dev).wait_recv()
                for copy in copies:
                    copy.start()

            for copy in copies:
                later(copy, is_agg)

        def follow(self, n):
            copies = (self.near_copy[n][0], self.pair_far[n][0])
            other = jnp.logical_not(is_agg)

            @pl.when(other)
            def _():
                self.far_copy[n].wait_recv()
                for copy in copies:
                    copy.start()

            for copy in copies:
                later(copy, other)

        def pair(self, n):
            self.near_copy[n][1].wait_recv()
            self.pair_near[n][0].start()
            later(self.pair_near[n][0])

        def ready(self):
            for n in (0, 1):

                @pl.when(jnp.logical_not(is_agg))
                def _():
                    self.pair_far[n][1].wait_recv()

                self.pair_near[n][1].wait_recv()

    w_qkv = Weight(wq, qkv_piece, qkv_place, qkv_chunk, stage_q)
    w_out = Weight(wo, out_piece, out_place, out_chunk, stage_o)
    w_up = Weight(wu, up_piece, up_place, up_chunk, stage_u)
    w_down = Weight(wd, down_piece, down_place, down_chunk, stage_d)

    def rows_of(ref, s, row):
        return ref.at[s, pl.ds(al(row, ROWS), ROWS), :]

    def slab_of(ref, s, row):
        return ref.at[s, :, pl.ds(al(row, 256), 256)]

    class Gather:
        def __init__(self, full, at, s, source=None):
            self.full, self.at, self.s = full, at, s
            self.source = source
            self.si, self.ri = [new("s"), new("s"), new("s")], new("r", 3)

        def send(self):
            mine = self.source if self.source is not None else self.at(self.full, self.s, r)
            place = self.at(self.full, self.s, r)
            for n, dev in ((0, y_dev), (1, core_dev)):
                copy = remote(self.si[n], self.ri + n, mine, place, dev)
                copy.start()
                later(copy)

        def forward(self):
            place = self.at(self.full, self.s, r2)
            remote(self.si[0], self.ri, place, place, y_dev).wait_recv()
            copy = remote(self.si[2], self.ri + 2, place, place, core_dev)
            copy.start()
            later(copy)

        def wait(self):
            near = self.at(self.full, self.s, r1)
            remote(self.si[1], self.ri + 1, near, near, core_dev).wait_recv()
            far = self.at(self.full, self.s, r3)
            remote(self.si[2], self.ri + 2, far, far, core_dev).wait_recv()

    class Scatter:
        def __init__(self, source, at, core_recv, y_send, y_recv, s):
            self.source, self.at = source, at
            self.core_recv, self.y_send, self.y_recv, self.s = core_recv, y_send, y_recv, s
            si, ri = [new("s"), new("s"), new("s")], new("r", 3)
            self.far = remote(si[0], ri, at(source, s, r3), core_recv.at[s, 1], core_dev)
            self.near = remote(si[1], ri + 1, at(source, s, r1), core_recv.at[s, 0], core_dev)
            self.cross = remote(si[2], ri + 2, y_send.at[s], y_recv.at[s], y_dev)

        def to_core(self):
            self.far.start()
            self.near.start()

        def to_y(self):
            self.far.wait_recv()
            total = self.at(self.source, self.s, r2)[...].astype(F32)
            self.y_send[self.s] = (total + self.core_recv[self.s, 1].astype(F32)).astype(BF)
            self.cross.start()

        def result(self):
            self.near.wait_recv()
            total = self.at(self.source, self.s, r)[...].astype(F32)
            total = total + self.core_recv[self.s, 0].astype(F32)
            self.cross.wait_recv()
            return total + self.y_recv[self.s].astype(F32)

        def sent(self):
            self.far.wait_send()
            self.near.wait_send()
            self.cross.wait_send()

    w_qkv.spread_rows()
    x_gather = [Gather(xf, slab_of, s, x_in.at[s]) for s in (0, 1)]
    x_own = [
        pltpu.make_async_copy(x_in.at[s], slab_of(xf, s, r), ls.at[new("l")]) for s in (0, 1)
    ]
    seg_s, seg_r, seg_l = new("s"), new("r"), new("l")
    seg_copy = remote(seg_s, seg_r, seg_in, seg, (d, c, r))
    seg_own = pltpu.make_async_copy(seg_in, seg, ls.at[seg_l])

    @pl.when(r != c)
    def _():
        seg_copy.start()

    @pl.when(r == c)
    def _():
        seg_own.start()

    bias_s, bias_r = new("s", 3), new("r", 4)
    for j in (1, 2, 3):
        copy = remote(
            bias_s + j - 1, bias_r + c, bias_in, biases.at[c], (d, r, (c + j) % 4)
        )
        copy.start()
        later(copy)
    biases[c] = bias_in[...]
    w_out.spread_rows()
    for s in (0, 1):
        x_gather[s].send()
        x_own[s].start()

    w_up.spread_rows()
    w_down.spread_rows()
    w_qkv.lead(0)
    w_qkv.relay()
    w_out.relay()
    w_qkv.follow(0)
    w_qkv.lead(1)
    w_out.lead(0)
    w_out.lead(1)
    w_up.lead(0)
    w_qkv.pair(0)
    w_qkv.follow(1)
    x_gather[0].forward()
    w_out.follow(0)
    w_qkv.pair(1)
    w_out.follow(1)
    x_gather[1].forward()
    w_out.pair(0)
    w_out.pair(1)
    w_up.relay()

    for j in (1, 2, 3):
        source = (c + j) % 4
        remote(bias_s, bias_r + source, biases.at[source], biases.at[source], core_dev).wait_recv()

    @pl.when(r != c)
    def _():
        seg_copy.wait_recv()

    @pl.when(r == c)
    def _():
        seg_own.wait()

    later(seg_copy, r != c)
    w_qkv.ready()

    vec_sum[...] = jnp.zeros_like(vec_sum)

    def project(s):
        rows = xf[s]

        def half(ci, carry):
            weight = wq[:, :, :, pl.ds(al(ci, 384), 384)].reshape(D, 384)
            q_bias = biases[2 * k + ci, 1:2, pl.ds(al(y, 128), 128)]
            v_bias = biases[2 * k + ci, 1:2, pl.ds(pl.multiple_of(256 + y * 128, 128), 128)]
            bias = jnp.concatenate([q_bias, jnp.zeros_like(q_bias), v_bias], 1)
            proj[s, :, pl.ds(al(ci, 384), 384)] = (dot(rows, weight, 1, 0) + bias).astype(BF)
            return carry

        lax.fori_loop(0, 2, half, 0)

    def columns(ci, n):
        return pl.ds(pl.multiple_of(ci * 384 + n * 128, 128), 128)

    def attend(s):
        labels = seg[s : s + 1, :]
        down = jnp.transpose(jnp.broadcast_to(labels, (128, SEQ)))[:, 0:1]
        mask[...] = jnp.where(down == labels, 0.0, -1e30)
        lane = lax.broadcasted_iota(jnp.int32, (SEQ, 128), 1)
        row = lax.broadcasted_iota(jnp.int32, (128, SEQ), 0)

        def pair(ci, carry):
            queries = proj[s, :, columns(ci, 0)]
            keys_in = proj[s, :, columns(ci, 1)]
            values_in = proj[s, :, columns(ci, 2)]
            parts = []
            for h in (0, 1):
                chosen = (lane < HEAD) if h == 0 else (lane >= HEAD)
                masked = jnp.where(chosen, queries, jnp.zeros_like(queries))
                scores = dot(keys_in, masked, 1, 1) * (float(HEAD) ** (-0.5)) + mask[...]
                weights = jnp.exp(scores - jnp.max(scores, 0, keepdims=True))
                totals = jnp.sum(weights, 0, keepdims=True)
                share = (weights * (1.0 / totals)).astype(BF)
                probs[s, ci * 2 + h] = share
                parts.append(dot(values_in, share, 0, 0))
            both = jnp.where(row < HEAD, parts[0], parts[1])
            ctx[s, :, pl.ds(al(ci, 128), 128)] = jnp.transpose(both).astype(BF)
            return carry

        lax.fori_loop(0, 2, pair, 0)

    def out_partial(s):
        part[s] = dot(ctx[s], wo[...].reshape(256, D), 1, 0).astype(BF)

    def norm_stats(summed):
        center = jnp.sum(summed, 1, keepdims=True) * (1.0 / D)
        spread = jnp.sum(summed * summed, 1, keepdims=True) * (1.0 / D) - center * center
        inverse = lax.rsqrt(spread + EPS)
        return (summed - center) * inverse, inverse

    def norm_pull(grad, normed, inverse, gain):
        scaled = grad * gain
        first = jnp.sum(scaled, 1, keepdims=True) * (1.0 / D)
        second = jnp.sum(scaled * normed, 1, keepdims=True) * (1.0 / D)
        return inverse * (scaled - first - normed * second)

    out_bias, gain1, offset1 = vecs[0:1, :], vecs[1:2, :], vecs[2:3, :]
    down_bias, gain2, offset2 = vecs[3:4, :], vecs[4:5, :], vecs[5:6, :]
    own_rows = pl.ds(al(r, ROWS), ROWS)

    def scatters():
        return [Scatter(part, rows_of, rsc, ysend, rsy, s) for s in (0, 1)]

    rs1 = scatters()
    ag1 = [Gather(hf, rows_of, s) for s in (0, 1)]

    def first_norm(s):
        first_sum = rs1[s].result() + out_bias + xf[s, own_rows, :].astype(F32)
        normed, inverse = norm_stats(first_sum)
        normed1[s] = normed
        inv1[s] = jnp.broadcast_to(inverse, (ROWS, 128))
        hf[s, own_rows, :] = (normed * gain1 + offset1).astype(BF)
        ag1[s].send()

    og_s, og_r, og_l = new("s", 3), new("r", 4), new("l")

    def og_place(row):
        return og.at[:, :, pl.ds(al(row, 256), 256)]

    og_own = pltpu.make_async_copy(og_in.at[:, pl.ds(al(r, ROWS), ROWS), :], og_place(r), ls.at[og_l])

    def send_og():
        og_own.start()
        for j in (1, 2, 3):
            row = (r + j) % 4
            copy = remote(
                og_s + j - 1,
                og_r + r,
                og_in.at[:, pl.ds(al(row, ROWS), ROWS), :],
                og_place(r),
                (d, row, c),
            )
            copy.start()
            later(copy)

    x_own[0].wait()
    x_gather[0].wait()
    project(0)
    w_up.lead(1)
    w_up.follow(0)
    attend(0)
    w_out.ready()
    out_partial(0)
    rs1[0].to_core()
    w_down.relay()
    w_down.lead(0)
    w_down.lead(1)
    rs1[0].to_y()
    x_own[1].wait()
    x_gather[1].wait()
    project(1)
    w_up.follow(1)
    w_up.pair(0)
    attend(1)
    out_partial(1)
    rs1[1].to_core()
    rs1[1].to_y()
    w_down.follow(0)
    first_norm(0)
    w_up.pair(1)
    w_down.pair(0)
    first_norm(1)
    w_down.follow(1)
    ag1[0].forward()
    w_down.pair(1)
    w_up.ready()
    ag1[0].wait()

    def up_bias_of(ci):
        return biases[2 * k + ci, 0:1, pl.ds(al(y, 512), 512)]

    def mlp_up(s):
        rows = hf[s]

        def tile(n, carry):
            cols = pl.ds(al(n, 256), 256)
            weight = wu[:, :, :, cols].reshape(D, 256)
            ci = n // 2
            bias = biases[2 * k + ci, 0:1, pl.ds(pl.multiple_of(y * 512 + (n % 2) * 256, 256), 256)]
            upward = dot(rows, weight, 1, 0) + bias
            share = 0.5 + 0.5 * lax.erf(upward * 0.7071067811865476)
            act[s, :, cols] = (upward * share).astype(BF)
            density = jnp.exp(-0.5 * upward * upward) * 0.3989422804014327
            gelup[s, :, cols] = (share + upward * density).astype(BF)
            return carry

        lax.fori_loop(0, 4, tile, 0)

    def mlp_down(s):
        rows = act[s]

        def tile(n, carry):
            cols = pl.ds(al(n, 256), 256)
            weight = wd[:, :, :, cols].reshape(D, 256)
            part[s, :, cols] = dot(rows, weight, 1, 0).astype(BF)
            return carry

        lax.fori_loop(0, 4, tile, 0)

    rs2 = scatters()
    ag2 = [Gather(gdf, rows_of, s) for s in (0, 1)]
    lo_s, lo_r, lo_l = new("s", 6), new("r", 8), new("l", 2)

    def second_norm(s):
        hidden = normed1[s] * gain1 + offset1
        second_sum = rs2[s].result() + down_bias + hidden
        normed, inverse = norm_stats(second_sum)
        lo[s] = (normed * gain2 + offset2).astype(BF)
        grad = og[s].astype(F32)
        vec_sum[0:1, :] += col_sum(grad * normed)
        vec_sum[1:2, :] += col_sum(grad)
        grad_second = norm_pull(grad, normed, inverse, gain2)
        gsec[s] = grad_second
        rounded = grad_second.astype(BF)
        vec_sum[4:5, :] += col_sum(rounded.astype(F32))
        gdf[s, own_rows, :] = rounded
        ag2[s].send()

    def lo_place(s, row):
        return lo_out.at[s, pl.ds(al(row, ROWS), ROWS), :]

    def lo_part(s, row):
        return lo.at[s, :, pl.ds(al(row, 256), 256)]

    lo_own = [
        pltpu.make_async_copy(lo_part(s, r), lo_place(s, r), ls.at[lo_l + s]) for s in (0, 1)
    ]

    def send_lo(s):
        lo_own[s].start()
        for j in (1, 2, 3):
            row = (r + j) % 4
            copy = remote(
                lo_s + 3 * s + j - 1, lo_r + 4 * s + r, lo_part(s, row), lo_place(s, r), (d, row, c)
            )
            copy.start()
            later(copy)

    mlp_up(0)
    ag1[1].forward()
    send_og()
    w_down.ready()
    rs1[0].sent()
    mlp_down(0)
    rs2[0].to_core()
    rs2[0].to_y()
    ag1[1].wait()
    mlp_up(1)
    rs1[1].sent()
    mlp_down(1)
    rs2[1].to_core()
    rs2[1].to_y()
    og_own.wait()
    for j in (1, 2, 3):
        source = (r + j) % 4
        remote(og_s, og_r + source, og_place(source), og_place(source), core_dev).wait_recv()

    second_norm(0)
    second_norm(1)
    ag2[0].forward()
    ag2[0].wait()

    class Grad:
        def __init__(self, buffer, chunk, both, by_ci, pair_recv, col_recv, place, pair_first):
            self.buffer, self.place, self.pair_first = buffer, place, pair_first
            pair_recvs, col_recvs = pair_recv, col_recv
            self.near_copy, self.far_copy, self.pair_copy = {}, {}, {}
            self.near_add, self.far_add, self.pair_add = {}, {}, {}
            self.own, self.rows_copies = None, {}
            self.chunk = chunk
            self.s3, self.r3, self.l3 = new("s", 7), new("r", 4), new("l")
            for n in (0, 1):
                chip = y if n == 0 else 1 - y
                pair_recv, col_recv = pair_recvs[n], col_recvs[n]
                if pair_first[n]:
                    pair_src, pair_dst = both(buffer, 1 - p, chip), both(buffer, p, chip)
                    near_src, held = chunk(buffer, p, 1 - ic, chip), chunk(buffer, p, ic, chip)
                else:
                    pair_src, pair_dst = chunk(buffer, 1 - p, ic, chip), chunk(buffer, p, ic, chip)
                    near_src, held = by_ci(buffer, 1 - ic, chip), by_ci(buffer, ic, chip)
                self.pair_copy[n] = remote(new("s"), new("r"), pair_src, pair_recv, x_dev)
                self.near_copy[n] = remote(new("s"), new("r"), near_src, col_recv.at[0], near_dev)
                self.far_copy[n] = remote(new("s"), new("r"), held, col_recv.at[1], far_dev)
                self.pair_add[n] = (pair_dst, pair_recv)
                self.near_add[n] = (held, col_recv.at[0])
                self.far_add[n] = (held, col_recv.at[1])

        def add(self, refs):
            mine, other = refs
            mine[...] = (mine[...].astype(F32) + other[...].astype(F32)).astype(BF)

        def arrival(self, half, yp):
            return self.r3 + 2 * half + yp

        def rows_of_chunk(self, n):
            copies = []
            here, there = d, d + 1 - 2 * p
            if n == 0:
                self.own = pltpu.make_async_copy(self.piece(r), self.place(p, y), ls.at[self.l3])
                targets = [(here, r1), (there, r), (there, r1)]
                at = 0
            else:
                targets = [(here, r2), (there, r2), (here, r3), (there, r3)]
                at = 3
            for plane, row in targets:
                copies.append(
                    remote(
                        self.s3 + at,
                        self.arrival(p, y),
                        self.piece(row),
                        self.place(p, y),
                        (plane, row, c),
                    )
                )
                at += 1
            return copies

        def begin(self, n):
            first = self.pair_copy[n] if self.pair_first[n] else self.near_copy[n]
            first.start()
            later(first)

        def second(self, n):
            if self.pair_first[n]:
                self.pair_copy[n].wait_recv()
                self.add(self.pair_add[n])
                self.near_copy[n].start()
                later(self.near_copy[n])
            else:
                self.near_copy[n].wait_recv()
                self.add(self.near_add[n])

                @pl.when(jnp.logical_not(is_agg))
                def _():
                    self.far_copy[n].start()

                later(self.far_copy[n], jnp.logical_not(is_agg))

        def third(self, n):
            if self.pair_first[n]:
                self.near_copy[n].wait_recv()
                self.add(self.near_add[n])

                @pl.when(jnp.logical_not(is_agg))
                def _():
                    self.far_copy[n].start()

                later(self.far_copy[n], jnp.logical_not(is_agg))
            else:

                @pl.when(is_agg)
                def _():
                    self.far_copy[n].wait_recv()
                    self.add(self.far_add[n])
                    self.pair_copy[n].start()

                later(self.pair_copy[n], is_agg)

        def to_rows(self, n):
            copies = self.rows_of_chunk(n)

            @pl.when(is_agg)
            def _():
                if self.pair_first[n]:
                    self.far_copy[n].wait_recv()
                    self.add(self.far_add[n])
                else:
                    self.pair_copy[n].wait_recv()
                    self.add(self.pair_add[n])
                if n == 0:
                    self.own.start()
                for copy in copies:
                    copy.start()

            for copy in copies:
                later(copy, is_agg)

        def done(self):
            @pl.when(is_agg)
            def _():
                self.own.wait()

            @pl.when(jnp.logical_not(is_agg))
            def _():
                place = self.place(p, y)
                remote(self.s3, self.arrival(p, y), place, place, core_dev).wait_recv()

            for half, yp in ((p, 1 - y), (1 - p, y), (1 - p, 1 - y)):
                place = self.place(half, yp)
                remote(self.s3, self.arrival(half, yp), place, place, core_dev).wait_recv()

    def rows_both(ref, half, chip):
        return ref.at[pl.ds(2 * chip, 2), half]

    def cols_both(ref, half, chip):
        return ref.at[:, half, :, pl.ds(al(chip, 512), 512)]

    def cols_of_ci(ref, ci, chip):
        return ref.at[ci, :, :, pl.ds(al(chip, 512), 512)]

    def rows_of_ci(ref, ci, chip):
        return ref.at[pl.ds(2 * chip, 2), :, :, pl.ds(al(ci, 384), 384)]

    def two(ref):
        return [ref.at[0], ref.at[1]]

    g_qkv = Grad(
        gq,
        qkv_chunk,
        rows_both,
        rows_of_ci,
        [xq, xq1],
        [zq, zq1],
        lambda half, yp: fin_q.at[half, :, pl.ds(al(yp, 384), 384)],
        (False, True),
    )
    g_qkv.piece = lambda row: gq.at[row, p, :, pl.ds(al(ic, 384), 384)]
    g_out = Grad(
        go, out_chunk, cols_both, None, two(xo), two(zo), lambda half, yp: fin_o.at[yp, half], (True, True)
    )
    g_out.piece = lambda row: go.at[ic, p, :, pl.ds(al(row, 256), 256)]
    g_up = Grad(
        gup,
        up_chunk,
        rows_both,
        None,
        two(xu),
        two(zu),
        lambda half, yp: fin_u.at[half, :, pl.ds(al(yp, 512), 512)],
        (True, True),
    )
    g_up.piece = lambda row: gup.at[row, p, :, pl.ds(al(ic, 512), 512)]
    g_down = Grad(
        gd,
        down_chunk,
        cols_both,
        cols_of_ci,
        [xd, xd1],
        [zd, zd1],
        lambda half, yp: fin_d.at[yp, half],
        (True, False),
    )
    g_down.piece = lambda row: gd.at[ic, p, :, pl.ds(al(row, 256), 256)]

    def tokens_by(ref, cols):
        return ref[:, :, cols].reshape(2 * SEQ, cols.size)

    def down_grad():
        def tile(n, carry):
            left = tokens_by(act, pl.ds(al(n, 256), 256))
            gd[n // 2, n % 2] = dot(left, gdf[...].reshape(2 * SEQ, D), 0, 0).astype(BF)
            return carry

        lax.fori_loop(0, 4, tile, 0)

    def up_grad():
        def tile(n, carry):
            left = tokens_by(hf, pl.ds(al(n, 256), 256))
            gup[n] = (
                dot(left, gu[...].reshape(2 * SEQ, D), 0, 0).astype(BF).reshape(2, 128, D)
            )
            return carry

        lax.fori_loop(0, 4, tile, 0)

    def out_grad():
        left = ctx[...].reshape(2 * SEQ, 256)
        go[...] = dot(left, gaf[...].reshape(2 * SEQ, D), 0, 0).astype(BF).reshape(2, 2, 64, D)

    def qkv_grad():
        def tile(n, carry):
            left = tokens_by(xf, pl.ds(al(n, 256), 256))
            gq[n] = (
                dot(left, gproj[...].reshape(2 * SEQ, 768), 0, 0).astype(BF).reshape(2, 128, 768)
            )
            return carry

        lax.fori_loop(0, 4, tile, 0)

    def pull_act(s):
        rows = gdf[s]

        def tile(n, carry):
            cols = pl.ds(al(n, 256), 256)
            grad = dot(rows, wd[n // 2, n % 2], 1, 1) * gelup[s, :, cols].astype(F32)
            rounded = grad.astype(BF)
            gu[s, :, cols] = rounded
            vec_sum[6:7, cols] += col_sum(rounded.astype(F32))
            return carry

        lax.fori_loop(0, 4, tile, 0)

    def pull_hidden(s):
        rows = gu[s]

        def tile(n, carry):
            weight = wu[n].reshape(256, D)
            part[s, :, pl.ds(al(n, 256), 256)] = dot(rows, weight, 1, 1).astype(BF)
            return carry

        lax.fori_loop(0, 4, tile, 0)

    rs3 = scatters()
    ag3 = [Gather(gaf, rows_of, s) for s in (0, 1)]

    def first_norm_pull(s):
        grad = gsec[s] + rs3[s].result()
        normed = normed1[s]
        vec_sum[2:3, :] += col_sum(grad * normed)
        vec_sum[3:4, :] += col_sum(grad)
        rounded = norm_pull(grad, normed, inv1[s][:, 0:1], gain1).astype(BF)
        vec_sum[5:6, :] += col_sum(rounded.astype(F32))
        gaf[s, own_rows, :] = rounded
        ag3[s].send()

    pull_act(0)
    rs2[0].sent()
    pull_hidden(0)
    rs3[0].to_core()
    ag2[1].forward()
    rs3[0].to_y()
    ag2[1].wait()
    down_grad()
    g_down.begin(1)
    g_down.begin(0)
    pull_act(1)
    rs2[1].sent()
    pull_hidden(1)
    rs3[1].to_core()
    rs3[1].to_y()
    first_norm_pull(0)
    up_grad()
    g_up.begin(1)
    g_up.begin(0)
    g_down.second(1)
    g_down.second(0)
    first_norm_pull(1)
    ag3[0].forward()
    ag3[0].wait()

    def pull_attend(s):
        gctx[...] = dot(gaf[s], wo[...].reshape(256, D), 1, 1).astype(BF)
        lane = lax.broadcasted_iota(jnp.int32, (SEQ, 128), 1)
        row = lax.broadcasted_iota(jnp.int32, (128, SEQ), 0)
        scale_factor = float(HEAD) ** (-0.5)

        def pair(ci, carry):
            queries = proj[s, :, columns(ci, 0)]
            keys_in = proj[s, :, columns(ci, 1)]
            values_in = proj[s, :, columns(ci, 2)]
            grad = gctx[:, pl.ds(al(ci, 128), 128)]
            grads_q, grads_k, grads_v = [], [], []
            for h in (0, 1):
                chosen = (lane < HEAD) if h == 0 else (lane >= HEAD)
                masked = jnp.where(chosen, grad, jnp.zeros_like(grad))
                share = probs[s, ci * 2 + h]
                wide = share.astype(F32)
                weighted = wide * dot(values_in, masked, 1, 1)
                total = jnp.sum(weighted, 0, keepdims=True)
                grad_scores = (weighted - wide * total).astype(BF)
                grads_v.append(dot(share, grad, 1, 0))
                grads_k.append(dot(grad_scores, queries, 1, 0))
                grads_q.append(dot(keys_in, grad_scores, 0, 0))
            both_q = jnp.transpose(jnp.where(row < HEAD, grads_q[0], grads_q[1]) * scale_factor)
            both_q = both_q.astype(BF)
            both_v = jnp.where(lane < HEAD, grads_v[0], grads_v[1]).astype(BF)
            both_k = jnp.where(lane < HEAD, grads_k[0], grads_k[1]) * scale_factor
            gproj[s, :, columns(ci, 0)] = both_q
            gproj[s, :, columns(ci, 1)] = both_k.astype(BF)
            gproj[s, :, columns(ci, 2)] = both_v
            at = pl.ds(al(ci, 128), 128)
            vec_sum[7:8, at] += col_sum(both_q.astype(F32))
            at = pl.ds(pl.multiple_of(256 + ci * 128, 128), 128)
            vec_sum[7:8, at] += col_sum(both_v.astype(F32))
            return carry

        lax.fori_loop(0, 2, pair, 0)

    def pull_tokens(s):
        rows = gproj[s]

        def tile(n, carry):
            partf[s, n] = dot(rows, wq[n].reshape(256, 768), 1, 1).astype(BF)
            return carry

        lax.fori_loop(0, 4, tile, 0)

    rs4 = [Scatter(partf, lambda ref, s, row: ref.at[s, row], rscf, ysendf, rsyf, s) for s in (0, 1)]
    tg_l = new("l", 2)
    tg_copy = [pltpu.make_async_copy(tg.at[s], tg_out.at[s], ls.at[tg_l + s]) for s in (0, 1)]

    def tokens_done(s):
        tg[s] = rs4[s].result() + slab_of(gaf, s, r)[...].astype(F32)
        tg_copy[s].start()

    class Sums:
        def __init__(self):
            self.si, self.ri = new("s", 7), new("r", 9)
            self.pair = remote(self.si + 6, self.ri + 8, vec_part, vec_pair, x_dev)

        def to_rows(self):
            vec_rows[r] = vec_sum[...]
            for j in (1, 2, 3):
                copy = remote(
                    self.si + j - 1, self.ri + r, vec_sum, vec_rows.at[r], (d, (r + j) % 4, c)
                )
                copy.start()
                later(copy)

        def to_cols(self):
            for j in (1, 2, 3):
                place = vec_rows.at[(r + j) % 4]
                remote(self.si, self.ri + (r + j) % 4, place, place, core_dev).wait_recv()
            mine = pl.ds(al(r, 256), 256)
            features = vec_rows[0, 0:6, mine] + vec_rows[1, 0:6, mine]
            features = features + vec_rows[2, 0:6, mine] + vec_rows[3, 0:6, mine]
            for j in (0, 1, 2, 3):
                to = (c + j) % 4
                slot = vec_out_parts.at[j]
                slot[0:6, :] = features
                for yp in (0, 1):
                    row = 2 * yp + to // 2
                    ci = to % 2
                    for n in (0, 1):
                        at = pl.ds(pl.multiple_of(ci * 512 + n * 256, 256), 256)
                        slot[6 + 2 * yp + n : 7 + 2 * yp + n, :] = vec_rows[row, 6:7, at]
                        at = pl.ds(pl.multiple_of(n * 256 + ci * 128, 128), 128)
                        slot[10 + n : 11 + n, yp * 128 : yp * 128 + 128] = vec_rows[row, 7:8, at]
                slot[12:16, :] = jnp.zeros((4, 256), F32)
                if j > 0:
                    copy = remote(
                        self.si + 2 + j,
                        self.ri + 4 + c,
                        slot,
                        vec_cols.at[c],
                        (d, r, to),
                    )
                    copy.start()
                    later(copy)

        def to_pair(self):
            total = vec_out_parts[0]
            for j in (1, 2, 3):
                source = (c + j) % 4
                place = vec_cols.at[source]
                remote(self.si, self.ri + 4 + source, place, place, core_dev).wait_recv()
                total = total + vec_cols[source]
            vec_part[...] = total
            self.pair.start()
            later(self.pair)

        def done(self):
            self.pair.wait_recv()
            vec_out[...] = vec_part[...] + vec_pair[...]

    pull_attend(0)
    ag3[1].forward()
    g_up.second(1)
    pull_tokens(0)
    rs4[0].to_core()
    g_down.third(1)
    rs4[0].to_y()
    g_down.third(0)
    ag3[1].wait()
    pull_attend(1)
    qkv_grad()
    g_qkv.begin(1)
    g_up.third(1)
    out_grad()
    g_out.begin(1)
    g_out.begin(0)
    g_up.second(0)
    g_qkv.begin(0)
    pull_tokens(1)
    rs4[1].to_core()
    g_down.to_rows(0)
    rs4[1].to_y()
    sums = Sums()
    sums.to_rows()
    g_down.to_rows(1)
    tokens_done(0)
    g_up.to_rows(1)
    sums.to_cols()
    g_up.third(0)
    g_qkv.second(1)
    g_qkv.second(0)
    tokens_done(1)
    g_out.second(1)
    g_out.second(0)
    g_up.to_rows(0)
    send_lo(0)
    send_lo(1)
    g_qkv.third(1)
    g_out.third(1)
    g_out.third(0)
    g_qkv.third(0)
    g_qkv.to_rows(1)
    g_out.to_rows(1)
    g_out.to_rows(0)
    g_qkv.to_rows(0)
    sums.to_pair()
    sums.done()
    for grad in (g_down, g_up, g_qkv, g_out):
        grad.done()

    for s in (0, 1):
        rs3[s].sent()
        rs4[s].sent()
        tg_copy[s].wait()
        lo_own[s].wait()
        for j in (1, 2, 3):
            source = (r + j) % 4
            place = lo_place(s, source)
            remote(lo_s, lo_r + 4 * s + source, place, place, core_dev).wait_recv()
    for condition, copy in late:
        if condition is None:
            copy.wait_send()
        else:
            pl.when(condition)(copy.wait_send)


S_SEMS = 240
R_SEMS = 240
L_SEMS = 32


def run_layer(seg, x, og, wq, wo, wu, wd, bias, vecs):
    any_spec = pl.BlockSpec(memory_space=pl.ANY)
    vmem = pl.BlockSpec(memory_space=pltpu.VMEM)
    out = jax.ShapeDtypeStruct
    outs = [
        (out((2, SEQ, 256), BF), any_spec),
        (out((2, SEQ, 256), F32), any_spec),
        (out((2, 128, 768), BF), any_spec),
        (out((2, 2, 64, 256), BF), any_spec),
        (out((2, 128, D), BF), any_spec),
        (out((2, 2, 256, 256), BF), any_spec),
        (out((16, 256), F32), vmem),
    ]
    full = ((2, SEQ, D), BF)
    scratch = [
        ((8, SEQ), F32),
        ((4, 8, D), F32),
        full,
        ((4, 2, 128, 768), BF),
        ((2, 2, 64, D), BF),
        ((4, 2, 128, D), BF),
        ((2, 2, 256, D), BF),
        ((2, 128, 384), BF),
        ((2, 64, 256), BF),
        ((2, 128, 512), BF),
        ((2, 256, 256), BF),
        ((2, SEQ, 768), BF),
        ((2, 4, SEQ, SEQ), BF),
        ((2, SEQ, 256), BF),
        ((SEQ, SEQ), F32),
        full,
        ((2, 2, ROWS, D), BF),
        ((2, ROWS, D), BF),
        ((2, ROWS, D), BF),
        ((2, ROWS, D), F32),
        ((2, ROWS, 128), F32),
        full,
        full,
        full,
        ((2, ROWS, D), BF),
        ((2, ROWS, D), BF),
        ((2, ROWS, D), F32),
        full,
        full,
        full,
        ((SEQ, 256), BF),
        ((2, SEQ, 768), BF),
        ((2, 4, SEQ, 256), BF),
        ((2, 2, SEQ, 256), BF),
        ((2, SEQ, 256), BF),
        ((2, SEQ, 256), BF),
        ((2, SEQ, 256), F32),
        ((4, 2, 128, 768), BF),
        ((2, 2, 64, D), BF),
        ((4, 2, 128, D), BF),
        ((2, 2, 256, D), BF),
        ((2, 128, 384), BF),
        ((2, 128, 768), BF),
        ((2, 2, 64, 512), BF),
        ((2, 2, 128, D), BF),
        ((2, 256, 512), BF),
        ((256, 512), BF),
        ((2, 2, 2, 128, 384), BF),
        ((2, 2, 128, 384), BF),
        ((2, 2, 64, 512), BF),
        ((2, 2, 2, 128, 512), BF),
        ((2, 256, 512), BF),
        ((2, 2, 256, 512), BF),
        ((8, D), F32),
        ((4, 8, D), F32),
        ((4, 16, 256), F32),
        ((4, 16, 256), F32),
        ((16, 256), F32),
        ((16, 256), F32),
    ]
    return pl.pallas_call(
        layer_kernel,
        out_shape=[o[0] for o in outs],
        in_specs=[any_spec] * 7 + [vmem] * 2,
        out_specs=[o[1] for o in outs],
        scratch_shapes=[pltpu.VMEM(shape, dtype) for shape, dtype in scratch]
        + [
            pltpu.SemaphoreType.DMA((S_SEMS,)),
            pltpu.SemaphoreType.DMA((R_SEMS,)),
            pltpu.SemaphoreType.DMA((L_SEMS,)),
        ],
        compiler_params=pltpu.CompilerParams(
            collective_id=0, has_side_effects=True, vmem_limit_bytes=62 * 1024 * 1024
        ),
        name="layer",
    )(seg, x, og, wq, wo, wu, wd, bias, vecs)


def shards(
    pairs,
    tokens,
    segments,
    qkv_weight,
    qv_bias,
    out_weight,
    out_bias,
    norm1_gain,
    norm1_bias,
    up_weight,
    up_bias,
    down_weight,
    down_bias,
    norm2_gain,
    norm2_bias,
    out_grad,
):
    labels = jnp.pad(segments.astype(F32), ((0, 6), (0, 0)))
    wq = qkv_weight.reshape(256, 3, 2, 128).transpose(0, 2, 1, 3).reshape(2, 128, 768)
    bias = jnp.zeros((8, D), F32)
    bias = bias.at[0].set(up_bias).at[1, :512].set(qv_bias.reshape(512))
    vecs = jnp.stack(
        [out_bias, norm1_gain, norm1_bias, down_bias, norm2_gain, norm2_bias, out_bias, out_bias]
    )
    lo, tg, fin_q, fin_o, fin_u, fin_d, vec = run_layer(
        labels,
        tokens.reshape(2, SEQ, 256),
        out_grad.reshape(2, SEQ, 256),
        wq,
        out_weight.reshape(2, 2, 64, 256),
        up_weight.reshape(2, 128, D),
        down_weight.reshape(2, 2, 256, 256),
        bias,
        vecs,
    )
    grads = (fin_q, fin_o, fin_u, fin_d, vec)
    if pairs is not None:
        grads = lax.psum(grads, "dp", axis_index_groups=pairs)
    fin_q, fin_o, fin_u, fin_d, vec = grads
    fin_q = fin_q.reshape(256, 2, 3, 128).transpose(0, 2, 1, 3).reshape(256, 3, 256)
    return (
        lo.reshape(2 * SEQ, 256),
        tg.reshape(2 * SEQ, 256),
        fin_q.astype(F32),
        vec[10:12],
        fin_o.reshape(256, 256).astype(F32),
        vec[5],
        vec[2],
        vec[3],
        fin_u.reshape(256, D).astype(F32),
        vec[6:10].reshape(D),
        fin_d.reshape(D, 256).astype(F32),
        vec[4],
        vec[0],
        vec[1],
    )


def solution(mesh):
    placed = (
        P(("dp", "col"), "row"),
        P(("dp", "row"), None),
        P("row", None, "col"),
        P(None, "col"),
        P("col", "row"),
        P(),
        P(),
        P(),
        P("row", "col"),
        P("col"),
        P("col", "row"),
        P(),
        P(),
        P(),
        P(("dp", "col"), "row"),
    )
    dp = mesh.shape["dp"]
    pairs = None
    if dp > 2:
        pairs = [list(range(0, dp, 2)), list(range(1, dp, 2))]
    return jax.shard_map(
        functools.partial(shards, pairs),
        mesh=mesh,
        in_specs=placed,
        out_specs=(
            P(("dp", "col"), "row"),
            P(("dp", "col"), "row"),
            P("row", None, "col"),
            P(None, "col"),
            P("col", "row"),
            P("row"),
            P("row"),
            P("row"),
            P("row", "col"),
            P("col"),
            P("col", "row"),
            P("row"),
            P("row"),
            P("row"),
        ),
        check_vma=False,
    )
```

```python
import functools

import jax
import jax.numpy as jnp
from jax import lax
from jax.experimental import pallas as pl
from jax.experimental.pallas import tpu as pltpu
from jax.sharding import PartitionSpec as P

D = 1024
HEAD = 64
SEQ = 512
EPS = 1e-05
MESH = pl.DeviceIdType.MESH
BF = jnp.bfloat16
F32 = jnp.float32
ROWS = 128


def dot(left, right, left_dim, right_dim):
    return lax.dot_general(
        left, right, (((left_dim,), (right_dim,)), ((), ())), preferred_element_type=F32
    )


def al(index, step):
    return pl.multiple_of(index * step, step)


def col_sum(values):
    return jnp.sum(values, 0, keepdims=True)


def layer_kernel(
    seg_in,
    x_in,
    og_in,
    wq_in,
    wo_in,
    wu_in,
    wd_in,
    up_bias_in,
    qv_bias_in,
    out_bias_in,
    gain1_in,
    offset1_in,
    down_bias_in,
    gain2_in,
    offset2_in,
    lo_out,
    tg_out,
    fin_q,
    fin_o,
    fin_u,
    fin_d,
    vec_out,
    seg,
    bias_own,
    biases,
    xf,
    wq,
    wo,
    wu,
    wd,
    stage_q,
    stage_o,
    stage_u,
    stage_d,
    proj,
    probs,
    ctx,
    mask,
    part,
    rsc,
    rsy,
    ysend,
    normed1,
    inv1,
    hf,
    act,
    gelup,
    og,
    og_stage,
    lo,
    gsec,
    gdf,
    gu,
    gaf,
    gctx,
    gproj,
    partf,
    rscf,
    rsyf,
    ysendf,
    tg,
    gq,
    go,
    gup,
    gd,
    xq,
    xq1,
    xo,
    xu,
    xd,
    xd1,
    zq,
    zq1,
    zo,
    zu,
    zd,
    zd1,
    vec_sum,
    vec_rows,
    vec_out_parts,
    vec_cols,
    vec_part,
    vec_pair,
    ss,
    rs,
    ls,
):
    d = lax.axis_index("dp")
    r = lax.axis_index("row")
    c = lax.axis_index("col")
    y = r // 2
    k = r % 2
    p = d % 2
    r1 = r + 1 - 2 * k
    r2 = (r + 2) % 4
    r3 = (r1 + 2) % 4
    kc = c // 2
    ic = c % 2
    is_agg = k == kc
    core_dev = (d, r1, c)
    y_dev = (d, r2, c)
    x_dev = (d + 1 - 2 * p, r, c)

    counts = {"s": 0, "r": 0, "l": 0}

    def new(kind, n=1):
        at = counts[kind]
        counts[kind] += n
        return at

    def remote(si, ri, src, dst, dev):
        return pltpu.make_async_remote_copy(
            src_ref=src,
            dst_ref=dst,
            send_sem=ss.at[si],
            recv_sem=rs.at[ri],
            device_id=dev,
            device_id_type=MESH,
        )

    late = []

    def later(copy, condition=None):
        late.append((condition, copy))

    barrier = pltpu.get_barrier_semaphore()
    for j in (1, 2, 3):
        pl.semaphore_signal(barrier, inc=1, device_id=(d, (r + j) % 4, c), device_id_type=MESH)
        pl.semaphore_signal(barrier, inc=1, device_id=(d, r, (c + j) % 4), device_id_type=MESH)
    pl.semaphore_signal(barrier, inc=1, device_id=x_dev, device_id_type=MESH)

    @pl.when(r != c)
    def _():
        pl.semaphore_signal(barrier, inc=1, device_id=(d, c, r), device_id_type=MESH)
        pl.semaphore_wait(barrier, 8)

    @pl.when(r == c)
    def _():
        pl.semaphore_wait(barrier, 7)

    def qkv_piece(yp, n):
        return wq_in.at[n, :, :, pl.ds(al(yp, 128), 128)]

    def out_piece(yp, n):
        return wo_in.at[yp]

    def up_piece(yp, n):
        return wu_in.at[:, :, pl.ds(al(yp, 512), 512)]

    def down_piece(yp, n):
        return wd_in.at[yp]

    def qkv_place(row, n):
        return wq.at[row, :, :, pl.ds(pl.multiple_of(ic * 384 + n * 128, 128), 128)]

    def out_place(row, n):
        return wo.at[ic, :, :, pl.ds(al(row, 256), 256)]

    def up_place(row, n):
        return wu.at[row, :, :, pl.ds(al(ic, 512), 512)]

    def down_place(row, n):
        return wd.at[ic, :, :, pl.ds(al(row, 256), 256)]

    def qkv_half(ref, half, ci):
        return ref.at[:, half, :, pl.ds(al(ci, 384), 384)]

    def out_half(ref, half, ci):
        return ref.at[ci, half]

    def up_half(ref, half, ci):
        return ref.at[:, half, :, pl.ds(al(ci, 512), 512)]

    def down_half(ref, half, ci):
        return ref.at[ci, half]

    def qkv_chunk(ref, half, ci, chip):
        return ref.at[pl.ds(2 * chip, 2), half, :, pl.ds(al(ci, 384), 384)]

    def out_chunk(ref, half, ci, chip):
        return ref.at[ci, half, :, pl.ds(al(chip, 512), 512)]

    def up_chunk(ref, half, ci, chip):
        return ref.at[pl.ds(2 * chip, 2), half, :, pl.ds(al(ci, 512), 512)]

    down_chunk = out_chunk
    far_dev = (d, r, (c + 2) % 4)
    near_dev = (d, r, c + 1 - 2 * ic)

    class Weight:
        def __init__(self, buffer, piece, place, chunk, stages):
            self.piece, self.place, self.stages = piece, place, stages
            self.parts = range(len(stages))
            self.s1, self.r1, self.l1 = [], [], []
            self.relay_copies, self.staged = [], []
            for q, stage in enumerate(stages):
                self.s1.append(new("s", 2))
                self.r1.append(new("r", 4))
                self.l1.append(new("l"))
                self.relay_copies.append(
                    remote(new("s"), self.r1[q] + r2, stage, place(r2, q), core_dev)
                )
                self.staged.append(remote(self.s1[q], self.r1[q] + r2, stage, stage, y_dev))
            self.far_copy, self.near_copy, self.pair_far, self.pair_near = {}, {}, {}, {}
            for n in (0, 1):
                chip = y if n == 0 else 1 - y
                held = chunk(buffer, p, ic, chip)
                wanted = chunk(buffer, p, 1 - ic, chip)
                self.far_copy[n] = remote(new("s"), new("r"), held, held, far_dev)
                si, ri = new("s"), new("r")
                self.near_copy[n] = (
                    remote(si, ri, held, held, near_dev),
                    remote(si, ri, wanted, wanted, near_dev),
                )
                si, ri = new("s"), new("r")
                missing = chunk(buffer, 1 - p, ic, chip)
                self.pair_far[n] = (
                    remote(si, ri, held, held, x_dev),
                    remote(si, ri, missing, missing, x_dev),
                )
                si, ri = new("s"), new("r")
                missing = chunk(buffer, 1 - p, 1 - ic, chip)
                self.pair_near[n] = (
                    remote(si, ri, wanted, wanted, x_dev),
                    remote(si, ri, missing, missing, x_dev),
                )

        def spread_rows(self):
            self.own = []
            for q in self.parts:
                mine, to = self.piece(y, q), self.place(r, q)
                across = self.piece(1 - y, q)
                near = remote(self.s1[q] + 1, self.r1[q] + r, mine, to, core_dev)
                own = pltpu.make_async_copy(mine, to, ls.at[self.l1[q]])
                direct = remote(self.s1[q], self.r1[q] + r, across, to, y_dev)
                staged = remote(self.s1[q], self.r1[q] + r, across, self.stages[q], y_dev)

                @pl.when(jnp.logical_not(is_agg))
                def _():
                    near.start()
                    staged.start()

                @pl.when(is_agg)
                def _():
                    own.start()
                    direct.start()

                later(near, jnp.logical_not(is_agg))
                later(direct)
                self.own.append(own)

        def relay(self):
            @pl.when(jnp.logical_not(is_agg))
            def _():
                for q in self.parts:
                    self.staged[q].wait_recv()
                    self.relay_copies[q].start()

            for copy in self.relay_copies:
                later(copy, jnp.logical_not(is_agg))

        def lead(self, n):
            copies = (self.far_copy[n], self.near_copy[n][0])

            @pl.when(is_agg)
            def _():
                rows = [r1] if n == 0 else [r2, r3]
                for q in self.parts:
                    if n == 0:
                        self.own[q].wait()
                    for row in rows:
                        place = self.place(row, q)
                        remote(self.s1[q], self.r1[q] + row, place, place, core_dev).wait_recv()
                for copy in copies:
                    copy.start()

            for copy in copies:
                later(copy, is_agg)

        def follow(self, n):
            copies = (self.near_copy[n][0], self.pair_far[n][0])
            other = jnp.logical_not(is_agg)

            @pl.when(other)
            def _():
                self.far_copy[n].wait_recv()
                for copy in copies:
                    copy.start()

            for copy in copies:
                later(copy, other)

        def pair(self, n):
            self.near_copy[n][1].wait_recv()
            self.pair_near[n][0].start()
            later(self.pair_near[n][0])

        def ready(self):
            for n in (0, 1):

                @pl.when(jnp.logical_not(is_agg))
                def _():
                    self.pair_far[n][1].wait_recv()

                self.pair_near[n][1].wait_recv()

    w_qkv = Weight(wq, qkv_piece, qkv_place, qkv_chunk, [stage_q.at[q] for q in (0, 1, 2)])
    w_out = Weight(wo, out_piece, out_place, out_chunk, [stage_o])
    w_up = Weight(wu, up_piece, up_place, up_chunk, [stage_u])
    w_down = Weight(wd, down_piece, down_place, down_chunk, [stage_d])

    def rows_of(ref, s, row):
        return ref.at[s, pl.ds(al(row, ROWS), ROWS), :]

    def slab_of(ref, s, row):
        return ref.at[s, :, pl.ds(al(row, 256), 256)]

    class Gather:
        def __init__(self, full, at, s, source=None):
            self.full, self.at, self.s = full, at, s
            self.source = source
            self.si, self.ri = [new("s"), new("s"), new("s")], new("r", 3)

        def send(self):
            mine = self.source if self.source is not None else self.at(self.full, self.s, r)
            place = self.at(self.full, self.s, r)
            for n, dev in ((0, y_dev), (1, core_dev)):
                copy = remote(self.si[n], self.ri + n, mine, place, dev)
                copy.start()
                later(copy)

        def forward(self):
            place = self.at(self.full, self.s, r2)
            remote(self.si[0], self.ri, place, place, y_dev).wait_recv()
            copy = remote(self.si[2], self.ri + 2, place, place, core_dev)
            copy.start()
            later(copy)

        def wait(self):
            near = self.at(self.full, self.s, r1)
            remote(self.si[1], self.ri + 1, near, near, core_dev).wait_recv()
            far = self.at(self.full, self.s, r3)
            remote(self.si[2], self.ri + 2, far, far, core_dev).wait_recv()

    class Scatter:
        def __init__(self, source, at, core_recv, y_send, y_recv, s):
            self.source, self.at = source, at
            self.core_recv, self.y_send, self.y_recv, self.s = core_recv, y_send, y_recv, s
            si, ri = [new("s"), new("s"), new("s")], new("r", 3)
            self.far = remote(si[0], ri, at(source, s, r3), core_recv.at[s, 1], core_dev)
            self.near = remote(si[1], ri + 1, at(source, s, r1), core_recv.at[s, 0], core_dev)
            self.cross = remote(si[2], ri + 2, y_send.at[s], y_recv.at[s], y_dev)

        def to_core(self):
            self.far.start()
            self.near.start()

        def to_y(self):
            self.far.wait_recv()
            total = self.at(self.source, self.s, r2)[...].astype(F32)
            self.y_send[self.s] = (total + self.core_recv[self.s, 1].astype(F32)).astype(BF)
            self.cross.start()

        def result(self):
            self.near.wait_recv()
            total = self.at(self.source, self.s, r)[...].astype(F32)
            total = total + self.core_recv[self.s, 0].astype(F32)
            self.cross.wait_recv()
            return total + self.y_recv[self.s].astype(F32)

        def sent(self):
            self.far.wait_send()
            self.near.wait_send()
            self.cross.wait_send()

    w_qkv.spread_rows()
    x_gather = [Gather(xf, slab_of, s, x_in.at[s]) for s in (0, 1)]
    x_own = [
        pltpu.make_async_copy(x_in.at[s], slab_of(xf, s, r), ls.at[new("l")]) for s in (0, 1)
    ]
    seg_s, seg_r, seg_l = new("s"), new("r"), new("l")
    seg_copy = remote(seg_s, seg_r, seg_in, seg, (d, c, r))
    seg_own = pltpu.make_async_copy(seg_in, seg, ls.at[seg_l])

    @pl.when(r != c)
    def _():
        seg_copy.start()

    @pl.when(r == c)
    def _():
        seg_own.start()

    bias_s, bias_r = new("s", 3), new("r", 4)
    bias_own[...] = jnp.zeros_like(bias_own)
    bias_own[0:1, :] = up_bias_in[...]
    bias_own[1:2, 0:256] = qv_bias_in[0:1, :]
    bias_own[1:2, 256:512] = qv_bias_in[1:2, :]
    for j in (1, 2, 3):
        copy = remote(bias_s + j - 1, bias_r + c, bias_own, biases.at[c], (d, r, (c + j) % 4))
        copy.start()
        later(copy)
    biases[c] = bias_own[...]
    w_out.spread_rows()
    for s in (0, 1):
        x_gather[s].send()
        x_own[s].start()

    w_up.spread_rows()
    w_down.spread_rows()
    og_s, og_r, og_l = new("s", 4), new("r", 5), new("l")

    def og_place(row):
        return og.at[:, :, pl.ds(al(row, 256), 256)]

    def og_rows(row):
        return og_in.at[:, pl.ds(al(row, ROWS), ROWS), :]

    og_own = pltpu.make_async_copy(og_rows(r), og_place(r), ls.at[og_l])
    og_own.start()
    og_copies = [
        remote(og_s, og_r + r, og_rows(r1), og_place(r), core_dev),
        remote(og_s + 1, og_r + r, og_rows(r2), og_place(r), y_dev),
        remote(og_s + 2, og_r + 4, og_rows(r3), og_stage, y_dev),
    ]
    for copy in og_copies:
        copy.start()
        later(copy)
    og_relay = remote(og_s + 3, og_r + r2, og_stage, og_place(r2), core_dev)

    def relay_og():
        remote(og_s + 2, og_r + 4, og_stage, og_stage, y_dev).wait_recv()
        og_relay.start()
        later(og_relay)

    def wait_og():
        og_own.wait()
        for j in (1, 2, 3):
            place = og_place((r + j) % 4)
            remote(og_s, og_r + (r + j) % 4, place, place, core_dev).wait_recv()

    w_qkv.lead(0)
    w_qkv.relay()
    w_out.relay()
    w_qkv.follow(0)
    w_qkv.lead(1)
    w_out.lead(0)
    w_out.lead(1)
    w_up.lead(0)
    w_qkv.pair(0)
    w_qkv.follow(1)
    x_gather[0].forward()
    w_out.follow(0)
    w_qkv.pair(1)
    w_out.follow(1)
    x_gather[1].forward()
    w_out.pair(0)
    w_out.pair(1)
    w_up.relay()

    for j in (1, 2, 3):
        source = (c + j) % 4
        remote(bias_s, bias_r + source, biases.at[source], biases.at[source], core_dev).wait_recv()

    @pl.when(r != c)
    def _():
        seg_copy.wait_recv()

    @pl.when(r == c)
    def _():
        seg_own.wait()

    later(seg_copy, r != c)
    w_qkv.ready()

    vec_sum[...] = jnp.zeros_like(vec_sum)

    def project(s):
        rows = xf[s]

        def half(ci, carry):
            weight = wq[:, :, :, pl.ds(al(ci, 384), 384)].reshape(D, 384)
            q_bias = biases[2 * k + ci, 1:2, pl.ds(al(y, 128), 128)]
            v_bias = biases[2 * k + ci, 1:2, pl.ds(pl.multiple_of(256 + y * 128, 128), 128)]
            bias = jnp.concatenate([q_bias, jnp.zeros_like(q_bias), v_bias], 1)
            proj[s, :, pl.ds(al(ci, 384), 384)] = (dot(rows, weight, 1, 0) + bias).astype(BF)
            return carry

        lax.fori_loop(0, 2, half, 0)

    def columns(ci, n):
        return pl.ds(pl.multiple_of(ci * 384 + n * 128, 128), 128)

    def attend(s):
        labels = seg[s : s + 1, :].astype(F32)
        down = jnp.transpose(jnp.broadcast_to(labels, (128, SEQ)))[:, 0:1]
        mask[...] = jnp.where(down == labels, 0.0, -1e30)
        lane = lax.broadcasted_iota(jnp.int32, (SEQ, 128), 1)
        row = lax.broadcasted_iota(jnp.int32, (128, SEQ), 0)

        def pair(ci, carry):
            queries = proj[s, :, columns(ci, 0)]
            keys_in = proj[s, :, columns(ci, 1)]
            values_in = proj[s, :, columns(ci, 2)]
            parts = []
            for h in (0, 1):
                chosen = (lane < HEAD) if h == 0 else (lane >= HEAD)
                masked = jnp.where(chosen, queries, jnp.zeros_like(queries))
                scores = dot(keys_in, masked, 1, 1) * (float(HEAD) ** (-0.5)) + mask[...]
                weights = jnp.exp(scores - jnp.max(scores, 0, keepdims=True))
                totals = jnp.sum(weights, 0, keepdims=True)
                share = (weights * (1.0 / totals)).astype(BF)
                probs[s, ci * 2 + h] = share
                parts.append(dot(values_in, share, 0, 0))
            both = jnp.where(row < HEAD, parts[0], parts[1])
            ctx[s, :, pl.ds(al(ci, 128), 128)] = jnp.transpose(both).astype(BF)
            return carry

        lax.fori_loop(0, 2, pair, 0)

    def out_partial(s):
        part[s] = dot(ctx[s], wo[...].reshape(256, D), 1, 0).astype(BF)

    def norm_stats(summed):
        center = jnp.sum(summed, 1, keepdims=True) * (1.0 / D)
        spread = jnp.sum(summed * summed, 1, keepdims=True) * (1.0 / D) - center * center
        inverse = lax.rsqrt(spread + EPS)
        return (summed - center) * inverse, inverse

    def norm_pull(grad, normed, inverse, gain):
        scaled = grad * gain
        first = jnp.sum(scaled, 1, keepdims=True) * (1.0 / D)
        second = jnp.sum(scaled * normed, 1, keepdims=True) * (1.0 / D)
        return inverse * (scaled - first - normed * second)

    out_bias, gain1, offset1 = out_bias_in[...], gain1_in[...], offset1_in[...]
    down_bias, gain2, offset2 = down_bias_in[...], gain2_in[...], offset2_in[...]
    own_rows = pl.ds(al(r, ROWS), ROWS)

    def scatters():
        return [Scatter(part, rows_of, rsc, ysend, rsy, s) for s in (0, 1)]

    rs1 = scatters()
    ag1 = [Gather(hf, rows_of, s) for s in (0, 1)]

    def first_norm(s):
        first_sum = rs1[s].result() + out_bias + xf[s, own_rows, :].astype(F32)
        normed, inverse = norm_stats(first_sum)
        normed1[s] = normed
        inv1[s] = jnp.broadcast_to(inverse, (ROWS, 128))
        hf[s, own_rows, :] = (normed * gain1 + offset1).astype(BF)
        ag1[s].send()

    x_own[0].wait()
    x_gather[0].wait()
    project(0)
    w_up.lead(1)
    w_up.follow(0)
    attend(0)
    w_out.ready()
    out_partial(0)
    rs1[0].to_core()
    w_down.relay()
    w_down.lead(0)
    w_down.lead(1)
    rs1[0].to_y()
    x_own[1].wait()
    x_gather[1].wait()
    project(1)
    w_up.follow(1)
    attend(1)
    out_partial(1)
    rs1[1].to_core()
    rs1[1].to_y()
    w_up.pair(0)
    w_down.follow(0)
    first_norm(0)
    w_up.pair(1)
    w_down.follow(1)
    w_down.pair(0)
    first_norm(1)
    w_down.pair(1)
    ag1[0].forward()
    w_up.ready()
    ag1[0].wait()

    def up_bias_of(ci):
        return biases[2 * k + ci, 0:1, pl.ds(al(y, 512), 512)]

    def mlp_up(s):
        rows = hf[s]

        def tile(n, carry):
            cols = pl.ds(al(n, 256), 256)
            weight = wu[:, :, :, cols].reshape(D, 256)
            ci = n // 2
            bias = biases[2 * k + ci, 0:1, pl.ds(pl.multiple_of(y * 512 + (n % 2) * 256, 256), 256)]
            upward = dot(rows, weight, 1, 0) + bias
            share = 0.5 + 0.5 * lax.erf(upward * 0.7071067811865476)
            act[s, :, cols] = (upward * share).astype(BF)
            density = jnp.exp(-0.5 * upward * upward) * 0.3989422804014327
            gelup[s, :, cols] = (share + upward * density).astype(BF)
            return carry

        lax.fori_loop(0, 4, tile, 0)

    def mlp_down(s):
        rows = act[s]

        def tile(n, carry):
            cols = pl.ds(al(n, 256), 256)
            weight = wd[:, :, :, cols].reshape(D, 256)
            part[s, :, cols] = dot(rows, weight, 1, 0).astype(BF)
            return carry

        lax.fori_loop(0, 4, tile, 0)

    rs2 = scatters()
    ag2 = [Gather(gdf, rows_of, s) for s in (0, 1)]
    lo_s, lo_r, lo_l = new("s", 6), new("r", 8), new("l", 2)

    def second_norm(s):
        hidden = normed1[s] * gain1 + offset1
        second_sum = rs2[s].result() + down_bias + hidden
        normed, inverse = norm_stats(second_sum)
        lo[s] = (normed * gain2 + offset2).astype(BF)
        grad = og[s].astype(F32)
        vec_sum[0:1, :] += col_sum(grad * normed)
        vec_sum[1:2, :] += col_sum(grad)
        grad_second = norm_pull(grad, normed, inverse, gain2)
        gsec[s] = grad_second
        rounded = grad_second.astype(BF)
        vec_sum[4:5, :] += col_sum(rounded.astype(F32))
        gdf[s, own_rows, :] = rounded
        ag2[s].send()

    def lo_place(s, row):
        return lo_out.at[s, pl.ds(al(row, ROWS), ROWS), :]

    def lo_part(s, row):
        return lo.at[s, :, pl.ds(al(row, 256), 256)]

    lo_own = [
        pltpu.make_async_copy(lo_part(s, r), lo_place(s, r), ls.at[lo_l + s]) for s in (0, 1)
    ]

    def send_lo(s):
        lo_own[s].start()
        for j in (1, 2, 3):
            row = (r + j) % 4
            copy = remote(
                lo_s + 3 * s + j - 1, lo_r + 4 * s + r, lo_part(s, row), lo_place(s, r), (d, row, c)
            )
            copy.start()
            later(copy)

    mlp_up(0)
    ag1[1].forward()
    relay_og()
    w_down.ready()
    rs1[0].sent()
    mlp_down(0)
    rs2[0].to_core()
    rs2[0].to_y()
    ag1[1].wait()
    mlp_up(1)
    rs1[1].sent()
    mlp_down(1)
    rs2[1].to_core()
    rs2[1].to_y()
    wait_og()
    second_norm(0)
    second_norm(1)
    ag2[0].forward()
    ag2[0].wait()

    class Grad:
        def __init__(self, buffer, chunk, both, by_ci, pair_recv, col_recv, place, pair_first):
            self.buffer, self.place, self.pair_first = buffer, place, pair_first
            pair_recvs, col_recvs = pair_recv, col_recv
            self.near_copy, self.far_copy, self.pair_copy = {}, {}, {}
            self.near_add, self.far_add, self.pair_add = {}, {}, {}
            self.own, self.rows_copies = None, {}
            self.chunk = chunk
            self.s3, self.r3, self.l3 = new("s", 7), new("r", 4), new("l")
            for n in (0, 1):
                chip = y if n == 0 else 1 - y
                pair_recv, col_recv = pair_recvs[n], col_recvs[n]
                if pair_first[n]:
                    pair_src, pair_dst = both(buffer, 1 - p, chip), both(buffer, p, chip)
                    near_src, held = chunk(buffer, p, 1 - ic, chip), chunk(buffer, p, ic, chip)
                else:
                    pair_src, pair_dst = chunk(buffer, 1 - p, ic, chip), chunk(buffer, p, ic, chip)
                    near_src, held = by_ci(buffer, 1 - ic, chip), by_ci(buffer, ic, chip)
                self.pair_copy[n] = remote(new("s"), new("r"), pair_src, pair_recv, x_dev)
                self.near_copy[n] = remote(new("s"), new("r"), near_src, col_recv.at[0], near_dev)
                self.far_copy[n] = remote(new("s"), new("r"), held, col_recv.at[1], far_dev)
                self.pair_add[n] = (pair_dst, pair_recv)
                self.near_add[n] = (held, col_recv.at[0])
                self.far_add[n] = (held, col_recv.at[1])

        def add(self, refs):
            mine, other = refs
            mine[...] = (mine[...].astype(F32) + other[...].astype(F32)).astype(BF)

        def arrival(self, half, yp):
            return self.r3 + 2 * half + yp

        def rows_of_chunk(self, n):
            copies = []
            here, there = d, d + 1 - 2 * p
            if n == 0:
                self.own = pltpu.make_async_copy(self.piece(r), self.place(p, y), ls.at[self.l3])
                targets = [(here, r1), (there, r), (there, r1)]
                at = 0
            else:
                targets = [(here, r2), (there, r2), (here, r3), (there, r3)]
                at = 3
            for plane, row in targets:
                copies.append(
                    remote(
                        self.s3 + at,
                        self.arrival(p, y),
                        self.piece(row),
                        self.place(p, y),
                        (plane, row, c),
                    )
                )
                at += 1
            return copies

        def begin(self, n):
            first = self.pair_copy[n] if self.pair_first[n] else self.near_copy[n]
            first.start()
            later(first)

        def second(self, n):
            if self.pair_first[n]:
                self.pair_copy[n].wait_recv()
                self.add(self.pair_add[n])
                self.near_copy[n].start()
                later(self.near_copy[n])
            else:
                self.near_copy[n].wait_recv()
                self.add(self.near_add[n])

                @pl.when(jnp.logical_not(is_agg))
                def _():
                    self.far_copy[n].start()

                later(self.far_copy[n], jnp.logical_not(is_agg))

        def third(self, n):
            if self.pair_first[n]:
                self.near_copy[n].wait_recv()
                self.add(self.near_add[n])

                @pl.when(jnp.logical_not(is_agg))
                def _():
                    self.far_copy[n].start()

                later(self.far_copy[n], jnp.logical_not(is_agg))
            else:

                @pl.when(is_agg)
                def _():
                    self.far_copy[n].wait_recv()
                    self.add(self.far_add[n])
                    self.pair_copy[n].start()

                later(self.pair_copy[n], is_agg)

        def to_rows(self, n):
            copies = self.rows_of_chunk(n)

            @pl.when(is_agg)
            def _():
                if self.pair_first[n]:
                    self.far_copy[n].wait_recv()
                    self.add(self.far_add[n])
                else:
                    self.pair_copy[n].wait_recv()
                    self.add(self.pair_add[n])
                if n == 0:
                    self.own.start()
                for copy in copies:
                    copy.start()

            for copy in copies:
                later(copy, is_agg)

        def done(self):
            @pl.when(is_agg)
            def _():
                self.own.wait()

            @pl.when(jnp.logical_not(is_agg))
            def _():
                place = self.place(p, y)
                remote(self.s3, self.arrival(p, y), place, place, core_dev).wait_recv()

            for half, yp in ((p, 1 - y), (1 - p, y), (1 - p, 1 - y)):
                place = self.place(half, yp)
                remote(self.s3, self.arrival(half, yp), place, place, core_dev).wait_recv()

    def rows_both(ref, half, chip):
        return ref.at[pl.ds(2 * chip, 2), half]

    def cols_both(ref, half, chip):
        return ref.at[:, half, :, pl.ds(al(chip, 512), 512)]

    def cols_of_ci(ref, ci, chip):
        return ref.at[ci, :, :, pl.ds(al(chip, 512), 512)]

    def rows_of_ci(ref, ci, chip):
        return ref.at[pl.ds(2 * chip, 2), :, :, pl.ds(al(ci, 384), 384)]

    def two(ref):
        return [ref.at[0], ref.at[1]]

    g_qkv = Grad(
        gq,
        qkv_chunk,
        rows_both,
        rows_of_ci,
        [xq, xq1],
        [zq, zq1],
        lambda half, yp: fin_q.at[half, :, pl.ds(al(yp, 384), 384)],
        (False, True),
    )
    g_qkv.piece = lambda row: gq.at[row, p, :, pl.ds(al(ic, 384), 384)]
    g_out = Grad(
        go, out_chunk, cols_both, None, two(xo), two(zo), lambda half, yp: fin_o.at[yp, half], (True, True)
    )
    g_out.piece = lambda row: go.at[ic, p, :, pl.ds(al(row, 256), 256)]
    g_up = Grad(
        gup,
        up_chunk,
        rows_both,
        None,
        two(xu),
        two(zu),
        lambda half, yp: fin_u.at[half, :, pl.ds(al(yp, 512), 512)],
        (True, True),
    )
    g_up.piece = lambda row: gup.at[row, p, :, pl.ds(al(ic, 512), 512)]
    g_down = Grad(
        gd,
        down_chunk,
        cols_both,
        cols_of_ci,
        [xd, xd1],
        [zd, zd1],
        lambda half, yp: fin_d.at[yp, half],
        (True, False),
    )
    g_down.piece = lambda row: gd.at[ic, p, :, pl.ds(al(row, 256), 256)]

    def tokens_by(ref, cols):
        return ref[:, :, cols].reshape(2 * SEQ, cols.size)

    def down_grad():
        def tile(n, carry):
            left = tokens_by(act, pl.ds(al(n, 256), 256))
            gd[n // 2, n % 2] = dot(left, gdf[...].reshape(2 * SEQ, D), 0, 0).astype(BF)
            return carry

        lax.fori_loop(0, 4, tile, 0)

    def up_grad():
        def tile(n, carry):
            left = tokens_by(hf, pl.ds(al(n, 256), 256))
            gup[n] = (
                dot(left, gu[...].reshape(2 * SEQ, D), 0, 0).astype(BF).reshape(2, 128, D)
            )
            return carry

        lax.fori_loop(0, 4, tile, 0)

    def out_grad():
        left = ctx[...].reshape(2 * SEQ, 256)
        go[...] = dot(left, gaf[...].reshape(2 * SEQ, D), 0, 0).astype(BF).reshape(2, 2, 64, D)

    def qkv_grad():
        def tile(n, carry):
            left = tokens_by(xf, pl.ds(al(n, 256), 256))
            gq[n] = (
                dot(left, gproj[...].reshape(2 * SEQ, 768), 0, 0).astype(BF).reshape(2, 128, 768)
            )
            return carry

        lax.fori_loop(0, 4, tile, 0)

    def pull_act(s):
        rows = gdf[s]

        def tile(n, carry):
            cols = pl.ds(al(n, 256), 256)
            grad = dot(rows, wd[n // 2, n % 2], 1, 1) * gelup[s, :, cols].astype(F32)
            rounded = grad.astype(BF)
            gu[s, :, cols] = rounded
            vec_sum[6:7, cols] += col_sum(rounded.astype(F32))
            return carry

        lax.fori_loop(0, 4, tile, 0)

    def pull_hidden(s):
        rows = gu[s]

        def tile(n, carry):
            weight = wu[n].reshape(256, D)
            part[s, :, pl.ds(al(n, 256), 256)] = dot(rows, weight, 1, 1).astype(BF)
            return carry

        lax.fori_loop(0, 4, tile, 0)

    rs3 = scatters()
    ag3 = [Gather(gaf, rows_of, s) for s in (0, 1)]

    def first_norm_pull(s):
        grad = gsec[s] + rs3[s].result()
        normed = normed1[s]
        vec_sum[2:3, :] += col_sum(grad * normed)
        vec_sum[3:4, :] += col_sum(grad)
        rounded = norm_pull(grad, normed, inv1[s][:, 0:1], gain1).astype(BF)
        vec_sum[5:6, :] += col_sum(rounded.astype(F32))
        gaf[s, own_rows, :] = rounded
        ag3[s].send()

    pull_act(0)
    rs2[0].sent()
    pull_hidden(0)
    rs3[0].to_core()
    ag2[1].forward()
    rs3[0].to_y()
    ag2[1].wait()
    down_grad()
    g_down.begin(1)
    g_down.begin(0)
    pull_act(1)
    rs2[1].sent()
    pull_hidden(1)
    rs3[1].to_core()
    rs3[1].to_y()
    first_norm_pull(0)
    up_grad()
    g_up.begin(1)
    g_up.begin(0)
    g_down.second(1)
    g_down.second(0)
    first_norm_pull(1)
    ag3[0].forward()
    ag3[0].wait()

    def pull_attend(s):
        gctx[...] = dot(gaf[s], wo[...].reshape(256, D), 1, 1).astype(BF)
        lane = lax.broadcasted_iota(jnp.int32, (SEQ, 128), 1)
        row = lax.broadcasted_iota(jnp.int32, (128, SEQ), 0)
        scale_factor = float(HEAD) ** (-0.5)

        def pair(ci, carry):
            queries = proj[s, :, columns(ci, 0)]
            keys_in = proj[s, :, columns(ci, 1)]
            values_in = proj[s, :, columns(ci, 2)]
            grad = gctx[:, pl.ds(al(ci, 128), 128)]
            grads_q, grads_k, grads_v = [], [], []
            for h in (0, 1):
                chosen = (lane < HEAD) if h == 0 else (lane >= HEAD)
                masked = jnp.where(chosen, grad, jnp.zeros_like(grad))
                share = probs[s, ci * 2 + h]
                wide = share.astype(F32)
                weighted = wide * dot(values_in, masked, 1, 1)
                total = jnp.sum(weighted, 0, keepdims=True)
                grad_scores = (weighted - wide * total).astype(BF)
                grads_v.append(dot(share, grad, 1, 0))
                grads_k.append(dot(grad_scores, queries, 1, 0))
                grads_q.append(dot(keys_in, grad_scores, 0, 0))
            both_q = jnp.transpose(jnp.where(row < HEAD, grads_q[0], grads_q[1]) * scale_factor)
            both_q = both_q.astype(BF)
            both_v = jnp.where(lane < HEAD, grads_v[0], grads_v[1]).astype(BF)
            both_k = jnp.where(lane < HEAD, grads_k[0], grads_k[1]) * scale_factor
            gproj[s, :, columns(ci, 0)] = both_q
            gproj[s, :, columns(ci, 1)] = both_k.astype(BF)
            gproj[s, :, columns(ci, 2)] = both_v
            at = pl.ds(al(ci, 128), 128)
            vec_sum[7:8, at] += col_sum(both_q.astype(F32))
            at = pl.ds(pl.multiple_of(256 + ci * 128, 128), 128)
            vec_sum[7:8, at] += col_sum(both_v.astype(F32))
            return carry

        lax.fori_loop(0, 2, pair, 0)

    def pull_tokens(s):
        rows = gproj[s]

        def tile(n, carry):
            partf[s, n] = dot(rows, wq[n].reshape(256, 768), 1, 1).astype(BF)
            return carry

        lax.fori_loop(0, 4, tile, 0)

    rs4 = [Scatter(partf, lambda ref, s, row: ref.at[s, row], rscf, ysendf, rsyf, s) for s in (0, 1)]
    tg_l = new("l", 2)
    tg_copy = [pltpu.make_async_copy(tg.at[s], tg_out.at[s], ls.at[tg_l + s]) for s in (0, 1)]

    def tokens_done(s):
        tg[s] = rs4[s].result() + slab_of(gaf, s, r)[...].astype(F32)
        tg_copy[s].start()

    class Sums:
        def __init__(self):
            self.si, self.ri = new("s", 7), new("r", 9)
            self.pair = remote(self.si + 6, self.ri + 8, vec_part, vec_pair, x_dev)

        def to_rows(self):
            vec_rows[r] = vec_sum[...]
            for j in (1, 2, 3):
                copy = remote(
                    self.si + j - 1, self.ri + r, vec_sum, vec_rows.at[r], (d, (r + j) % 4, c)
                )
                copy.start()
                later(copy)

        def to_cols(self):
            for j in (1, 2, 3):
                place = vec_rows.at[(r + j) % 4]
                remote(self.si, self.ri + (r + j) % 4, place, place, core_dev).wait_recv()
            mine = pl.ds(al(r, 256), 256)
            features = vec_rows[0, 0:6, mine] + vec_rows[1, 0:6, mine]
            features = features + vec_rows[2, 0:6, mine] + vec_rows[3, 0:6, mine]
            for j in (0, 1, 2, 3):
                to = (c + j) % 4
                slot = vec_out_parts.at[j]
                slot[0:6, :] = features
                for yp in (0, 1):
                    row = 2 * yp + to // 2
                    ci = to % 2
                    for n in (0, 1):
                        at = pl.ds(pl.multiple_of(ci * 512 + n * 256, 256), 256)
                        slot[6 + 2 * yp + n : 7 + 2 * yp + n, :] = vec_rows[row, 6:7, at]
                        at = pl.ds(pl.multiple_of(n * 256 + ci * 128, 128), 128)
                        slot[10 + n : 11 + n, yp * 128 : yp * 128 + 128] = vec_rows[row, 7:8, at]
                slot[12:16, :] = jnp.zeros((4, 256), F32)
                if j > 0:
                    copy = remote(
                        self.si + 2 + j,
                        self.ri + 4 + c,
                        slot,
                        vec_cols.at[c],
                        (d, r, to),
                    )
                    copy.start()
                    later(copy)

        def to_pair(self):
            total = vec_out_parts[0]
            for j in (1, 2, 3):
                source = (c + j) % 4
                place = vec_cols.at[source]
                remote(self.si, self.ri + 4 + source, place, place, core_dev).wait_recv()
                total = total + vec_cols[source]
            vec_part[...] = total
            self.pair.start()
            later(self.pair)

        def done(self):
            self.pair.wait_recv()
            vec_out[...] = vec_part[...] + vec_pair[...]

    pull_attend(0)
    ag3[1].forward()
    g_up.second(1)
    pull_tokens(0)
    rs4[0].to_core()
    g_down.third(1)
    rs4[0].to_y()
    g_down.third(0)
    ag3[1].wait()
    pull_attend(1)
    sums = Sums()
    sums.to_rows()
    qkv_grad()
    g_qkv.begin(1)
    g_up.third(1)
    out_grad()
    g_out.begin(1)
    g_out.begin(0)
    g_up.second(0)
    g_qkv.begin(0)
    pull_tokens(1)
    rs4[1].to_core()
    g_down.to_rows(0)
    rs4[1].to_y()
    g_down.to_rows(1)
    tokens_done(0)
    g_up.to_rows(1)
    sums.to_cols()
    g_up.third(0)
    g_qkv.second(1)
    g_qkv.second(0)
    tokens_done(1)
    g_out.second(1)
    g_out.second(0)
    g_up.to_rows(0)
    send_lo(0)
    send_lo(1)
    g_qkv.third(1)
    g_out.third(1)
    g_out.third(0)
    g_qkv.third(0)
    g_qkv.to_rows(1)
    g_out.to_rows(1)
    g_out.to_rows(0)
    g_qkv.to_rows(0)
    sums.to_pair()
    sums.done()
    for grad in (g_down, g_up, g_qkv, g_out):
        grad.done()

    for s in (0, 1):
        rs3[s].sent()
        rs4[s].sent()
        tg_copy[s].wait()
        lo_own[s].wait()
        for j in (1, 2, 3):
            source = (r + j) % 4
            place = lo_place(s, source)
            remote(lo_s, lo_r + 4 * s + source, place, place, core_dev).wait_recv()
    for condition, copy in late:
        if condition is None:
            copy.wait_send()
        else:
            pl.when(condition)(copy.wait_send)


S_SEMS = 240
R_SEMS = 240
L_SEMS = 32


def run_layer(seg, x, og, wq, wo, wu, wd, *vecs):
    any_spec = pl.BlockSpec(memory_space=pl.ANY)
    vmem = pl.BlockSpec(memory_space=pltpu.VMEM)
    out = jax.ShapeDtypeStruct
    outs = [
        (out((2, SEQ, 256), BF), any_spec),
        (out((2, SEQ, 256), F32), any_spec),
        (out((2, 128, 768), BF), any_spec),
        (out((2, 2, 64, 256), BF), any_spec),
        (out((2, 128, D), BF), any_spec),
        (out((2, 2, 256, 256), BF), any_spec),
        (out((16, 256), F32), vmem),
    ]
    full = ((2, SEQ, D), BF)
    scratch = [
        ((2, SEQ), jnp.int32),
        ((8, D), F32),
        ((4, 8, D), F32),
        full,
        ((4, 2, 128, 768), BF),
        ((2, 2, 64, D), BF),
        ((4, 2, 128, D), BF),
        ((2, 2, 256, D), BF),
        ((3, 2, 128, 128), BF),
        ((2, 64, 256), BF),
        ((2, 128, 512), BF),
        ((2, 256, 256), BF),
        ((2, SEQ, 768), BF),
        ((2, 4, SEQ, SEQ), BF),
        ((2, SEQ, 256), BF),
        ((SEQ, SEQ), F32),
        full,
        ((2, 2, ROWS, D), BF),
        ((2, ROWS, D), BF),
        ((2, ROWS, D), BF),
        ((2, ROWS, D), F32),
        ((2, ROWS, 128), F32),
        full,
        full,
        full,
        ((2, ROWS, D), BF),
        ((2, ROWS, 256), BF),
        ((2, ROWS, D), BF),
        ((2, ROWS, D), F32),
        full,
        full,
        full,
        ((SEQ, 256), BF),
        ((2, SEQ, 768), BF),
        ((2, 4, SEQ, 256), BF),
        ((2, 2, SEQ, 256), BF),
        ((2, SEQ, 256), BF),
        ((2, SEQ, 256), BF),
        ((2, SEQ, 256), F32),
        ((4, 2, 128, 768), BF),
        ((2, 2, 64, D), BF),
        ((4, 2, 128, D), BF),
        ((2, 2, 256, D), BF),
        ((2, 128, 384), BF),
        ((2, 128, 768), BF),
        ((2, 2, 64, 512), BF),
        ((2, 2, 128, D), BF),
        ((2, 256, 512), BF),
        ((256, 512), BF),
        ((2, 2, 2, 128, 384), BF),
        ((2, 2, 128, 384), BF),
        ((2, 2, 64, 512), BF),
        ((2, 2, 2, 128, 512), BF),
        ((2, 256, 512), BF),
        ((2, 2, 256, 512), BF),
        ((8, D), F32),
        ((4, 8, D), F32),
        ((4, 16, 256), F32),
        ((4, 16, 256), F32),
        ((16, 256), F32),
        ((16, 256), F32),
    ]
    return pl.pallas_call(
        layer_kernel,
        out_shape=[o[0] for o in outs],
        in_specs=[any_spec] * 7 + [vmem] * len(vecs),
        out_specs=[o[1] for o in outs],
        scratch_shapes=[pltpu.VMEM(shape, dtype) for shape, dtype in scratch]
        + [
            pltpu.SemaphoreType.DMA((S_SEMS,)),
            pltpu.SemaphoreType.DMA((R_SEMS,)),
            pltpu.SemaphoreType.DMA((L_SEMS,)),
        ],
        compiler_params=pltpu.CompilerParams(
            collective_id=0, has_side_effects=True, vmem_limit_bytes=62 * 1024 * 1024
        ),
        name="layer",
    )(seg, x, og, wq, wo, wu, wd, *vecs)


def finish_kernel(lo, tg, fq, fo, fu, fd, vec, lo_out, tg_out, q_out, o_out, u_out, d_out, *vectors):
    lo_out[...] = lo[...]
    tg_out[...] = tg[...]
    for yp in (0, 1):
        for n in (0, 1, 2):
            at = yp * 384 + n * 128
            q_out[n, :, yp * 128 : yp * 128 + 128] = fq[:, at : at + 128].astype(F32)
    o_out[...] = fo[...].astype(F32)
    u_out[...] = fu[...].astype(F32)
    d_out[...] = fd[...].astype(F32)
    for n in range(6):
        vectors[n][...] = vec[n : n + 1, :]
    for n in range(4):
        vectors[6][:, n * 256 : n * 256 + 256] = vec[6 + n : 7 + n, :]
    vectors[7][...] = vec[10:12, :]


def finish(*arrays):
    steps = 4
    out = jax.ShapeDtypeStruct

    def rows_spec(shape):
        return pl.BlockSpec((shape[0] // steps, shape[1]), lambda i: (i, 0))

    def whole(shape):
        return pl.BlockSpec(shape, lambda i: (0, 0))

    shapes = [out(arrays[0].shape, BF)] + [out(a.shape, F32) for a in arrays[1:6]]
    vectors = [out((1, 256), F32)] * 6 + [out((1, D), F32), out((2, 256), F32)]
    shapes[2] = out((3, 256, 256), F32)
    out_specs = [rows_spec(a.shape) for a in shapes] + [whole(v.shape) for v in vectors]
    out_specs[2] = pl.BlockSpec((3, 256 // steps, 256), lambda i: (0, i, 0))
    return pl.pallas_call(
        finish_kernel,
        grid=(steps,),
        in_specs=[rows_spec(a.shape) for a in arrays[:6]] + [whole(arrays[6].shape)],
        out_specs=out_specs,
        out_shape=shapes + vectors,
        name="finish",
    )(*arrays)


def shards(
    pairs,
    tokens,
    segments,
    qkv_weight,
    qv_bias,
    out_weight,
    out_bias,
    norm1_gain,
    norm1_bias,
    up_weight,
    up_bias,
    down_weight,
    down_bias,
    norm2_gain,
    norm2_bias,
    out_grad,
):
    lo, tg, fin_q, fin_o, fin_u, fin_d, vec = run_layer(
        segments,
        tokens.reshape(2, SEQ, 256),
        out_grad.reshape(2, SEQ, 256),
        qkv_weight.transpose(1, 0, 2).reshape(3, 2, 128, 256),
        out_weight.reshape(2, 2, 64, 256),
        up_weight.reshape(2, 128, D),
        down_weight.reshape(2, 2, 256, 256),
        up_bias.reshape(1, D),
        qv_bias,
        out_bias.reshape(1, D),
        norm1_gain.reshape(1, D),
        norm1_bias.reshape(1, D),
        down_bias.reshape(1, D),
        norm2_gain.reshape(1, D),
        norm2_bias.reshape(1, D),
    )
    grads = (fin_q, fin_o, fin_u, fin_d, vec)
    if pairs is not None:
        grads = lax.psum(grads, "dp", axis_index_groups=pairs)
    fin_q, fin_o, fin_u, fin_d, vec = grads
    results = finish(
        lo.reshape(2 * SEQ, 256),
        tg.reshape(2 * SEQ, 256),
        fin_q.reshape(256, 768),
        fin_o.reshape(256, 256),
        fin_u.reshape(256, D),
        fin_d.reshape(D, 256),
        vec,
    )
    layer_out, tokens_grad, qkv_grad, out_grad_w, up_grad, down_grad = results[:6]
    n2_gain, n2_bias, n1_gain, n1_bias, down_b, out_b, up_b, qv_b = results[6:]
    return (
        layer_out,
        tokens_grad,
        qkv_grad.transpose(1, 0, 2),
        qv_b,
        out_grad_w,
        out_b.reshape(256),
        n1_gain.reshape(256),
        n1_bias.reshape(256),
        up_grad,
        up_b.reshape(D),
        down_grad,
        down_b.reshape(256),
        n2_gain.reshape(256),
        n2_bias.reshape(256),
    )


def solution(mesh):
    placed = (
        P(("dp", "col"), "row"),
        P(("dp", "row"), None),
        P("row", None, "col"),
        P(None, "col"),
        P("col", "row"),
        P(),
        P(),
        P(),
        P("row", "col"),
        P("col"),
        P("col", "row"),
        P(),
        P(),
        P(),
        P(("dp", "col"), "row"),
    )
    dp = mesh.shape["dp"]
    pairs = None
    if dp > 2:
        pairs = [list(range(0, dp, 2)), list(range(1, dp, 2))]
    return jax.shard_map(
        functools.partial(shards, pairs),
        mesh=mesh,
        in_specs=placed,
        out_specs=(
            P(("dp", "col"), "row"),
            P(("dp", "col"), "row"),
            P("row", None, "col"),
            P(None, "col"),
            P("col", "row"),
            P("row"),
            P("row"),
            P("row"),
            P("row", "col"),
            P("col"),
            P("col", "row"),
            P("row"),
            P("row"),
            P("row"),
        ),
        check_vma=False,
    )
```

```python
import functools

import jax
import jax.numpy as jnp
from jax import lax
from jax.experimental import pallas as pl
from jax.experimental.pallas import tpu as pltpu
from jax.sharding import PartitionSpec as P

D = 1024
HEAD = 64
SEQ = 512
EPS = 1e-05
MESH = pl.DeviceIdType.MESH
BF = jnp.bfloat16
F32 = jnp.float32
ROWS = 128


def dot(left, right, left_dim, right_dim):
    return lax.dot_general(
        left, right, (((left_dim,), (right_dim,)), ((), ())), preferred_element_type=F32
    )


def al(index, step):
    return pl.multiple_of(index * step, step)


def col_sum(values):
    return jnp.sum(values, 0, keepdims=True)


def layer_kernel(
    seg_in,
    x_in,
    og_in,
    wq_in,
    wo_in,
    wu_in,
    wd_in,
    up_bias_in,
    qv_bias_in,
    out_bias_in,
    gain1_in,
    offset1_in,
    down_bias_in,
    gain2_in,
    offset2_in,
    lo_out,
    tg_out,
    fin_q,
    fin_o,
    fin_u,
    fin_d,
    vec_out,
    seg,
    bias_own,
    biases,
    xf,
    wq,
    wo,
    wu,
    wd,
    stage_q,
    stage_o,
    stage_u,
    stage_d,
    proj,
    probs,
    ctx,
    mask,
    part,
    rsc,
    rsy,
    ysend,
    normed1,
    inv1,
    hf,
    act,
    gelup,
    og,
    og_stage,
    lo,
    gsec,
    gdf,
    gu,
    gaf,
    gctx,
    gproj,
    partf,
    rscf,
    rsyf,
    ysendf,
    tg,
    gq,
    go,
    gup,
    gd,
    xq,
    xo,
    xu,
    xd,
    xd1,
    zq,
    zo,
    zu,
    zd,
    zd1,
    vec_sum,
    vec_rows,
    vec_out_parts,
    vec_cols,
    vec_part,
    vec_pair,
    ss,
    rs,
    ls,
):
    d = lax.axis_index("dp")
    r = lax.axis_index("row")
    c = lax.axis_index("col")
    y = r // 2
    k = r % 2
    p = d % 2
    r1 = r + 1 - 2 * k
    r2 = (r + 2) % 4
    r3 = (r1 + 2) % 4
    kc = c // 2
    ic = c % 2
    is_agg = k == kc
    core_dev = (d, r1, c)
    y_dev = (d, r2, c)
    x_dev = (d + 1 - 2 * p, r, c)

    counts = {"s": 0, "r": 0, "l": 0}

    def new(kind, n=1):
        at = counts[kind]
        counts[kind] += n
        return at

    def remote(si, ri, src, dst, dev):
        return pltpu.make_async_remote_copy(
            src_ref=src,
            dst_ref=dst,
            send_sem=ss.at[si],
            recv_sem=rs.at[ri],
            device_id=dev,
            device_id_type=MESH,
        )

    late = []

    def later(copy, condition=None):
        late.append((condition, copy))

    barrier = pltpu.get_barrier_semaphore()
    for j in (1, 2, 3):
        pl.semaphore_signal(barrier, inc=1, device_id=(d, (r + j) % 4, c), device_id_type=MESH)
        pl.semaphore_signal(barrier, inc=1, device_id=(d, r, (c + j) % 4), device_id_type=MESH)
    pl.semaphore_signal(barrier, inc=1, device_id=x_dev, device_id_type=MESH)

    @pl.when(r != c)
    def _():
        pl.semaphore_signal(barrier, inc=1, device_id=(d, c, r), device_id_type=MESH)
        pl.semaphore_wait(barrier, 8)

    @pl.when(r == c)
    def _():
        pl.semaphore_wait(barrier, 7)

    def qkv_piece(yp, n):
        return wq_in.at[n, :, :, pl.ds(al(yp, 128), 128)]

    def out_piece(yp, n):
        return wo_in.at[yp]

    def up_piece(yp, n):
        return wu_in.at[:, :, pl.ds(al(yp, 512), 512)]

    def down_piece(yp, n):
        return wd_in.at[yp]

    def qkv_place(row, n):
        return wq.at[row, :, :, pl.ds(pl.multiple_of(ic * 384 + n * 128, 128), 128)]

    def out_place(row, n):
        return wo.at[ic, :, :, pl.ds(al(row, 256), 256)]

    def up_place(row, n):
        return wu.at[row, :, :, pl.ds(al(ic, 512), 512)]

    def down_place(row, n):
        return wd.at[ic, :, :, pl.ds(al(row, 256), 256)]

    def qkv_half(ref, half, ci):
        return ref.at[:, half, :, pl.ds(al(ci, 384), 384)]

    def out_half(ref, half, ci):
        return ref.at[ci, half]

    def up_half(ref, half, ci):
        return ref.at[:, half, :, pl.ds(al(ci, 512), 512)]

    def down_half(ref, half, ci):
        return ref.at[ci, half]

    def out_chunk(ref, half, ci, chip):
        return ref.at[ci, half, :, pl.ds(al(chip, 512), 512)]

    def up_chunk(ref, half, ci, chip):
        return ref.at[pl.ds(2 * chip, 2), half, :, pl.ds(al(ci, 512), 512)]

    down_chunk = out_chunk

    def qkv_row(ref, half, ci, row):
        return ref.at[row, half, :, pl.ds(al(ci, 384), 384)]

    def out_row(ref, half, ci, row):
        return ref.at[ci, half, :, pl.ds(al(row, 256), 256)]

    def up_row(ref, half, ci, row):
        return ref.at[row, half, :, pl.ds(al(ci, 512), 512)]

    down_row = out_row
    chip_rows = ((r, r1), (r2, r3))
    far_dev = (d, r, (c + 2) % 4)
    near_dev = (d, r, c + 1 - 2 * ic)

    class Weight:
        def __init__(self, buffer, piece, place, at_row, stages):
            self.piece, self.place, self.stages = piece, place, stages
            self.parts = range(len(stages))
            self.s1, self.r1, self.l1 = [], [], []
            self.relay_copies, self.staged = [], []
            for q, stage in enumerate(stages):
                self.s1.append(new("s", 2))
                self.r1.append(new("r", 4))
                self.l1.append(new("l"))
                self.relay_copies.append(
                    remote(new("s"), self.r1[q] + r2, stage, place(r2, q), core_dev)
                )
                self.staged.append(remote(self.s1[q], self.r1[q] + r2, stage, stage, y_dev))
            self.far_copy, self.near_copy, self.pair_far, self.pair_near = {}, {}, {}, {}
            for n, m in ((0, 0), (0, 1), (1, 0), (1, 1)):
                row = chip_rows[n][m]
                held = at_row(buffer, p, ic, row)
                wanted = at_row(buffer, p, 1 - ic, row)
                self.far_copy[n, m] = remote(new("s"), new("r"), held, held, far_dev)
                si, ri = new("s"), new("r")
                self.near_copy[n, m] = (
                    remote(si, ri, held, held, near_dev),
                    remote(si, ri, wanted, wanted, near_dev),
                )
                si, ri = new("s"), new("r")
                missing = at_row(buffer, 1 - p, ic, row)
                self.pair_far[n, m] = (
                    remote(si, ri, held, held, x_dev),
                    remote(si, ri, missing, missing, x_dev),
                )
                si, ri = new("s"), new("r")
                missing = at_row(buffer, 1 - p, 1 - ic, row)
                self.pair_near[n, m] = (
                    remote(si, ri, wanted, wanted, x_dev),
                    remote(si, ri, missing, missing, x_dev),
                )

        def spread_rows(self):
            self.own = []
            for q in self.parts:
                mine, to = self.piece(y, q), self.place(r, q)
                across = self.piece(1 - y, q)
                near = remote(self.s1[q] + 1, self.r1[q] + r, mine, to, core_dev)
                own = pltpu.make_async_copy(mine, to, ls.at[self.l1[q]])
                direct = remote(self.s1[q], self.r1[q] + r, across, to, y_dev)
                staged = remote(self.s1[q], self.r1[q] + r, across, self.stages[q], y_dev)

                @pl.when(jnp.logical_not(is_agg))
                def _():
                    near.start()
                    staged.start()

                @pl.when(is_agg)
                def _():
                    own.start()
                    direct.start()

                later(near, jnp.logical_not(is_agg))
                later(direct)
                self.own.append(own)

        def relay(self):
            @pl.when(jnp.logical_not(is_agg))
            def _():
                for q in self.parts:
                    self.staged[q].wait_recv()
                    self.relay_copies[q].start()

            for copy in self.relay_copies:
                later(copy, jnp.logical_not(is_agg))

        def lead(self, n):
            @pl.when(is_agg)
            def _():
                for m in (0, 1):
                    row = chip_rows[n][m]
                    for q in self.parts:
                        if (n, m) == (0, 0):
                            self.own[q].wait()
                        else:
                            place = self.place(row, q)
                            remote(
                                self.s1[q], self.r1[q] + row, place, place, core_dev
                            ).wait_recv()
                    self.far_copy[n, m].start()
                    self.near_copy[n, m][0].start()

            for m in (0, 1):
                later(self.far_copy[n, m], is_agg)
                later(self.near_copy[n, m][0], is_agg)

        def follow(self, n):
            other = jnp.logical_not(is_agg)

            @pl.when(other)
            def _():
                for m in (0, 1):
                    self.far_copy[n, m].wait_recv()
                    self.near_copy[n, m][0].start()
                    self.pair_far[n, m][0].start()

            for m in (0, 1):
                later(self.near_copy[n, m][0], other)
                later(self.pair_far[n, m][0], other)

        def pair(self, n):
            for m in (0, 1):
                self.near_copy[n, m][1].wait_recv()
                self.pair_near[n, m][0].start()
                later(self.pair_near[n, m][0])

        def ready(self):
            for key in ((0, 0), (0, 1), (1, 0), (1, 1)):

                @pl.when(jnp.logical_not(is_agg))
                def _():
                    self.pair_far[key][1].wait_recv()

                self.pair_near[key][1].wait_recv()

    w_qkv = Weight(wq, qkv_piece, qkv_place, qkv_row, [stage_q.at[q] for q in (0, 1, 2)])
    w_out = Weight(wo, out_piece, out_place, out_row, [stage_o])
    w_up = Weight(wu, up_piece, up_place, up_row, [stage_u])
    w_down = Weight(wd, down_piece, down_place, down_row, [stage_d])

    def rows_of(ref, s, row):
        return ref.at[s, pl.ds(al(row, ROWS), ROWS), :]

    def slab_of(ref, s, row):
        return ref.at[s, :, pl.ds(al(row, 256), 256)]

    class Gather:
        def __init__(self, full, at, s, source=None):
            self.full, self.at, self.s = full, at, s
            self.source = source
            self.si, self.ri = [new("s"), new("s"), new("s")], new("r", 3)

        def send(self):
            mine = self.source if self.source is not None else self.at(self.full, self.s, r)
            place = self.at(self.full, self.s, r)
            for n, dev in ((0, y_dev), (1, core_dev)):
                copy = remote(self.si[n], self.ri + n, mine, place, dev)
                copy.start()
                later(copy)

        def forward(self):
            place = self.at(self.full, self.s, r2)
            remote(self.si[0], self.ri, place, place, y_dev).wait_recv()
            copy = remote(self.si[2], self.ri + 2, place, place, core_dev)
            copy.start()
            later(copy)

        def wait(self):
            near = self.at(self.full, self.s, r1)
            remote(self.si[1], self.ri + 1, near, near, core_dev).wait_recv()
            far = self.at(self.full, self.s, r3)
            remote(self.si[2], self.ri + 2, far, far, core_dev).wait_recv()

    class Scatter:
        def __init__(self, source, at, core_recv, y_send, y_recv, s):
            self.source, self.at = source, at
            self.core_recv, self.y_send, self.y_recv, self.s = core_recv, y_send, y_recv, s
            si, ri = [new("s"), new("s"), new("s")], new("r", 3)
            self.far = remote(si[0], ri, at(source, s, r3), core_recv.at[s, 1], core_dev)
            self.near = remote(si[1], ri + 1, at(source, s, r1), core_recv.at[s, 0], core_dev)
            self.cross = remote(si[2], ri + 2, y_send.at[s], y_recv.at[s], y_dev)

        def to_core(self):
            self.far.start()
            self.near.start()

        def to_y(self):
            self.far.wait_recv()
            total = self.at(self.source, self.s, r2)[...].astype(F32)
            self.y_send[self.s] = (total + self.core_recv[self.s, 1].astype(F32)).astype(BF)
            self.cross.start()

        def result(self):
            self.near.wait_recv()
            total = self.at(self.source, self.s, r)[...].astype(F32)
            total = total + self.core_recv[self.s, 0].astype(F32)
            self.cross.wait_recv()
            return total + self.y_recv[self.s].astype(F32)

        def sent(self):
            self.far.wait_send()
            self.near.wait_send()
            self.cross.wait_send()

    w_qkv.spread_rows()
    x_gather = [Gather(xf, slab_of, s, x_in.at[s]) for s in (0, 1)]
    x_own = [
        pltpu.make_async_copy(x_in.at[s], slab_of(xf, s, r), ls.at[new("l")]) for s in (0, 1)
    ]
    seg_s, seg_r, seg_l = new("s"), new("r"), new("l")
    seg_copy = remote(seg_s, seg_r, seg_in, seg, (d, c, r))
    seg_own = pltpu.make_async_copy(seg_in, seg, ls.at[seg_l])

    @pl.when(r != c)
    def _():
        seg_copy.start()

    @pl.when(r == c)
    def _():
        seg_own.start()

    bias_s, bias_r = new("s", 3), new("r", 4)
    bias_own[...] = jnp.zeros_like(bias_own)
    bias_own[0:1, :] = up_bias_in[...]
    bias_own[1:2, 0:256] = qv_bias_in[0:1, :]
    bias_own[1:2, 256:512] = qv_bias_in[1:2, :]
    for j in (1, 2, 3):
        copy = remote(bias_s + j - 1, bias_r + c, bias_own, biases.at[c], (d, r, (c + j) % 4))
        copy.start()
        later(copy)
    biases[c] = bias_own[...]
    w_out.spread_rows()
    for s in (0, 1):
        x_gather[s].send()
        x_own[s].start()

    w_up.spread_rows()
    w_down.spread_rows()
    og_s, og_r, og_l = new("s", 4), new("r", 5), new("l")

    def og_place(row):
        return og.at[:, :, pl.ds(al(row, 256), 256)]

    def og_rows(row):
        return og_in.at[:, pl.ds(al(row, ROWS), ROWS), :]

    og_own = pltpu.make_async_copy(og_rows(r), og_place(r), ls.at[og_l])
    og_own.start()
    og_copies = [
        remote(og_s, og_r + r, og_rows(r1), og_place(r), core_dev),
        remote(og_s + 1, og_r + r, og_rows(r2), og_place(r), y_dev),
        remote(og_s + 2, og_r + 4, og_rows(r3), og_stage, y_dev),
    ]
    for copy in og_copies:
        copy.start()
        later(copy)
    og_relay = remote(og_s + 3, og_r + r2, og_stage, og_place(r2), core_dev)

    def relay_og():
        remote(og_s + 2, og_r + 4, og_stage, og_stage, y_dev).wait_recv()
        og_relay.start()
        later(og_relay)

    def wait_og():
        og_own.wait()
        for j in (1, 2, 3):
            place = og_place((r + j) % 4)
            remote(og_s, og_r + (r + j) % 4, place, place, core_dev).wait_recv()

    w_qkv.lead(0)
    w_qkv.relay()
    w_out.relay()
    w_qkv.follow(0)
    w_qkv.lead(1)
    w_out.lead(0)
    w_out.lead(1)
    w_up.lead(0)
    w_qkv.pair(0)
    w_qkv.follow(1)
    x_gather[0].forward()
    w_out.follow(0)
    w_qkv.pair(1)
    w_out.follow(1)
    x_gather[1].forward()
    w_out.pair(0)
    w_out.pair(1)
    w_up.relay()

    for j in (1, 2, 3):
        source = (c + j) % 4
        remote(bias_s, bias_r + source, biases.at[source], biases.at[source], core_dev).wait_recv()

    @pl.when(r != c)
    def _():
        seg_copy.wait_recv()

    @pl.when(r == c)
    def _():
        seg_own.wait()

    later(seg_copy, r != c)
    w_qkv.ready()

    vec_sum[...] = jnp.zeros_like(vec_sum)

    def project(s):
        rows = xf[s]

        def half(ci, carry):
            weight = wq[:, :, :, pl.ds(al(ci, 384), 384)].reshape(D, 384)
            q_bias = biases[2 * k + ci, 1:2, pl.ds(al(y, 128), 128)]
            v_bias = biases[2 * k + ci, 1:2, pl.ds(pl.multiple_of(256 + y * 128, 128), 128)]
            bias = jnp.concatenate([q_bias, jnp.zeros_like(q_bias), v_bias], 1)
            proj[s, :, pl.ds(al(ci, 384), 384)] = (dot(rows, weight, 1, 0) + bias).astype(BF)
            return carry

        lax.fori_loop(0, 2, half, 0)

    def columns(ci, n):
        return pl.ds(pl.multiple_of(ci * 384 + n * 128, 128), 128)

    def attend(s):
        labels = seg[s : s + 1, :].astype(F32)
        down = jnp.transpose(jnp.broadcast_to(labels, (128, SEQ)))[:, 0:1]
        mask[...] = jnp.where(down == labels, 0.0, -1e30)
        lane = lax.broadcasted_iota(jnp.int32, (SEQ, 128), 1)
        row = lax.broadcasted_iota(jnp.int32, (128, SEQ), 0)

        def pair(ci, carry):
            queries = proj[s, :, columns(ci, 0)]
            keys_in = proj[s, :, columns(ci, 1)]
            values_in = proj[s, :, columns(ci, 2)]
            parts = []
            for h in (0, 1):
                chosen = (lane < HEAD) if h == 0 else (lane >= HEAD)
                masked = jnp.where(chosen, queries, jnp.zeros_like(queries))
                scores = dot(keys_in, masked, 1, 1) * (float(HEAD) ** (-0.5)) + mask[...]
                weights = jnp.exp(scores - jnp.max(scores, 0, keepdims=True))
                totals = jnp.sum(weights, 0, keepdims=True)
                share = (weights * (1.0 / totals)).astype(BF)
                probs[s, ci * 2 + h] = share
                parts.append(dot(values_in, share, 0, 0))
            both = jnp.where(row < HEAD, parts[0], parts[1])
            ctx[s, :, pl.ds(al(ci, 128), 128)] = jnp.transpose(both).astype(BF)
            return carry

        lax.fori_loop(0, 2, pair, 0)

    def out_partial(s):
        part[s] = dot(ctx[s], wo[...].reshape(256, D), 1, 0).astype(BF)

    def norm_stats(summed):
        center = jnp.sum(summed, 1, keepdims=True) * (1.0 / D)
        spread = jnp.sum(summed * summed, 1, keepdims=True) * (1.0 / D) - center * center
        inverse = lax.rsqrt(spread + EPS)
        return (summed - center) * inverse, inverse

    def norm_pull(grad, normed, inverse, gain):
        scaled = grad * gain
        first = jnp.sum(scaled, 1, keepdims=True) * (1.0 / D)
        second = jnp.sum(scaled * normed, 1, keepdims=True) * (1.0 / D)
        return inverse * (scaled - first - normed * second)

    out_bias, gain1, offset1 = out_bias_in[...], gain1_in[...], offset1_in[...]
    down_bias, gain2, offset2 = down_bias_in[...], gain2_in[...], offset2_in[...]
    own_rows = pl.ds(al(r, ROWS), ROWS)

    def scatters():
        return [Scatter(part, rows_of, rsc, ysend, rsy, s) for s in (0, 1)]

    rs1 = scatters()
    ag1 = [Gather(hf, rows_of, s) for s in (0, 1)]

    def first_norm(s):
        first_sum = rs1[s].result() + out_bias + xf[s, own_rows, :].astype(F32)
        normed, inverse = norm_stats(first_sum)
        normed1[s] = normed
        inv1[s] = jnp.broadcast_to(inverse, (ROWS, 128))
        hf[s, own_rows, :] = (normed * gain1 + offset1).astype(BF)
        ag1[s].send()

    x_own[0].wait()
    x_gather[0].wait()
    project(0)
    w_up.lead(1)
    w_up.follow(0)
    attend(0)
    w_out.ready()
    out_partial(0)
    rs1[0].to_core()
    w_down.relay()
    w_down.lead(0)
    rs1[0].to_y()
    x_own[1].wait()
    x_gather[1].wait()
    project(1)
    w_down.lead(1)
    w_up.follow(1)
    attend(1)
    out_partial(1)
    rs1[1].to_core()
    rs1[1].to_y()
    w_up.pair(0)
    w_down.follow(0)
    first_norm(0)
    w_up.pair(1)
    w_down.follow(1)
    w_down.pair(0)
    first_norm(1)
    w_down.pair(1)
    ag1[0].forward()
    w_up.ready()
    ag1[0].wait()

    def up_bias_of(ci):
        return biases[2 * k + ci, 0:1, pl.ds(al(y, 512), 512)]

    def mlp_up(s):
        rows = hf[s]

        def tile(n, carry):
            cols = pl.ds(al(n, 256), 256)
            weight = wu[:, :, :, cols].reshape(D, 256)
            ci = n // 2
            bias = biases[2 * k + ci, 0:1, pl.ds(pl.multiple_of(y * 512 + (n % 2) * 256, 256), 256)]
            upward = dot(rows, weight, 1, 0) + bias
            share = 0.5 + 0.5 * lax.erf(upward * 0.7071067811865476)
            act[s, :, cols] = (upward * share).astype(BF)
            density = jnp.exp(-0.5 * upward * upward) * 0.3989422804014327
            gelup[s, :, cols] = (share + upward * density).astype(BF)
            return carry

        lax.fori_loop(0, 4, tile, 0)

    def mlp_down(s):
        rows = act[s]

        def tile(n, carry):
            cols = pl.ds(al(n, 256), 256)
            weight = wd[:, :, :, cols].reshape(D, 256)
            part[s, :, cols] = dot(rows, weight, 1, 0).astype(BF)
            return carry

        lax.fori_loop(0, 4, tile, 0)

    rs2 = scatters()
    ag2 = [Gather(gdf, rows_of, s) for s in (0, 1)]
    lo_s, lo_r, lo_l = new("s", 6), new("r", 8), new("l", 2)

    def second_norm(s):
        hidden = normed1[s] * gain1 + offset1
        second_sum = rs2[s].result() + down_bias + hidden
        normed, inverse = norm_stats(second_sum)
        lo[s] = (normed * gain2 + offset2).astype(BF)
        grad = og[s].astype(F32)
        vec_sum[0:1, :] += col_sum(grad * normed)
        vec_sum[1:2, :] += col_sum(grad)
        grad_second = norm_pull(grad, normed, inverse, gain2)
        gsec[s] = grad_second
        rounded = grad_second.astype(BF)
        vec_sum[4:5, :] += col_sum(rounded.astype(F32))
        gdf[s, own_rows, :] = rounded
        ag2[s].send()

    def lo_place(s, row):
        return lo_out.at[s, pl.ds(al(row, ROWS), ROWS), :]

    def lo_part(s, row):
        return lo.at[s, :, pl.ds(al(row, 256), 256)]

    lo_own = [
        pltpu.make_async_copy(lo_part(s, r), lo_place(s, r), ls.at[lo_l + s]) for s in (0, 1)
    ]

    def send_lo(s):
        lo_own[s].start()
        for j in (1, 2, 3):
            row = (r + j) % 4
            copy = remote(
                lo_s + 3 * s + j - 1, lo_r + 4 * s + r, lo_part(s, row), lo_place(s, r), (d, row, c)
            )
            copy.start()
            later(copy)

    mlp_up(0)
    ag1[1].forward()
    relay_og()
    ag1[1].wait()
    mlp_up(1)
    w_down.ready()
    rs1[0].sent()
    mlp_down(0)
    rs2[0].to_core()
    rs1[1].sent()
    rs2[0].to_y()
    mlp_down(1)
    rs2[1].to_core()
    rs2[1].to_y()
    wait_og()
    second_norm(0)
    second_norm(1)
    ag2[0].forward()
    ag2[0].wait()

    class Grad:
        def __init__(
            self, buffer, chunk, both, by_ci, pair_recv, col_recv, place, pair_first, by_row=False
        ):
            self.buffer, self.place, self.pair_first = buffer, place, pair_first
            pair_recvs, col_recvs = pair_recv, col_recv
            self.by_row = by_row
            self.rows = (r, r1, r2, r3)
            self.near_copy, self.far_copy, self.pair_copy = {}, {}, {}
            self.near_add, self.far_add, self.pair_add = {}, {}, {}
            self.own, self.rows_copies = None, {}
            self.chunk = chunk
            self.s3, self.r3, self.l3 = new("s", 7), new("r", 4), new("l")
            for n in range(len(pair_recv)):
                chip = self.rows[n] if by_row else (y if n == 0 else 1 - y)
                pair_recv, col_recv = pair_recvs[n], col_recvs[n]
                if pair_first[n]:
                    pair_src, pair_dst = both(buffer, 1 - p, chip), both(buffer, p, chip)
                    near_src, held = chunk(buffer, p, 1 - ic, chip), chunk(buffer, p, ic, chip)
                else:
                    pair_src, pair_dst = chunk(buffer, 1 - p, ic, chip), chunk(buffer, p, ic, chip)
                    near_src, held = by_ci(buffer, 1 - ic, chip), by_ci(buffer, ic, chip)
                self.pair_copy[n] = remote(new("s"), new("r"), pair_src, pair_recv, x_dev)
                self.near_copy[n] = remote(new("s"), new("r"), near_src, col_recv.at[0], near_dev)
                self.far_copy[n] = remote(new("s"), new("r"), held, col_recv.at[1], far_dev)
                self.pair_add[n] = (pair_dst, pair_recv)
                self.near_add[n] = (held, col_recv.at[0])
                self.far_add[n] = (held, col_recv.at[1])

        def add(self, refs):
            mine, other = refs
            mine[...] = (mine[...].astype(F32) + other[...].astype(F32)).astype(BF)

        def arrival(self, half, yp):
            return self.r3 + 2 * half + yp

        def rows_of_chunk(self, n):
            copies = []
            here, there = d, d + 1 - 2 * p
            if n == 0:
                self.own = pltpu.make_async_copy(self.piece(r), self.place(p, y), ls.at[self.l3])
            if self.by_row:
                targets = [(here, self.rows[n]), (there, self.rows[n])]
                at = 2 * n - 1
                if n == 0:
                    targets, at = targets[1:], 0
            elif n == 0:
                targets = [(here, r1), (there, r), (there, r1)]
                at = 0
            else:
                targets = [(here, r2), (there, r2), (here, r3), (there, r3)]
                at = 3
            for plane, row in targets:
                copies.append(
                    remote(
                        self.s3 + at,
                        self.arrival(p, y),
                        self.piece(row),
                        self.place(p, y),
                        (plane, row, c),
                    )
                )
                at += 1
            return copies

        def begin(self, n):
            first = self.pair_copy[n] if self.pair_first[n] else self.near_copy[n]
            first.start()
            later(first)

        def second(self, n):
            if self.pair_first[n]:
                self.pair_copy[n].wait_recv()
                self.add(self.pair_add[n])
                self.near_copy[n].start()
                later(self.near_copy[n])
            else:
                self.near_copy[n].wait_recv()
                self.add(self.near_add[n])

                @pl.when(jnp.logical_not(is_agg))
                def _():
                    self.far_copy[n].start()

                later(self.far_copy[n], jnp.logical_not(is_agg))

        def third(self, n):
            if self.pair_first[n]:
                self.near_copy[n].wait_recv()
                self.add(self.near_add[n])

                @pl.when(jnp.logical_not(is_agg))
                def _():
                    self.far_copy[n].start()

                later(self.far_copy[n], jnp.logical_not(is_agg))
            else:

                @pl.when(is_agg)
                def _():
                    self.far_copy[n].wait_recv()
                    self.add(self.far_add[n])
                    self.pair_copy[n].start()

                later(self.pair_copy[n], is_agg)

        def to_rows(self, n):
            copies = self.rows_of_chunk(n)

            @pl.when(is_agg)
            def _():
                if self.pair_first[n]:
                    self.far_copy[n].wait_recv()
                    self.add(self.far_add[n])
                else:
                    self.pair_copy[n].wait_recv()
                    self.add(self.pair_add[n])
                if n == 0:
                    self.own.start()
                for copy in copies:
                    copy.start()

            for copy in copies:
                later(copy, is_agg)

        def done(self):
            @pl.when(is_agg)
            def _():
                self.own.wait()

            @pl.when(jnp.logical_not(is_agg))
            def _():
                place = self.place(p, y)
                remote(self.s3, self.arrival(p, y), place, place, core_dev).wait_recv()

            for half, yp in ((p, 1 - y), (1 - p, y), (1 - p, 1 - y)):
                place = self.place(half, yp)
                remote(self.s3, self.arrival(half, yp), place, place, core_dev).wait_recv()

    def rows_both(ref, half, chip):
        return ref.at[pl.ds(2 * chip, 2), half]

    def cols_both(ref, half, chip):
        return ref.at[:, half, :, pl.ds(al(chip, 512), 512)]

    def cols_of_ci(ref, ci, chip):
        return ref.at[ci, :, :, pl.ds(al(chip, 512), 512)]

    def two(ref):
        return [ref.at[0], ref.at[1]]

    def qkv_row_both(ref, half, row):
        return ref.at[row, half]

    g_qkv = Grad(
        gq,
        qkv_row,
        qkv_row_both,
        None,
        [xq.at[n] for n in range(4)],
        [zq.at[n] for n in range(4)],
        lambda half, yp: fin_q.at[half, :, pl.ds(al(yp, 384), 384)],
        (True,) * 4,
        by_row=True,
    )
    g_qkv.piece = lambda row: gq.at[row, p, :, pl.ds(al(ic, 384), 384)]
    g_out = Grad(
        go, out_chunk, cols_both, None, two(xo), two(zo), lambda half, yp: fin_o.at[yp, half], (True, True)
    )
    g_out.piece = lambda row: go.at[ic, p, :, pl.ds(al(row, 256), 256)]
    g_up = Grad(
        gup,
        up_chunk,
        rows_both,
        None,
        two(xu),
        two(zu),
        lambda half, yp: fin_u.at[half, :, pl.ds(al(yp, 512), 512)],
        (True, True),
    )
    g_up.piece = lambda row: gup.at[row, p, :, pl.ds(al(ic, 512), 512)]
    g_down = Grad(
        gd,
        down_chunk,
        cols_both,
        cols_of_ci,
        [xd, xd1],
        [zd, zd1],
        lambda half, yp: fin_d.at[yp, half],
        (True, False),
    )
    g_down.piece = lambda row: gd.at[ic, p, :, pl.ds(al(row, 256), 256)]

    def tokens_by(ref, cols):
        return ref[:, :, cols].reshape(2 * SEQ, cols.size)

    def down_grad(m):
        cols = pl.ds(al(y if m == 0 else 1 - y, 512), 512)

        def tile(n, carry):
            left = tokens_by(act, pl.ds(al(n, 256), 256))
            right = gdf[:, :, cols].reshape(2 * SEQ, 512)
            gd[n // 2, n % 2, :, cols] = dot(left, right, 0, 0).astype(BF)
            return carry

        lax.fori_loop(0, 4, tile, 0)

    def up_grad():
        def tile(n, carry):
            left = tokens_by(hf, pl.ds(al(n, 256), 256))
            gup[n] = (
                dot(left, gu[...].reshape(2 * SEQ, D), 0, 0).astype(BF).reshape(2, 128, D)
            )
            return carry

        lax.fori_loop(0, 4, tile, 0)

    def out_grad():
        left = ctx[...].reshape(2 * SEQ, 256)
        go[...] = dot(left, gaf[...].reshape(2 * SEQ, D), 0, 0).astype(BF).reshape(2, 2, 64, D)

    def qkv_grad():
        def tile(n, carry):
            left = tokens_by(xf, pl.ds(al(n, 256), 256))
            gq[n] = (
                dot(left, gproj[...].reshape(2 * SEQ, 768), 0, 0).astype(BF).reshape(2, 128, 768)
            )
            return carry

        lax.fori_loop(0, 4, tile, 0)

    def pull_act(s):
        rows = gdf[s]

        def tile(n, carry):
            cols = pl.ds(al(n, 256), 256)
            grad = dot(rows, wd[n // 2, n % 2], 1, 1) * gelup[s, :, cols].astype(F32)
            rounded = grad.astype(BF)
            gu[s, :, cols] = rounded
            vec_sum[6:7, cols] += col_sum(rounded.astype(F32))
            return carry

        lax.fori_loop(0, 4, tile, 0)

    def pull_hidden(s):
        rows = gu[s]

        def tile(n, carry):
            weight = wu[n].reshape(256, D)
            part[s, :, pl.ds(al(n, 256), 256)] = dot(rows, weight, 1, 1).astype(BF)
            return carry

        lax.fori_loop(0, 4, tile, 0)

    rs3 = scatters()
    ag3 = [Gather(gaf, rows_of, s) for s in (0, 1)]

    def first_norm_pull(s):
        grad = gsec[s] + rs3[s].result()
        normed = normed1[s]
        vec_sum[2:3, :] += col_sum(grad * normed)
        vec_sum[3:4, :] += col_sum(grad)
        rounded = norm_pull(grad, normed, inv1[s][:, 0:1], gain1).astype(BF)
        vec_sum[5:6, :] += col_sum(rounded.astype(F32))
        gaf[s, own_rows, :] = rounded
        ag3[s].send()

    pull_act(0)
    rs2[0].sent()
    pull_hidden(0)
    rs3[0].to_core()
    ag2[1].forward()
    rs3[0].to_y()
    ag2[1].wait()
    down_grad(0)
    g_down.begin(0)
    down_grad(1)
    g_down.begin(1)
    pull_act(1)
    rs2[1].sent()
    pull_hidden(1)
    rs3[1].to_core()
    rs3[1].to_y()
    first_norm_pull(0)
    up_grad()
    g_up.begin(1)
    g_up.begin(0)
    g_down.second(1)
    g_down.second(0)
    first_norm_pull(1)
    ag3[0].forward()
    ag3[0].wait()

    def pull_attend(s):
        gctx[...] = dot(gaf[s], wo[...].reshape(256, D), 1, 1).astype(BF)
        lane = lax.broadcasted_iota(jnp.int32, (SEQ, 128), 1)
        row = lax.broadcasted_iota(jnp.int32, (128, SEQ), 0)
        scale_factor = float(HEAD) ** (-0.5)

        def pair(ci, carry):
            queries = proj[s, :, columns(ci, 0)]
            keys_in = proj[s, :, columns(ci, 1)]
            values_in = proj[s, :, columns(ci, 2)]
            grad = gctx[:, pl.ds(al(ci, 128), 128)]
            grads_q, grads_k, grads_v = [], [], []
            for h in (0, 1):
                chosen = (lane < HEAD) if h == 0 else (lane >= HEAD)
                masked = jnp.where(chosen, grad, jnp.zeros_like(grad))
                share = probs[s, ci * 2 + h]
                wide = share.astype(F32)
                weighted = wide * dot(values_in, masked, 1, 1)
                total = jnp.sum(weighted, 0, keepdims=True)
                grad_scores = (weighted - wide * total).astype(BF)
                grads_v.append(dot(share, grad, 1, 0))
                grads_k.append(dot(grad_scores, queries, 1, 0))
                grads_q.append(dot(keys_in, grad_scores, 0, 0))
            both_q = jnp.transpose(jnp.where(row < HEAD, grads_q[0], grads_q[1]) * scale_factor)
            both_q = both_q.astype(BF)
            both_v = jnp.where(lane < HEAD, grads_v[0], grads_v[1]).astype(BF)
            both_k = jnp.where(lane < HEAD, grads_k[0], grads_k[1]) * scale_factor
            gproj[s, :, columns(ci, 0)] = both_q
            gproj[s, :, columns(ci, 1)] = both_k.astype(BF)
            gproj[s, :, columns(ci, 2)] = both_v
            at = pl.ds(al(ci, 128), 128)
            vec_sum[7:8, at] += col_sum(both_q.astype(F32))
            at = pl.ds(pl.multiple_of(256 + ci * 128, 128), 128)
            vec_sum[7:8, at] += col_sum(both_v.astype(F32))
            return carry

        lax.fori_loop(0, 2, pair, 0)

    def pull_tokens(s):
        rows = gproj[s]

        def tile(n, carry):
            partf[s, n] = dot(rows, wq[n].reshape(256, 768), 1, 1).astype(BF)
            return carry

        lax.fori_loop(0, 4, tile, 0)

    rs4 = [Scatter(partf, lambda ref, s, row: ref.at[s, row], rscf, ysendf, rsyf, s) for s in (0, 1)]
    tg_l = new("l", 2)
    tg_copy = [pltpu.make_async_copy(tg.at[s], tg_out.at[s], ls.at[tg_l + s]) for s in (0, 1)]

    def tokens_done(s):
        tg[s] = rs4[s].result() + slab_of(gaf, s, r)[...].astype(F32)
        tg_copy[s].start()

    class Sums:
        def __init__(self):
            self.si, self.ri = new("s", 7), new("r", 9)
            self.pair = remote(self.si + 6, self.ri + 8, vec_part, vec_pair, x_dev)

        def to_rows(self):
            vec_rows[r] = vec_sum[...]
            for j in (1, 2, 3):
                copy = remote(
                    self.si + j - 1, self.ri + r, vec_sum, vec_rows.at[r], (d, (r + j) % 4, c)
                )
                copy.start()
                later(copy)

        def to_cols(self):
            for j in (1, 2, 3):
                place = vec_rows.at[(r + j) % 4]
                remote(self.si, self.ri + (r + j) % 4, place, place, core_dev).wait_recv()
            mine = pl.ds(al(r, 256), 256)
            features = vec_rows[0, 0:6, mine] + vec_rows[1, 0:6, mine]
            features = features + vec_rows[2, 0:6, mine] + vec_rows[3, 0:6, mine]
            for j in (0, 1, 2, 3):
                to = (c + j) % 4
                slot = vec_out_parts.at[j]
                slot[0:6, :] = features
                for yp in (0, 1):
                    row = 2 * yp + to // 2
                    ci = to % 2
                    for n in (0, 1):
                        at = pl.ds(pl.multiple_of(ci * 512 + n * 256, 256), 256)
                        slot[6 + 2 * yp + n : 7 + 2 * yp + n, :] = vec_rows[row, 6:7, at]
                        at = pl.ds(pl.multiple_of(n * 256 + ci * 128, 128), 128)
                        slot[10 + n : 11 + n, yp * 128 : yp * 128 + 128] = vec_rows[row, 7:8, at]
                slot[12:16, :] = jnp.zeros((4, 256), F32)
                if j > 0:
                    copy = remote(
                        self.si + 2 + j,
                        self.ri + 4 + c,
                        slot,
                        vec_cols.at[c],
                        (d, r, to),
                    )
                    copy.start()
                    later(copy)

        def to_pair(self):
            total = vec_out_parts[0]
            for j in (1, 2, 3):
                source = (c + j) % 4
                place = vec_cols.at[source]
                remote(self.si, self.ri + 4 + source, place, place, core_dev).wait_recv()
                total = total + vec_cols[source]
            vec_part[...] = total
            self.pair.start()
            later(self.pair)

        def done(self):
            self.pair.wait_recv()
            vec_out[...] = vec_part[...] + vec_pair[...]

    pull_attend(0)
    ag3[1].forward()
    g_up.second(1)
    pull_tokens(0)
    rs4[0].to_core()
    g_down.third(1)
    rs4[0].to_y()
    g_down.third(0)
    ag3[1].wait()
    pull_attend(1)
    sums = Sums()
    sums.to_rows()
    qkv_grad()
    g_qkv.begin(3)
    g_qkv.begin(2)
    g_qkv.begin(1)
    g_up.second(0)
    out_grad()
    g_out.begin(1)
    g_out.begin(0)
    g_qkv.begin(0)
    g_up.third(1)
    pull_tokens(1)
    rs4[1].to_core()
    g_down.to_rows(0)
    rs4[1].to_y()
    send_lo(0)
    send_lo(1)
    g_down.to_rows(1)
    tokens_done(0)
    g_qkv.second(3)
    sums.to_cols()
    g_up.to_rows(1)
    g_qkv.second(2)
    g_up.third(0)
    tokens_done(1)
    g_qkv.third(3)
    g_qkv.second(1)
    g_qkv.third(2)
    g_qkv.to_rows(3)
    g_up.to_rows(0)
    g_out.second(1)
    sums.to_pair()
    g_qkv.third(1)
    g_qkv.to_rows(2)
    g_out.second(0)
    g_qkv.second(0)
    g_out.third(1)
    g_qkv.to_rows(1)
    g_out.third(0)
    g_qkv.third(0)
    g_out.to_rows(1)
    g_out.to_rows(0)
    g_qkv.to_rows(0)
    sums.done()
    g_down.done()
    g_up.done()
    g_out.done()
    g_qkv.done()

    for s in (0, 1):
        rs3[s].sent()
        rs4[s].sent()
        tg_copy[s].wait()
        lo_own[s].wait()
        for j in (1, 2, 3):
            source = (r + j) % 4
            place = lo_place(s, source)
            remote(lo_s, lo_r + 4 * s + source, place, place, core_dev).wait_recv()
    for condition, copy in late:
        if condition is None:
            copy.wait_send()
        else:
            pl.when(condition)(copy.wait_send)


S_SEMS = 320
R_SEMS = 320
L_SEMS = 32


def run_layer(seg, x, og, wq, wo, wu, wd, *vecs):
    any_spec = pl.BlockSpec(memory_space=pl.ANY)
    vmem = pl.BlockSpec(memory_space=pltpu.VMEM)
    out = jax.ShapeDtypeStruct
    outs = [
        (out((2, SEQ, 256), BF), any_spec),
        (out((2, SEQ, 256), F32), any_spec),
        (out((2, 128, 768), BF), any_spec),
        (out((2, 2, 64, 256), BF), any_spec),
        (out((2, 128, D), BF), any_spec),
        (out((2, 2, 256, 256), BF), any_spec),
        (out((16, 256), F32), vmem),
    ]
    full = ((2, SEQ, D), BF)
    scratch = [
        ((2, SEQ), jnp.int32),
        ((8, D), F32),
        ((4, 8, D), F32),
        full,
        ((4, 2, 128, 768), BF),
        ((2, 2, 64, D), BF),
        ((4, 2, 128, D), BF),
        ((2, 2, 256, D), BF),
        ((3, 2, 128, 128), BF),
        ((2, 64, 256), BF),
        ((2, 128, 512), BF),
        ((2, 256, 256), BF),
        ((2, SEQ, 768), BF),
        ((2, 4, SEQ, SEQ), BF),
        ((2, SEQ, 256), BF),
        ((SEQ, SEQ), F32),
        full,
        ((2, 2, ROWS, D), BF),
        ((2, ROWS, D), BF),
        ((2, ROWS, D), BF),
        ((2, ROWS, D), F32),
        ((2, ROWS, 128), F32),
        full,
        full,
        full,
        ((2, ROWS, D), BF),
        ((2, ROWS, 256), BF),
        ((2, ROWS, D), BF),
        ((2, ROWS, D), F32),
        full,
        full,
        full,
        ((SEQ, 256), BF),
        ((2, SEQ, 768), BF),
        ((2, 4, SEQ, 256), BF),
        ((2, 2, SEQ, 256), BF),
        ((2, SEQ, 256), BF),
        ((2, SEQ, 256), BF),
        ((2, SEQ, 256), F32),
        ((4, 2, 128, 768), BF),
        ((2, 2, 64, D), BF),
        ((4, 2, 128, D), BF),
        ((2, 2, 256, D), BF),
        ((4, 128, 768), BF),
        ((2, 2, 64, 512), BF),
        ((2, 2, 128, D), BF),
        ((2, 256, 512), BF),
        ((256, 512), BF),
        ((4, 2, 128, 384), BF),
        ((2, 2, 64, 512), BF),
        ((2, 2, 2, 128, 512), BF),
        ((2, 256, 512), BF),
        ((2, 2, 256, 512), BF),
        ((8, D), F32),
        ((4, 8, D), F32),
        ((4, 16, 256), F32),
        ((4, 16, 256), F32),
        ((16, 256), F32),
        ((16, 256), F32),
    ]
    return pl.pallas_call(
        layer_kernel,
        out_shape=[o[0] for o in outs],
        in_specs=[any_spec] * 7 + [vmem] * len(vecs),
        out_specs=[o[1] for o in outs],
        scratch_shapes=[pltpu.VMEM(shape, dtype) for shape, dtype in scratch]
        + [
            pltpu.SemaphoreType.DMA((S_SEMS,)),
            pltpu.SemaphoreType.DMA((R_SEMS,)),
            pltpu.SemaphoreType.DMA((L_SEMS,)),
        ],
        compiler_params=pltpu.CompilerParams(
            collective_id=0, has_side_effects=True, vmem_limit_bytes=62 * 1024 * 1024
        ),
        name="layer",
    )(seg, x, og, wq, wo, wu, wd, *vecs)


def finish_kernel(lo, tg, fq, fo, fu, fd, vec, lo_out, tg_out, q_out, o_out, u_out, d_out, *vectors):
    lo_out[...] = lo[...]
    tg_out[...] = tg[...]
    for yp in (0, 1):
        for n in (0, 1, 2):
            at = yp * 384 + n * 128
            q_out[n, :, yp * 128 : yp * 128 + 128] = fq[:, at : at + 128].astype(F32)
    o_out[...] = fo[...].astype(F32)
    u_out[...] = fu[...].astype(F32)
    d_out[...] = fd[...].astype(F32)
    for n in range(6):
        vectors[n][...] = vec[n : n + 1, :]
    for n in range(4):
        vectors[6][:, n * 256 : n * 256 + 256] = vec[6 + n : 7 + n, :]
    vectors[7][...] = vec[10:12, :]


def finish(*arrays):
    steps = 2
    out = jax.ShapeDtypeStruct

    def rows_spec(shape):
        return pl.BlockSpec((shape[0] // steps, shape[1]), lambda i: (i, 0))

    def whole(shape):
        return pl.BlockSpec(shape, lambda i: (0, 0))

    shapes = [out(arrays[0].shape, BF)] + [out(a.shape, F32) for a in arrays[1:6]]
    vectors = [out((1, 256), F32)] * 6 + [out((1, D), F32), out((2, 256), F32)]
    shapes[2] = out((3, 256, 256), F32)
    out_specs = [rows_spec(a.shape) for a in shapes] + [whole(v.shape) for v in vectors]
    out_specs[2] = pl.BlockSpec((3, 256 // steps, 256), lambda i: (0, i, 0))
    return pl.pallas_call(
        finish_kernel,
        grid=(steps,),
        in_specs=[rows_spec(a.shape) for a in arrays[:6]] + [whole(arrays[6].shape)],
        out_specs=out_specs,
        out_shape=shapes + vectors,
        name="finish",
    )(*arrays)


def shards(
    pairs,
    tokens,
    segments,
    qkv_weight,
    qv_bias,
    out_weight,
    out_bias,
    norm1_gain,
    norm1_bias,
    up_weight,
    up_bias,
    down_weight,
    down_bias,
    norm2_gain,
    norm2_bias,
    out_grad,
):
    lo, tg, fin_q, fin_o, fin_u, fin_d, vec = run_layer(
        segments,
        tokens.reshape(2, SEQ, 256),
        out_grad.reshape(2, SEQ, 256),
        qkv_weight.transpose(1, 0, 2).reshape(3, 2, 128, 256),
        out_weight.reshape(2, 2, 64, 256),
        up_weight.reshape(2, 128, D),
        down_weight.reshape(2, 2, 256, 256),
        up_bias.reshape(1, D),
        qv_bias,
        out_bias.reshape(1, D),
        norm1_gain.reshape(1, D),
        norm1_bias.reshape(1, D),
        down_bias.reshape(1, D),
        norm2_gain.reshape(1, D),
        norm2_bias.reshape(1, D),
    )
    grads = (fin_q, fin_o, fin_u, fin_d, vec)
    if pairs is not None:
        grads = lax.psum(grads, "dp", axis_index_groups=pairs)
    fin_q, fin_o, fin_u, fin_d, vec = grads
    results = finish(
        lo.reshape(2 * SEQ, 256),
        tg.reshape(2 * SEQ, 256),
        fin_q.reshape(256, 768),
        fin_o.reshape(256, 256),
        fin_u.reshape(256, D),
        fin_d.reshape(D, 256),
        vec,
    )
    layer_out, tokens_grad, qkv_grad, out_grad_w, up_grad, down_grad = results[:6]
    n2_gain, n2_bias, n1_gain, n1_bias, down_b, out_b, up_b, qv_b = results[6:]
    return (
        layer_out,
        tokens_grad,
        qkv_grad.transpose(1, 0, 2),
        qv_b,
        out_grad_w,
        out_b.reshape(256),
        n1_gain.reshape(256),
        n1_bias.reshape(256),
        up_grad,
        up_b.reshape(D),
        down_grad,
        down_b.reshape(256),
        n2_gain.reshape(256),
        n2_bias.reshape(256),
    )


def solution(mesh):
    placed = (
        P(("dp", "col"), "row"),
        P(("dp", "row"), None),
        P("row", None, "col"),
        P(None, "col"),
        P("col", "row"),
        P(),
        P(),
        P(),
        P("row", "col"),
        P("col"),
        P("col", "row"),
        P(),
        P(),
        P(),
        P(("dp", "col"), "row"),
    )
    dp = mesh.shape["dp"]
    pairs = None
    if dp > 2:
        pairs = [list(range(0, dp, 2)), list(range(1, dp, 2))]
    return jax.shard_map(
        functools.partial(shards, pairs),
        mesh=mesh,
        in_specs=placed,
        out_specs=(
            P(("dp", "col"), "row"),
            P(("dp", "col"), "row"),
            P("row", None, "col"),
            P(None, "col"),
            P("col", "row"),
            P("row"),
            P("row"),
            P("row"),
            P("row", "col"),
            P("col"),
            P("col", "row"),
            P("row"),
            P("row"),
            P("row"),
        ),
        check_vma=False,
    )
```

```python
import functools

import jax
import jax.numpy as jnp
from jax import lax
from jax.experimental import pallas as pl
from jax.experimental.pallas import tpu as pltpu
from jax.sharding import PartitionSpec as P

D = 1024
HEAD = 64
SEQ = 512
EPS = 1e-05
MESH = pl.DeviceIdType.MESH
BF = jnp.bfloat16
F32 = jnp.float32
ROWS = 128


def dot(left, right, left_dim, right_dim):
    return lax.dot_general(
        left, right, (((left_dim,), (right_dim,)), ((), ())), preferred_element_type=F32
    )


def al(index, step):
    return pl.multiple_of(index * step, step)


def col_sum(values):
    return jnp.sum(values, 0, keepdims=True)


def layer_kernel(
    seg_in,
    x_in,
    og_in,
    wq_in,
    wo_in,
    wu_in,
    wd_in,
    up_bias_in,
    qv_bias_in,
    out_bias_in,
    gain1_in,
    offset1_in,
    down_bias_in,
    gain2_in,
    offset2_in,
    lo_out,
    tg_out,
    fin_q,
    fin_o,
    fin_u,
    fin_d,
    vec_out,
    seg,
    bias_own,
    biases,
    xf,
    wq,
    wo,
    wu,
    wd,
    stage_q,
    stage_o,
    stage_u,
    stage_d,
    proj,
    probs,
    ctx,
    mask,
    part,
    rsc,
    rsy,
    ysend,
    normed1,
    inv1,
    hf,
    act,
    gelup,
    og,
    og_stage,
    lo,
    gsec,
    gdf,
    gu,
    gaf,
    gctx,
    gproj,
    partf,
    rscf,
    rsyf,
    ysendf,
    tg,
    gq,
    go,
    gup,
    gd,
    xq,
    xo,
    xu,
    xd,
    xd1,
    zq,
    zo,
    zu,
    zd,
    zd1,
    vec_sum,
    vec_rows,
    vec_out_parts,
    vec_cols,
    vec_part,
    vec_pair,
    ss,
    rs,
    ls,
):
    d = lax.axis_index("dp")
    r = lax.axis_index("row")
    c = lax.axis_index("col")
    y = r // 2
    k = r % 2
    p = d % 2
    r1 = r + 1 - 2 * k
    r2 = (r + 2) % 4
    r3 = (r1 + 2) % 4
    kc = c // 2
    ic = c % 2
    is_agg = k == kc
    core_dev = (d, r1, c)
    y_dev = (d, r2, c)
    x_dev = (d + 1 - 2 * p, r, c)

    counts = {"s": 0, "r": 0, "l": 0}

    def new(kind, n=1):
        at = counts[kind]
        counts[kind] += n
        return at

    def remote(si, ri, src, dst, dev):
        return pltpu.make_async_remote_copy(
            src_ref=src,
            dst_ref=dst,
            send_sem=ss.at[si],
            recv_sem=rs.at[ri],
            device_id=dev,
            device_id_type=MESH,
        )

    late = []

    def later(copy, condition=None):
        late.append((condition, copy))

    barrier = pltpu.get_barrier_semaphore()
    for j in (1, 2, 3):
        pl.semaphore_signal(barrier, inc=1, device_id=(d, (r + j) % 4, c), device_id_type=MESH)
        pl.semaphore_signal(barrier, inc=1, device_id=(d, r, (c + j) % 4), device_id_type=MESH)
    pl.semaphore_signal(barrier, inc=1, device_id=x_dev, device_id_type=MESH)

    @pl.when(r != c)
    def _():
        pl.semaphore_signal(barrier, inc=1, device_id=(d, c, r), device_id_type=MESH)
        pl.semaphore_wait(barrier, 8)

    @pl.when(r == c)
    def _():
        pl.semaphore_wait(barrier, 7)

    def qkv_piece(yp, n):
        return wq_in.at[n, :, :, pl.ds(al(yp, 128), 128)]

    def out_piece(yp, n):
        return wo_in.at[yp]

    def up_piece(yp, n):
        return wu_in.at[:, :, pl.ds(al(yp, 512), 512)]

    def down_piece(yp, n):
        return wd_in.at[yp]

    def qkv_place(row, n):
        return wq.at[row, :, :, pl.ds(pl.multiple_of(ic * 384 + n * 128, 128), 128)]

    def out_place(row, n):
        return wo.at[ic, :, :, pl.ds(al(row, 256), 256)]

    def up_place(row, n):
        return wu.at[row, :, :, pl.ds(al(ic, 512), 512)]

    def down_place(row, n):
        return wd.at[ic, :, :, pl.ds(al(row, 256), 256)]

    def qkv_half(ref, half, ci):
        return ref.at[:, half, :, pl.ds(al(ci, 384), 384)]

    def out_half(ref, half, ci):
        return ref.at[ci, half]

    def up_half(ref, half, ci):
        return ref.at[:, half, :, pl.ds(al(ci, 512), 512)]

    def down_half(ref, half, ci):
        return ref.at[ci, half]

    def out_chunk(ref, half, ci, chip):
        return ref.at[ci, half, :, pl.ds(al(chip, 512), 512)]

    def up_chunk(ref, half, ci, chip):
        return ref.at[pl.ds(2 * chip, 2), half, :, pl.ds(al(ci, 512), 512)]

    down_chunk = out_chunk

    def qkv_row(ref, half, ci, row):
        return ref.at[row, half, :, pl.ds(al(ci, 384), 384)]

    def out_row(ref, half, ci, row):
        return ref.at[ci, half, :, pl.ds(al(row, 256), 256)]

    def up_row(ref, half, ci, row):
        return ref.at[row, half, :, pl.ds(al(ci, 512), 512)]

    down_row = out_row
    chip_rows = ((r, r1), (r2, r3))
    far_dev = (d, r, (c + 2) % 4)
    near_dev = (d, r, c + 1 - 2 * ic)

    class Weight:
        def __init__(self, buffer, piece, place, at_row, stages):
            self.piece, self.place, self.stages = piece, place, stages
            self.parts = range(len(stages))
            self.s1, self.r1, self.l1 = [], [], []
            self.relay_copies, self.staged = [], []
            for q, stage in enumerate(stages):
                self.s1.append(new("s", 2))
                self.r1.append(new("r", 4))
                self.l1.append(new("l"))
                self.relay_copies.append(
                    remote(new("s"), self.r1[q] + r2, stage, place(r2, q), core_dev)
                )
                self.staged.append(remote(self.s1[q], self.r1[q] + r2, stage, stage, y_dev))
            self.far_copy, self.near_copy, self.pair_far, self.pair_near = {}, {}, {}, {}
            for n, m in ((0, 0), (0, 1), (1, 0), (1, 1)):
                row = chip_rows[n][m]
                held = at_row(buffer, p, ic, row)
                wanted = at_row(buffer, p, 1 - ic, row)
                self.far_copy[n, m] = remote(new("s"), new("r"), held, held, far_dev)
                si, ri = new("s"), new("r")
                self.near_copy[n, m] = (
                    remote(si, ri, held, held, near_dev),
                    remote(si, ri, wanted, wanted, near_dev),
                )
                si, ri = new("s"), new("r")
                missing = at_row(buffer, 1 - p, ic, row)
                self.pair_far[n, m] = (
                    remote(si, ri, held, held, x_dev),
                    remote(si, ri, missing, missing, x_dev),
                )
                si, ri = new("s"), new("r")
                missing = at_row(buffer, 1 - p, 1 - ic, row)
                self.pair_near[n, m] = (
                    remote(si, ri, wanted, wanted, x_dev),
                    remote(si, ri, missing, missing, x_dev),
                )

        def spread_rows(self):
            self.own = []
            for q in self.parts:
                mine, to = self.piece(y, q), self.place(r, q)
                across = self.piece(1 - y, q)
                near = remote(self.s1[q] + 1, self.r1[q] + r, mine, to, core_dev)
                own = pltpu.make_async_copy(mine, to, ls.at[self.l1[q]])
                direct = remote(self.s1[q], self.r1[q] + r, across, to, y_dev)
                staged = remote(self.s1[q], self.r1[q] + r, across, self.stages[q], y_dev)

                @pl.when(jnp.logical_not(is_agg))
                def _():
                    near.start()
                    staged.start()

                @pl.when(is_agg)
                def _():
                    own.start()
                    direct.start()

                later(near, jnp.logical_not(is_agg))
                later(direct)
                self.own.append(own)

        def relay(self):
            @pl.when(jnp.logical_not(is_agg))
            def _():
                for q in self.parts:
                    self.staged[q].wait_recv()
                    self.relay_copies[q].start()

            for copy in self.relay_copies:
                later(copy, jnp.logical_not(is_agg))

        def lead(self, n):
            @pl.when(is_agg)
            def _():
                for m in (0, 1):
                    row = chip_rows[n][m]
                    for q in self.parts:
                        if (n, m) == (0, 0):
                            self.own[q].wait()
                        else:
                            place = self.place(row, q)
                            remote(
                                self.s1[q], self.r1[q] + row, place, place, core_dev
                            ).wait_recv()
                    self.far_copy[n, m].start()
                    self.near_copy[n, m][0].start()

            for m in (0, 1):
                later(self.far_copy[n, m], is_agg)
                later(self.near_copy[n, m][0], is_agg)

        def follow(self, n):
            other = jnp.logical_not(is_agg)

            @pl.when(other)
            def _():
                for m in (0, 1):
                    self.far_copy[n, m].wait_recv()
                    self.near_copy[n, m][0].start()
                    self.pair_far[n, m][0].start()

            for m in (0, 1):
                later(self.near_copy[n, m][0], other)
                later(self.pair_far[n, m][0], other)

        def pair(self, n, spreading):
            mine = is_agg if spreading else jnp.logical_not(is_agg)

            @pl.when(mine)
            def _():
                for m in (0, 1):
                    self.near_copy[n, m][1].wait_recv()
                    self.pair_near[n, m][0].start()

            for m in (0, 1):
                later(self.pair_near[n, m][0], mine)

        def ready(self):
            for key in ((0, 0), (0, 1), (1, 0), (1, 1)):

                @pl.when(jnp.logical_not(is_agg))
                def _():
                    self.pair_far[key][1].wait_recv()

                self.pair_near[key][1].wait_recv()

    w_qkv = Weight(wq, qkv_piece, qkv_place, qkv_row, [stage_q.at[q] for q in (0, 1, 2)])
    w_out = Weight(wo, out_piece, out_place, out_row, [stage_o])
    w_up = Weight(wu, up_piece, up_place, up_row, [stage_u])
    w_down = Weight(wd, down_piece, down_place, down_row, [stage_d])

    def rows_of(ref, s, row):
        return ref.at[s, pl.ds(al(row, ROWS), ROWS), :]

    def slab_of(ref, s, row):
        return ref.at[s, :, pl.ds(al(row, 256), 256)]

    class Gather:
        def __init__(self, full, at, s, source=None):
            self.full, self.at, self.s = full, at, s
            self.source = source
            self.si, self.ri = [new("s"), new("s"), new("s")], new("r", 3)

        def send(self):
            mine = self.source if self.source is not None else self.at(self.full, self.s, r)
            place = self.at(self.full, self.s, r)
            for n, dev in ((0, y_dev), (1, core_dev)):
                copy = remote(self.si[n], self.ri + n, mine, place, dev)
                copy.start()
                later(copy)

        def forward(self):
            place = self.at(self.full, self.s, r2)
            remote(self.si[0], self.ri, place, place, y_dev).wait_recv()
            copy = remote(self.si[2], self.ri + 2, place, place, core_dev)
            copy.start()
            later(copy)

        def wait(self):
            near = self.at(self.full, self.s, r1)
            remote(self.si[1], self.ri + 1, near, near, core_dev).wait_recv()
            far = self.at(self.full, self.s, r3)
            remote(self.si[2], self.ri + 2, far, far, core_dev).wait_recv()

    class Scatter:
        def __init__(self, source, at, core_recv, y_send, y_recv, s):
            self.source, self.at = source, at
            self.core_recv, self.y_send, self.y_recv, self.s = core_recv, y_send, y_recv, s
            si, ri = [new("s"), new("s"), new("s")], new("r", 3)
            self.far = remote(si[0], ri, at(source, s, r3), core_recv.at[s, 1], core_dev)
            self.near = remote(si[1], ri + 1, at(source, s, r1), core_recv.at[s, 0], core_dev)
            self.cross = remote(si[2], ri + 2, y_send.at[s], y_recv.at[s], y_dev)

        def to_core(self):
            self.far.start()
            self.near.start()

        def to_y(self):
            self.far.wait_recv()
            total = self.at(self.source, self.s, r2)[...].astype(F32)
            self.y_send[self.s] = (total + self.core_recv[self.s, 1].astype(F32)).astype(BF)
            self.cross.start()

        def result(self):
            self.near.wait_recv()
            total = self.at(self.source, self.s, r)[...].astype(F32)
            total = total + self.core_recv[self.s, 0].astype(F32)
            self.cross.wait_recv()
            return total + self.y_recv[self.s].astype(F32)

        def sent(self):
            self.far.wait_send()
            self.near.wait_send()
            self.cross.wait_send()

    w_qkv.spread_rows()
    x_gather = [Gather(xf, slab_of, s, x_in.at[s]) for s in (0, 1)]
    x_own = [
        pltpu.make_async_copy(x_in.at[s], slab_of(xf, s, r), ls.at[new("l")]) for s in (0, 1)
    ]
    seg_s, seg_r, seg_l = new("s"), new("r"), new("l")
    seg_copy = remote(seg_s, seg_r, seg_in, seg, (d, c, r))
    seg_own = pltpu.make_async_copy(seg_in, seg, ls.at[seg_l])

    @pl.when(r != c)
    def _():
        seg_copy.start()

    @pl.when(r == c)
    def _():
        seg_own.start()

    bias_s, bias_r = new("s", 3), new("r", 4)
    bias_own[...] = jnp.zeros_like(bias_own)
    bias_own[0:1, :] = up_bias_in[...]
    bias_own[1:2, 0:256] = qv_bias_in[0:1, :]
    bias_own[1:2, 256:512] = qv_bias_in[1:2, :]
    for j in (1, 2, 3):
        copy = remote(bias_s + j - 1, bias_r + c, bias_own, biases.at[c], (d, r, (c + j) % 4))
        copy.start()
        later(copy)
    biases[c] = bias_own[...]
    w_out.spread_rows()
    for s in (0, 1):
        x_gather[s].send()
        x_own[s].start()

    w_up.spread_rows()
    w_down.spread_rows()
    og_s, og_r, og_l = new("s", 4), new("r", 5), new("l")

    def og_place(row):
        return og.at[:, :, pl.ds(al(row, 256), 256)]

    def og_rows(row):
        return og_in.at[:, pl.ds(al(row, ROWS), ROWS), :]

    og_own = pltpu.make_async_copy(og_rows(r), og_place(r), ls.at[og_l])
    og_own.start()
    og_copies = [
        remote(og_s, og_r + r, og_rows(r1), og_place(r), core_dev),
        remote(og_s + 1, og_r + r, og_rows(r2), og_place(r), y_dev),
        remote(og_s + 2, og_r + 4, og_rows(r3), og_stage, y_dev),
    ]
    for copy in og_copies:
        copy.start()
        later(copy)
    og_relay = remote(og_s + 3, og_r + r2, og_stage, og_place(r2), core_dev)

    def relay_og():
        remote(og_s + 2, og_r + 4, og_stage, og_stage, y_dev).wait_recv()
        og_relay.start()
        later(og_relay)

    def wait_og():
        og_own.wait()
        for j in (1, 2, 3):
            place = og_place((r + j) % 4)
            remote(og_s, og_r + (r + j) % 4, place, place, core_dev).wait_recv()

    w_qkv.lead(0)
    w_qkv.relay()
    w_out.relay()
    w_qkv.follow(0)
    w_qkv.lead(1)
    w_out.lead(0)
    w_out.lead(1)
    w_up.lead(0)
    w_qkv.pair(0, True)
    w_qkv.pair(0, False)
    w_qkv.follow(1)
    x_gather[0].forward()
    w_out.follow(0)
    w_qkv.pair(1, True)
    w_qkv.pair(1, False)
    w_out.follow(1)
    x_gather[1].forward()
    w_out.pair(0, True)
    w_out.pair(0, False)
    w_out.pair(1, True)
    w_out.pair(1, False)
    w_up.relay()

    for j in (1, 2, 3):
        source = (c + j) % 4
        remote(bias_s, bias_r + source, biases.at[source], biases.at[source], core_dev).wait_recv()

    @pl.when(r != c)
    def _():
        seg_copy.wait_recv()

    @pl.when(r == c)
    def _():
        seg_own.wait()

    later(seg_copy, r != c)
    w_qkv.ready()

    vec_sum[...] = jnp.zeros_like(vec_sum)

    def project(s):
        rows = xf[s]

        def half(ci, carry):
            weight = wq[:, :, :, pl.ds(al(ci, 384), 384)].reshape(D, 384)
            q_bias = biases[2 * k + ci, 1:2, pl.ds(al(y, 128), 128)]
            v_bias = biases[2 * k + ci, 1:2, pl.ds(pl.multiple_of(256 + y * 128, 128), 128)]
            bias = jnp.concatenate([q_bias, jnp.zeros_like(q_bias), v_bias], 1)
            proj[s, :, pl.ds(al(ci, 384), 384)] = (dot(rows, weight, 1, 0) + bias).astype(BF)
            return carry

        lax.fori_loop(0, 2, half, 0)

    def columns(ci, n):
        return pl.ds(pl.multiple_of(ci * 384 + n * 128, 128), 128)

    def attend(s):
        labels = seg[s : s + 1, :].astype(F32)
        down = jnp.transpose(jnp.broadcast_to(labels, (128, SEQ)))[:, 0:1]
        mask[...] = jnp.where(down == labels, 0.0, -1e30)
        lane = lax.broadcasted_iota(jnp.int32, (SEQ, 128), 1)
        row = lax.broadcasted_iota(jnp.int32, (128, SEQ), 0)

        def pair(ci, carry):
            queries = proj[s, :, columns(ci, 0)]
            keys_in = proj[s, :, columns(ci, 1)]
            values_in = proj[s, :, columns(ci, 2)]
            parts = []
            for h in (0, 1):
                chosen = (lane < HEAD) if h == 0 else (lane >= HEAD)
                masked = jnp.where(chosen, queries, jnp.zeros_like(queries))
                scores = dot(keys_in, masked, 1, 1) * (float(HEAD) ** (-0.5)) + mask[...]
                weights = jnp.exp(scores - jnp.max(scores, 0, keepdims=True))
                totals = jnp.sum(weights, 0, keepdims=True)
                share = (weights * (1.0 / totals)).astype(BF)
                probs[s, ci * 2 + h] = share
                parts.append(dot(values_in, share, 0, 0))
            both = jnp.where(row < HEAD, parts[0], parts[1])
            ctx[s, :, pl.ds(al(ci, 128), 128)] = jnp.transpose(both).astype(BF)
            return carry

        lax.fori_loop(0, 2, pair, 0)

    def out_partial(s):
        part[s] = dot(ctx[s], wo[...].reshape(256, D), 1, 0).astype(BF)

    def norm_stats(summed):
        center = jnp.sum(summed, 1, keepdims=True) * (1.0 / D)
        spread = jnp.sum(summed * summed, 1, keepdims=True) * (1.0 / D) - center * center
        inverse = lax.rsqrt(spread + EPS)
        return (summed - center) * inverse, inverse

    def norm_pull(grad, normed, inverse, gain):
        scaled = grad * gain
        first = jnp.sum(scaled, 1, keepdims=True) * (1.0 / D)
        second = jnp.sum(scaled * normed, 1, keepdims=True) * (1.0 / D)
        return inverse * (scaled - first - normed * second)

    out_bias, gain1, offset1 = out_bias_in[...], gain1_in[...], offset1_in[...]
    down_bias, gain2, offset2 = down_bias_in[...], gain2_in[...], offset2_in[...]
    own_rows = pl.ds(al(r, ROWS), ROWS)

    def scatters():
        return [Scatter(part, rows_of, rsc, ysend, rsy, s) for s in (0, 1)]

    rs1 = scatters()
    ag1 = [Gather(hf, rows_of, s) for s in (0, 1)]

    def first_norm(s):
        first_sum = rs1[s].result() + out_bias + xf[s, own_rows, :].astype(F32)
        normed, inverse = norm_stats(first_sum)
        normed1[s] = normed
        inv1[s] = jnp.broadcast_to(inverse, (ROWS, 128))
        hf[s, own_rows, :] = (normed * gain1 + offset1).astype(BF)
        ag1[s].send()

    x_own[0].wait()
    x_gather[0].wait()
    project(0)
    w_up.lead(1)
    w_up.follow(0)
    attend(0)
    w_up.pair(0, True)
    w_out.ready()
    out_partial(0)
    rs1[0].to_core()
    w_down.relay()
    w_down.lead(0)
    rs1[0].to_y()
    x_own[1].wait()
    x_gather[1].wait()
    project(1)
    w_down.lead(1)
    w_up.follow(1)
    attend(1)
    w_up.pair(1, True)
    out_partial(1)
    rs1[1].to_core()
    rs1[1].to_y()
    w_up.pair(0, False)
    w_down.pair(0, True)
    w_down.follow(0)
    first_norm(0)
    w_up.pair(1, False)
    w_down.follow(1)
    w_down.pair(0, False)
    first_norm(1)
    w_down.pair(1, True)
    w_down.pair(1, False)
    ag1[0].forward()
    w_up.ready()
    ag1[0].wait()

    def up_bias_of(ci):
        return biases[2 * k + ci, 0:1, pl.ds(al(y, 512), 512)]

    def mlp_up(s):
        rows = hf[s]

        def tile(n, carry):
            cols = pl.ds(al(n, 256), 256)
            weight = wu[:, :, :, cols].reshape(D, 256)
            ci = n // 2
            bias = biases[2 * k + ci, 0:1, pl.ds(pl.multiple_of(y * 512 + (n % 2) * 256, 256), 256)]
            upward = dot(rows, weight, 1, 0) + bias
            share = 0.5 + 0.5 * lax.erf(upward * 0.7071067811865476)
            act[s, :, cols] = (upward * share).astype(BF)
            density = jnp.exp(-0.5 * upward * upward) * 0.3989422804014327
            gelup[s, :, cols] = (share + upward * density).astype(BF)
            return carry

        lax.fori_loop(0, 4, tile, 0)

    def mlp_down(s):
        rows = act[s]

        def tile(n, carry):
            cols = pl.ds(al(n, 256), 256)
            weight = wd[:, :, :, cols].reshape(D, 256)
            part[s, :, cols] = dot(rows, weight, 1, 0).astype(BF)
            return carry

        lax.fori_loop(0, 4, tile, 0)

    rs2 = scatters()
    ag2 = [Gather(gdf, rows_of, s) for s in (0, 1)]
    lo_s, lo_r, lo_l = new("s", 6), new("r", 8), new("l", 2)

    def second_norm(s):
        hidden = normed1[s] * gain1 + offset1
        second_sum = rs2[s].result() + down_bias + hidden
        normed, inverse = norm_stats(second_sum)
        lo[s] = (normed * gain2 + offset2).astype(BF)
        grad = og[s].astype(F32)
        vec_sum[0:1, :] += col_sum(grad * normed)
        vec_sum[1:2, :] += col_sum(grad)
        grad_second = norm_pull(grad, normed, inverse, gain2)
        gsec[s] = grad_second
        rounded = grad_second.astype(BF)
        vec_sum[4:5, :] += col_sum(rounded.astype(F32))
        gdf[s, own_rows, :] = rounded
        ag2[s].send()

    def lo_place(s, row):
        return lo_out.at[s, pl.ds(al(row, ROWS), ROWS), :]

    def lo_part(s, row):
        return lo.at[s, :, pl.ds(al(row, 256), 256)]

    lo_own = [
        pltpu.make_async_copy(lo_part(s, r), lo_place(s, r), ls.at[lo_l + s]) for s in (0, 1)
    ]

    def send_lo(s):
        lo_own[s].start()
        for j in (1, 2, 3):
            row = (r + j) % 4
            copy = remote(
                lo_s + 3 * s + j - 1, lo_r + 4 * s + r, lo_part(s, row), lo_place(s, r), (d, row, c)
            )
            copy.start()
            later(copy)

    mlp_up(0)
    ag1[1].forward()
    relay_og()
    ag1[1].wait()
    mlp_up(1)
    w_down.ready()
    rs1[0].sent()
    mlp_down(0)
    rs2[0].to_core()
    rs1[1].sent()
    rs2[0].to_y()
    mlp_down(1)
    rs2[1].to_core()
    rs2[1].to_y()
    wait_og()
    second_norm(0)
    second_norm(1)
    ag2[0].forward()
    ag2[0].wait()

    class Grad:
        def __init__(
            self, buffer, chunk, both, by_ci, pair_recv, col_recv, place, pair_first, by_row=False
        ):
            self.buffer, self.place, self.pair_first = buffer, place, pair_first
            pair_recvs, col_recvs = pair_recv, col_recv
            self.by_row = by_row
            self.rows = (r, r1, r2, r3)
            self.near_copy, self.far_copy, self.pair_copy = {}, {}, {}
            self.near_add, self.far_add, self.pair_add = {}, {}, {}
            self.own, self.rows_copies = None, {}
            self.chunk = chunk
            self.s3, self.r3, self.l3 = new("s", 7), new("r", 4), new("l")
            for n in range(len(pair_recv)):
                chip = self.rows[n] if by_row else (y if n == 0 else 1 - y)
                pair_recv, col_recv = pair_recvs[n], col_recvs[n]
                if pair_first[n]:
                    pair_src, pair_dst = both(buffer, 1 - p, chip), both(buffer, p, chip)
                    near_src, held = chunk(buffer, p, 1 - ic, chip), chunk(buffer, p, ic, chip)
                else:
                    pair_src, pair_dst = chunk(buffer, 1 - p, ic, chip), chunk(buffer, p, ic, chip)
                    near_src, held = by_ci(buffer, 1 - ic, chip), by_ci(buffer, ic, chip)
                self.pair_copy[n] = remote(new("s"), new("r"), pair_src, pair_recv, x_dev)
                self.near_copy[n] = remote(new("s"), new("r"), near_src, col_recv.at[0], near_dev)
                self.far_copy[n] = remote(new("s"), new("r"), held, col_recv.at[1], far_dev)
                self.pair_add[n] = (pair_dst, pair_recv)
                self.near_add[n] = (held, col_recv.at[0])
                self.far_add[n] = (held, col_recv.at[1])

        def add(self, refs):
            mine, other = refs
            mine[...] = (mine[...].astype(F32) + other[...].astype(F32)).astype(BF)

        def arrival(self, half, yp):
            return self.r3 + 2 * half + yp

        def rows_of_chunk(self, n):
            copies = []
            here, there = d, d + 1 - 2 * p
            if n == 0:
                self.own = pltpu.make_async_copy(self.piece(r), self.place(p, y), ls.at[self.l3])
            if self.by_row:
                targets = [(here, self.rows[n]), (there, self.rows[n])]
                at = 2 * n - 1
                if n == 0:
                    targets, at = targets[1:], 0
            elif n == 0:
                targets = [(here, r1), (there, r), (there, r1)]
                at = 0
            else:
                targets = [(here, r2), (there, r2), (here, r3), (there, r3)]
                at = 3
            for plane, row in targets:
                copies.append(
                    remote(
                        self.s3 + at,
                        self.arrival(p, y),
                        self.piece(row),
                        self.place(p, y),
                        (plane, row, c),
                    )
                )
                at += 1
            return copies

        def begin(self, n):
            first = self.pair_copy[n] if self.pair_first[n] else self.near_copy[n]
            first.start()
            later(first)

        def second(self, n):
            if self.pair_first[n]:
                self.pair_copy[n].wait_recv()
                self.add(self.pair_add[n])
                self.near_copy[n].start()
                later(self.near_copy[n])
            else:
                self.near_copy[n].wait_recv()
                self.add(self.near_add[n])

                @pl.when(jnp.logical_not(is_agg))
                def _():
                    self.far_copy[n].start()

                later(self.far_copy[n], jnp.logical_not(is_agg))

        def third(self, n):
            if self.pair_first[n]:
                self.near_copy[n].wait_recv()
                self.add(self.near_add[n])

                @pl.when(jnp.logical_not(is_agg))
                def _():
                    self.far_copy[n].start()

                later(self.far_copy[n], jnp.logical_not(is_agg))
            else:

                @pl.when(is_agg)
                def _():
                    self.far_copy[n].wait_recv()
                    self.add(self.far_add[n])
                    self.pair_copy[n].start()

                later(self.pair_copy[n], is_agg)

        def to_rows(self, n):
            copies = self.rows_of_chunk(n)

            @pl.when(is_agg)
            def _():
                if self.pair_first[n]:
                    self.far_copy[n].wait_recv()
                    self.add(self.far_add[n])
                else:
                    self.pair_copy[n].wait_recv()
                    self.add(self.pair_add[n])
                if n == 0:
                    self.own.start()
                for copy in copies:
                    copy.start()

            for copy in copies:
                later(copy, is_agg)

        def done(self):
            @pl.when(is_agg)
            def _():
                self.own.wait()

            @pl.when(jnp.logical_not(is_agg))
            def _():
                place = self.place(p, y)
                remote(self.s3, self.arrival(p, y), place, place, core_dev).wait_recv()

            for half, yp in ((p, 1 - y), (1 - p, y), (1 - p, 1 - y)):
                place = self.place(half, yp)
                remote(self.s3, self.arrival(half, yp), place, place, core_dev).wait_recv()

    def rows_both(ref, half, chip):
        return ref.at[pl.ds(2 * chip, 2), half]

    def cols_both(ref, half, chip):
        return ref.at[:, half, :, pl.ds(al(chip, 512), 512)]

    def cols_of_ci(ref, ci, chip):
        return ref.at[ci, :, :, pl.ds(al(chip, 512), 512)]

    def two(ref):
        return [ref.at[0], ref.at[1]]

    def qkv_row_both(ref, half, row):
        return ref.at[row, half]

    g_qkv = Grad(
        gq,
        qkv_row,
        qkv_row_both,
        None,
        [xq.at[n] for n in range(4)],
        [zq.at[n] for n in range(4)],
        lambda half, yp: fin_q.at[half, :, pl.ds(al(yp, 384), 384)],
        (True,) * 4,
        by_row=True,
    )
    g_qkv.piece = lambda row: gq.at[row, p, :, pl.ds(al(ic, 384), 384)]
    g_out = Grad(
        go, out_chunk, cols_both, None, two(xo), two(zo), lambda half, yp: fin_o.at[yp, half], (True, True)
    )
    g_out.piece = lambda row: go.at[ic, p, :, pl.ds(al(row, 256), 256)]
    g_up = Grad(
        gup,
        up_chunk,
        rows_both,
        None,
        two(xu),
        two(zu),
        lambda half, yp: fin_u.at[half, :, pl.ds(al(yp, 512), 512)],
        (True, True),
    )
    g_up.piece = lambda row: gup.at[row, p, :, pl.ds(al(ic, 512), 512)]
    g_down = Grad(
        gd,
        down_chunk,
        cols_both,
        cols_of_ci,
        [xd, xd1],
        [zd, zd1],
        lambda half, yp: fin_d.at[yp, half],
        (True, False),
    )
    g_down.piece = lambda row: gd.at[ic, p, :, pl.ds(al(row, 256), 256)]

    def tokens_by(ref, cols):
        return ref[:, :, cols].reshape(2 * SEQ, cols.size)

    def down_grad(m):
        cols = pl.ds(al(y if m == 0 else 1 - y, 512), 512)

        def tile(n, carry):
            left = tokens_by(act, pl.ds(al(n, 256), 256))
            right = gdf[:, :, cols].reshape(2 * SEQ, 512)
            gd[n // 2, n % 2, :, cols] = dot(left, right, 0, 0).astype(BF)
            return carry

        lax.fori_loop(0, 4, tile, 0)

    def up_grad():
        def tile(n, carry):
            left = tokens_by(hf, pl.ds(al(n, 256), 256))
            gup[n] = (
                dot(left, gu[...].reshape(2 * SEQ, D), 0, 0).astype(BF).reshape(2, 128, D)
            )
            return carry

        lax.fori_loop(0, 4, tile, 0)

    def out_grad():
        left = ctx[...].reshape(2 * SEQ, 256)
        go[...] = dot(left, gaf[...].reshape(2 * SEQ, D), 0, 0).astype(BF).reshape(2, 2, 64, D)

    def qkv_grad():
        def tile(n, carry):
            left = tokens_by(xf, pl.ds(al(n, 256), 256))
            gq[n] = (
                dot(left, gproj[...].reshape(2 * SEQ, 768), 0, 0).astype(BF).reshape(2, 128, 768)
            )
            return carry

        lax.fori_loop(0, 4, tile, 0)

    def pull_act(s):
        rows = gdf[s]

        def tile(n, carry):
            cols = pl.ds(al(n, 256), 256)
            grad = dot(rows, wd[n // 2, n % 2], 1, 1) * gelup[s, :, cols].astype(F32)
            rounded = grad.astype(BF)
            gu[s, :, cols] = rounded
            vec_sum[6:7, cols] += col_sum(rounded.astype(F32))
            return carry

        lax.fori_loop(0, 4, tile, 0)

    def pull_hidden(s):
        rows = gu[s]

        def tile(n, carry):
            weight = wu[n].reshape(256, D)
            part[s, :, pl.ds(al(n, 256), 256)] = dot(rows, weight, 1, 1).astype(BF)
            return carry

        lax.fori_loop(0, 4, tile, 0)

    rs3 = scatters()
    ag3 = [Gather(gaf, rows_of, s) for s in (0, 1)]

    def first_norm_pull(s):
        grad = gsec[s] + rs3[s].result()
        normed = normed1[s]
        vec_sum[2:3, :] += col_sum(grad * normed)
        vec_sum[3:4, :] += col_sum(grad)
        rounded = norm_pull(grad, normed, inv1[s][:, 0:1], gain1).astype(BF)
        vec_sum[5:6, :] += col_sum(rounded.astype(F32))
        gaf[s, own_rows, :] = rounded
        ag3[s].send()

    pull_act(0)
    rs2[0].sent()
    pull_hidden(0)
    rs3[0].to_core()
    ag2[1].forward()
    rs3[0].to_y()
    ag2[1].wait()
    down_grad(0)
    g_down.begin(0)
    down_grad(1)
    g_down.begin(1)
    pull_act(1)
    rs2[1].sent()
    pull_hidden(1)
    rs3[1].to_core()
    rs3[1].to_y()
    first_norm_pull(0)
    up_grad()
    g_up.begin(1)
    g_up.begin(0)
    g_down.second(1)
    g_down.second(0)
    first_norm_pull(1)
    ag3[0].forward()
    ag3[0].wait()

    def pull_attend(s):
        gctx[...] = dot(gaf[s], wo[...].reshape(256, D), 1, 1).astype(BF)
        lane = lax.broadcasted_iota(jnp.int32, (SEQ, 128), 1)
        row = lax.broadcasted_iota(jnp.int32, (128, SEQ), 0)
        scale_factor = float(HEAD) ** (-0.5)

        def pair(ci, carry):
            queries = proj[s, :, columns(ci, 0)]
            keys_in = proj[s, :, columns(ci, 1)]
            values_in = proj[s, :, columns(ci, 2)]
            grad = gctx[:, pl.ds(al(ci, 128), 128)]
            grads_q, grads_k, grads_v = [], [], []
            for h in (0, 1):
                chosen = (lane < HEAD) if h == 0 else (lane >= HEAD)
                masked = jnp.where(chosen, grad, jnp.zeros_like(grad))
                share = probs[s, ci * 2 + h]
                wide = share.astype(F32)
                weighted = wide * dot(values_in, masked, 1, 1)
                total = jnp.sum(weighted, 0, keepdims=True)
                grad_scores = (weighted - wide * total).astype(BF)
                grads_v.append(dot(share, grad, 1, 0))
                grads_k.append(dot(grad_scores, queries, 1, 0))
                grads_q.append(dot(keys_in, grad_scores, 0, 0))
            both_q = jnp.transpose(jnp.where(row < HEAD, grads_q[0], grads_q[1]) * scale_factor)
            both_q = both_q.astype(BF)
            both_v = jnp.where(lane < HEAD, grads_v[0], grads_v[1]).astype(BF)
            both_k = jnp.where(lane < HEAD, grads_k[0], grads_k[1]) * scale_factor
            gproj[s, :, columns(ci, 0)] = both_q
            gproj[s, :, columns(ci, 1)] = both_k.astype(BF)
            gproj[s, :, columns(ci, 2)] = both_v
            at = pl.ds(al(ci, 128), 128)
            vec_sum[7:8, at] += col_sum(both_q.astype(F32))
            at = pl.ds(pl.multiple_of(256 + ci * 128, 128), 128)
            vec_sum[7:8, at] += col_sum(both_v.astype(F32))
            return carry

        lax.fori_loop(0, 2, pair, 0)

    def pull_tokens(s):
        rows = gproj[s]

        def tile(n, carry):
            partf[s, n] = dot(rows, wq[n].reshape(256, 768), 1, 1).astype(BF)
            return carry

        lax.fori_loop(0, 4, tile, 0)

    rs4 = [Scatter(partf, lambda ref, s, row: ref.at[s, row], rscf, ysendf, rsyf, s) for s in (0, 1)]
    tg_l = new("l", 2)
    tg_copy = [pltpu.make_async_copy(tg.at[s], tg_out.at[s], ls.at[tg_l + s]) for s in (0, 1)]

    def tokens_done(s):
        tg[s] = rs4[s].result() + slab_of(gaf, s, r)[...].astype(F32)
        tg_copy[s].start()

    class Sums:
        def __init__(self):
            self.si, self.ri = new("s", 7), new("r", 9)
            self.pair = remote(self.si + 6, self.ri + 8, vec_part, vec_pair, x_dev)

        def to_rows(self):
            vec_rows[r] = vec_sum[...]
            for j in (1, 2, 3):
                copy = remote(
                    self.si + j - 1, self.ri + r, vec_sum, vec_rows.at[r], (d, (r + j) % 4, c)
                )
                copy.start()
                later(copy)

        def to_cols(self):
            for j in (1, 2, 3):
                place = vec_rows.at[(r + j) % 4]
                remote(self.si, self.ri + (r + j) % 4, place, place, core_dev).wait_recv()
            mine = pl.ds(al(r, 256), 256)
            features = vec_rows[0, 0:6, mine] + vec_rows[1, 0:6, mine]
            features = features + vec_rows[2, 0:6, mine] + vec_rows[3, 0:6, mine]
            for j in (0, 1, 2, 3):
                to = (c + j) % 4
                slot = vec_out_parts.at[j]
                slot[0:6, :] = features
                for yp in (0, 1):
                    row = 2 * yp + to // 2
                    ci = to % 2
                    for n in (0, 1):
                        at = pl.ds(pl.multiple_of(ci * 512 + n * 256, 256), 256)
                        slot[6 + 2 * yp + n : 7 + 2 * yp + n, :] = vec_rows[row, 6:7, at]
                        at = pl.ds(pl.multiple_of(n * 256 + ci * 128, 128), 128)
                        slot[10 + n : 11 + n, yp * 128 : yp * 128 + 128] = vec_rows[row, 7:8, at]
                slot[12:16, :] = jnp.zeros((4, 256), F32)
                if j > 0:
                    copy = remote(
                        self.si + 2 + j,
                        self.ri + 4 + c,
                        slot,
                        vec_cols.at[c],
                        (d, r, to),
                    )
                    copy.start()
                    later(copy)

        def to_pair(self):
            total = vec_out_parts[0]
            for j in (1, 2, 3):
                source = (c + j) % 4
                place = vec_cols.at[source]
                remote(self.si, self.ri + 4 + source, place, place, core_dev).wait_recv()
                total = total + vec_cols[source]
            vec_part[...] = total
            self.pair.start()
            later(self.pair)

        def done(self):
            self.pair.wait_recv()
            vec_out[...] = vec_part[...] + vec_pair[...]

    pull_attend(0)
    ag3[1].forward()
    g_up.second(1)
    pull_tokens(0)
    rs4[0].to_core()
    g_down.third(1)
    rs4[0].to_y()
    g_down.third(0)
    ag3[1].wait()
    pull_attend(1)
    sums = Sums()
    sums.to_rows()
    qkv_grad()
    g_qkv.begin(3)
    g_qkv.begin(2)
    g_qkv.begin(1)
    g_up.second(0)
    out_grad()
    g_out.begin(1)
    g_out.begin(0)
    g_qkv.begin(0)
    g_up.third(1)
    pull_tokens(1)
    rs4[1].to_core()
    g_down.to_rows(0)
    rs4[1].to_y()
    send_lo(0)
    send_lo(1)
    g_down.to_rows(1)
    tokens_done(0)
    g_qkv.second(3)
    sums.to_cols()
    g_up.to_rows(1)
    g_qkv.second(2)
    g_up.third(0)
    tokens_done(1)
    g_qkv.third(3)
    g_qkv.second(1)
    g_qkv.third(2)
    g_qkv.to_rows(3)
    g_up.to_rows(0)
    g_out.second(1)
    sums.to_pair()
    g_qkv.third(1)
    g_qkv.to_rows(2)
    g_out.second(0)
    g_qkv.second(0)
    g_out.third(1)
    g_qkv.to_rows(1)
    g_out.third(0)
    g_qkv.third(0)
    g_out.to_rows(1)
    g_out.to_rows(0)
    g_qkv.to_rows(0)
    sums.done()
    g_down.done()
    g_up.done()
    g_out.done()
    g_qkv.done()

    for s in (0, 1):
        rs3[s].sent()
        rs4[s].sent()
        tg_copy[s].wait()
        lo_own[s].wait()
        for j in (1, 2, 3):
            source = (r + j) % 4
            place = lo_place(s, source)
            remote(lo_s, lo_r + 4 * s + source, place, place, core_dev).wait_recv()
    for condition, copy in late:
        if condition is None:
            copy.wait_send()
        else:
            pl.when(condition)(copy.wait_send)


S_SEMS = 320
R_SEMS = 320
L_SEMS = 32


def run_layer(seg, x, og, wq, wo, wu, wd, *vecs):
    any_spec = pl.BlockSpec(memory_space=pl.ANY)
    vmem = pl.BlockSpec(memory_space=pltpu.VMEM)
    out = jax.ShapeDtypeStruct
    outs = [
        (out((2, SEQ, 256), BF), any_spec),
        (out((2, SEQ, 256), F32), any_spec),
        (out((2, 128, 768), BF), any_spec),
        (out((2, 2, 64, 256), BF), any_spec),
        (out((2, 128, D), BF), any_spec),
        (out((2, 2, 256, 256), BF), any_spec),
        (out((16, 256), F32), vmem),
    ]
    full = ((2, SEQ, D), BF)
    scratch = [
        ((2, SEQ), jnp.int32),
        ((8, D), F32),
        ((4, 8, D), F32),
        full,
        ((4, 2, 128, 768), BF),
        ((2, 2, 64, D), BF),
        ((4, 2, 128, D), BF),
        ((2, 2, 256, D), BF),
        ((3, 2, 128, 128), BF),
        ((2, 64, 256), BF),
        ((2, 128, 512), BF),
        ((2, 256, 256), BF),
        ((2, SEQ, 768), BF),
        ((2, 4, SEQ, SEQ), BF),
        ((2, SEQ, 256), BF),
        ((SEQ, SEQ), F32),
        full,
        ((2, 2, ROWS, D), BF),
        ((2, ROWS, D), BF),
        ((2, ROWS, D), BF),
        ((2, ROWS, D), F32),
        ((2, ROWS, 128), F32),
        full,
        full,
        full,
        ((2, ROWS, D), BF),
        ((2, ROWS, 256), BF),
        ((2, ROWS, D), BF),
        ((2, ROWS, D), F32),
        full,
        full,
        full,
        ((SEQ, 256), BF),
        ((2, SEQ, 768), BF),
        ((2, 4, SEQ, 256), BF),
        ((2, 2, SEQ, 256), BF),
        ((2, SEQ, 256), BF),
        ((2, SEQ, 256), BF),
        ((2, SEQ, 256), F32),
        ((4, 2, 128, 768), BF),
        ((2, 2, 64, D), BF),
        ((4, 2, 128, D), BF),
        ((2, 2, 256, D), BF),
        ((4, 128, 768), BF),
        ((2, 2, 64, 512), BF),
        ((2, 2, 128, D), BF),
        ((2, 256, 512), BF),
        ((256, 512), BF),
        ((4, 2, 128, 384), BF),
        ((2, 2, 64, 512), BF),
        ((2, 2, 2, 128, 512), BF),
        ((2, 256, 512), BF),
        ((2, 2, 256, 512), BF),
        ((8, D), F32),
        ((4, 8, D), F32),
        ((4, 16, 256), F32),
        ((4, 16, 256), F32),
        ((16, 256), F32),
        ((16, 256), F32),
    ]
    return pl.pallas_call(
        layer_kernel,
        out_shape=[o[0] for o in outs],
        in_specs=[any_spec] * 7 + [vmem] * len(vecs),
        out_specs=[o[1] for o in outs],
        scratch_shapes=[pltpu.VMEM(shape, dtype) for shape, dtype in scratch]
        + [
            pltpu.SemaphoreType.DMA((S_SEMS,)),
            pltpu.SemaphoreType.DMA((R_SEMS,)),
            pltpu.SemaphoreType.DMA((L_SEMS,)),
        ],
        compiler_params=pltpu.CompilerParams(
            collective_id=0, has_side_effects=True, vmem_limit_bytes=62 * 1024 * 1024
        ),
        name="layer",
    )(seg, x, og, wq, wo, wu, wd, *vecs)


def finish_kernel(lo, tg, fq, fo, fu, fd, vec, lo_out, tg_out, q_out, o_out, u_out, d_out, *vectors):
    lo_out[...] = lo[...]
    tg_out[...] = tg[...]
    for yp in (0, 1):
        for n in (0, 1, 2):
            at = yp * 384 + n * 128
            q_out[n, :, yp * 128 : yp * 128 + 128] = fq[:, at : at + 128].astype(F32)
    o_out[...] = fo[...].astype(F32)
    u_out[...] = fu[...].astype(F32)
    d_out[...] = fd[...].astype(F32)
    for n in range(6):
        vectors[n][...] = vec[n : n + 1, :]
    for n in range(4):
        vectors[6][:, n * 256 : n * 256 + 256] = vec[6 + n : 7 + n, :]
    vectors[7][...] = vec[10:12, :]


def finish(*arrays):
    steps = 2
    out = jax.ShapeDtypeStruct

    def rows_spec(shape):
        return pl.BlockSpec((shape[0] // steps, shape[1]), lambda i: (i, 0))

    def whole(shape):
        return pl.BlockSpec(shape, lambda i: (0, 0))

    shapes = [out(arrays[0].shape, BF)] + [out(a.shape, F32) for a in arrays[1:6]]
    vectors = [out((1, 256), F32)] * 6 + [out((1, D), F32), out((2, 256), F32)]
    shapes[2] = out((3, 256, 256), F32)
    out_specs = [rows_spec(a.shape) for a in shapes] + [whole(v.shape) for v in vectors]
    out_specs[2] = pl.BlockSpec((3, 256 // steps, 256), lambda i: (0, i, 0))
    return pl.pallas_call(
        finish_kernel,
        grid=(steps,),
        in_specs=[rows_spec(a.shape) for a in arrays[:6]] + [whole(arrays[6].shape)],
        out_specs=out_specs,
        out_shape=shapes + vectors,
        name="finish",
    )(*arrays)


def shards(
    pairs,
    tokens,
    segments,
    qkv_weight,
    qv_bias,
    out_weight,
    out_bias,
    norm1_gain,
    norm1_bias,
    up_weight,
    up_bias,
    down_weight,
    down_bias,
    norm2_gain,
    norm2_bias,
    out_grad,
):
    lo, tg, fin_q, fin_o, fin_u, fin_d, vec = run_layer(
        segments,
        tokens.reshape(2, SEQ, 256),
        out_grad.reshape(2, SEQ, 256),
        qkv_weight.transpose(1, 0, 2).reshape(3, 2, 128, 256),
        out_weight.reshape(2, 2, 64, 256),
        up_weight.reshape(2, 128, D),
        down_weight.reshape(2, 2, 256, 256),
        up_bias.reshape(1, D),
        qv_bias,
        out_bias.reshape(1, D),
        norm1_gain.reshape(1, D),
        norm1_bias.reshape(1, D),
        down_bias.reshape(1, D),
        norm2_gain.reshape(1, D),
        norm2_bias.reshape(1, D),
    )
    grads = (fin_q, fin_o, fin_u, fin_d, vec)
    if pairs is not None:
        grads = lax.psum(grads, "dp", axis_index_groups=pairs)
    fin_q, fin_o, fin_u, fin_d, vec = grads
    results = finish(
        lo.reshape(2 * SEQ, 256),
        tg.reshape(2 * SEQ, 256),
        fin_q.reshape(256, 768),
        fin_o.reshape(256, 256),
        fin_u.reshape(256, D),
        fin_d.reshape(D, 256),
        vec,
    )
    layer_out, tokens_grad, qkv_grad, out_grad_w, up_grad, down_grad = results[:6]
    n2_gain, n2_bias, n1_gain, n1_bias, down_b, out_b, up_b, qv_b = results[6:]
    return (
        layer_out,
        tokens_grad,
        qkv_grad.transpose(1, 0, 2),
        qv_b,
        out_grad_w,
        out_b.reshape(256),
        n1_gain.reshape(256),
        n1_bias.reshape(256),
        up_grad,
        up_b.reshape(D),
        down_grad,
        down_b.reshape(256),
        n2_gain.reshape(256),
        n2_bias.reshape(256),
    )


def solution(mesh):
    placed = (
        P(("dp", "col"), "row"),
        P(("dp", "row"), None),
        P("row", None, "col"),
        P(None, "col"),
        P("col", "row"),
        P(),
        P(),
        P(),
        P("row", "col"),
        P("col"),
        P("col", "row"),
        P(),
        P(),
        P(),
        P(("dp", "col"), "row"),
    )
    dp = mesh.shape["dp"]
    pairs = None
    if dp > 2:
        pairs = [list(range(0, dp, 2)), list(range(1, dp, 2))]
    return jax.shard_map(
        functools.partial(shards, pairs),
        mesh=mesh,
        in_specs=placed,
        out_specs=(
            P(("dp", "col"), "row"),
            P(("dp", "col"), "row"),
            P("row", None, "col"),
            P(None, "col"),
            P("col", "row"),
            P("row"),
            P("row"),
            P("row"),
            P("row", "col"),
            P("col"),
            P("col", "row"),
            P("row"),
            P("row"),
            P("row"),
        ),
        check_vma=False,
    )
```

```python
import functools

import jax
import jax.numpy as jnp
from jax import lax
from jax.experimental import pallas as pl
from jax.experimental.pallas import tpu as pltpu
from jax.sharding import PartitionSpec as P

D = 1024
HEAD = 64
SEQ = 512
EPS = 1e-05
MESH = pl.DeviceIdType.MESH
BF = jnp.bfloat16
F32 = jnp.float32
ROWS = 128


def dot(left, right, left_dim, right_dim):
    return lax.dot_general(
        left, right, (((left_dim,), (right_dim,)), ((), ())), preferred_element_type=F32
    )


def al(index, step):
    return pl.multiple_of(index * step, step)


def col_sum(values):
    return jnp.sum(values, 0, keepdims=True)


def layer_kernel(
    seg_in,
    x_in,
    og_in,
    wq_in,
    wo_in,
    wu_in,
    wd_in,
    up_bias_in,
    qv_bias_in,
    out_bias_in,
    gain1_in,
    offset1_in,
    down_bias_in,
    gain2_in,
    offset2_in,
    lo_out,
    tg_out,
    fin_q,
    fin_o,
    fin_u,
    fin_d,
    vec_out,
    seg,
    bias_own,
    biases,
    xf,
    wq,
    wo,
    wu,
    wd,
    stage_q,
    stage_o,
    stage_u,
    stage_d,
    proj,
    probs,
    ctx,
    mask,
    part,
    rsc,
    rsy,
    ysend,
    normed1,
    inv1,
    hf,
    act,
    gelup,
    og,
    og_stage,
    lo,
    gsec,
    gdf,
    gu,
    gaf,
    gctx,
    gproj,
    partf,
    rscf,
    rsyf,
    ysendf,
    tg,
    gq,
    go,
    gup,
    gd,
    xq,
    xo,
    xu,
    xd,
    xd1,
    zq,
    zo,
    zu,
    zd,
    zd1,
    vec_sum,
    vec_rows,
    vec_out_parts,
    vec_cols,
    vec_part,
    vec_pair,
    ss,
    rs,
    ls,
):
    d = lax.axis_index("dp")
    r = lax.axis_index("row")
    c = lax.axis_index("col")
    y = r // 2
    k = r % 2
    p = d % 2
    r1 = r + 1 - 2 * k
    r2 = (r + 2) % 4
    r3 = (r1 + 2) % 4
    kc = c // 2
    ic = c % 2
    is_agg = k == kc
    core_dev = (d, r1, c)
    y_dev = (d, r2, c)
    x_dev = (d + 1 - 2 * p, r, c)

    counts = {"s": 0, "r": 0, "l": 0}

    def new(kind, n=1):
        at = counts[kind]
        counts[kind] += n
        return at

    def remote(si, ri, src, dst, dev):
        return pltpu.make_async_remote_copy(
            src_ref=src,
            dst_ref=dst,
            send_sem=ss.at[si],
            recv_sem=rs.at[ri],
            device_id=dev,
            device_id_type=MESH,
        )

    late = []

    def later(copy, condition=None):
        late.append((condition, copy))

    barrier = pltpu.get_barrier_semaphore()
    for j in (1, 2, 3):
        pl.semaphore_signal(barrier, inc=1, device_id=(d, (r + j) % 4, c), device_id_type=MESH)
        pl.semaphore_signal(barrier, inc=1, device_id=(d, r, (c + j) % 4), device_id_type=MESH)
    pl.semaphore_signal(barrier, inc=1, device_id=x_dev, device_id_type=MESH)

    @pl.when(r != c)
    def _():
        pl.semaphore_signal(barrier, inc=1, device_id=(d, c, r), device_id_type=MESH)
        pl.semaphore_wait(barrier, 8)

    @pl.when(r == c)
    def _():
        pl.semaphore_wait(barrier, 7)

    def qkv_piece(yp, n):
        return wq_in.at[n, :, :, pl.ds(al(yp, 128), 128)]

    def out_piece(yp, n):
        return wo_in.at[yp]

    def up_piece(yp, n):
        return wu_in.at[:, :, pl.ds(al(yp, 512), 512)]

    def down_piece(yp, n):
        return wd_in.at[yp]

    def qkv_place(row, n):
        return wq.at[row, :, :, pl.ds(pl.multiple_of(ic * 384 + n * 128, 128), 128)]

    def out_place(row, n):
        return wo.at[ic, :, :, pl.ds(al(row, 256), 256)]

    def up_place(row, n):
        return wu.at[row, :, :, pl.ds(al(ic, 512), 512)]

    def down_place(row, n):
        return wd.at[ic, :, :, pl.ds(al(row, 256), 256)]

    def qkv_half(ref, half, ci):
        return ref.at[:, half, :, pl.ds(al(ci, 384), 384)]

    def out_half(ref, half, ci):
        return ref.at[ci, half]

    def up_half(ref, half, ci):
        return ref.at[:, half, :, pl.ds(al(ci, 512), 512)]

    def down_half(ref, half, ci):
        return ref.at[ci, half]

    def out_chunk(ref, half, ci, chip):
        return ref.at[ci, half, :, pl.ds(al(chip, 512), 512)]

    def up_chunk(ref, half, ci, chip):
        return ref.at[pl.ds(2 * chip, 2), half, :, pl.ds(al(ci, 512), 512)]

    down_chunk = out_chunk

    def qkv_row(ref, half, ci, row):
        return ref.at[row, half, :, pl.ds(al(ci, 384), 384)]

    def out_row(ref, half, ci, row):
        return ref.at[ci, half, :, pl.ds(al(row, 256), 256)]

    def up_row(ref, half, ci, row):
        return ref.at[row, half, :, pl.ds(al(ci, 512), 512)]

    down_row = out_row
    chip_rows = ((r, r1), (r2, r3))
    far_dev = (d, r, (c + 2) % 4)
    near_dev = (d, r, c + 1 - 2 * ic)

    class Weight:
        def __init__(self, buffer, piece, place, at_row, stages):
            self.piece, self.place, self.stages = piece, place, stages
            self.parts = range(len(stages))
            self.s1, self.r1, self.l1 = [], [], []
            self.relay_copies, self.staged = [], []
            for q, stage in enumerate(stages):
                self.s1.append(new("s", 2))
                self.r1.append(new("r", 4))
                self.l1.append(new("l"))
                self.relay_copies.append(
                    remote(new("s"), self.r1[q] + r2, stage, place(r2, q), core_dev)
                )
                self.staged.append(remote(self.s1[q], self.r1[q] + r2, stage, stage, y_dev))
            self.far_copy, self.near_copy, self.pair_far, self.pair_near = {}, {}, {}, {}
            for n, m in ((0, 0), (0, 1), (1, 0), (1, 1)):
                row = chip_rows[n][m]
                held = at_row(buffer, p, ic, row)
                wanted = at_row(buffer, p, 1 - ic, row)
                self.far_copy[n, m] = remote(new("s"), new("r"), held, held, far_dev)
                si, ri = new("s"), new("r")
                self.near_copy[n, m] = (
                    remote(si, ri, held, held, near_dev),
                    remote(si, ri, wanted, wanted, near_dev),
                )
                si, ri = new("s"), new("r")
                missing = at_row(buffer, 1 - p, ic, row)
                self.pair_far[n, m] = (
                    remote(si, ri, held, held, x_dev),
                    remote(si, ri, missing, missing, x_dev),
                )
                si, ri = new("s"), new("r")
                missing = at_row(buffer, 1 - p, 1 - ic, row)
                self.pair_near[n, m] = (
                    remote(si, ri, wanted, wanted, x_dev),
                    remote(si, ri, missing, missing, x_dev),
                )

        def spread_rows(self):
            self.own = []
            for q in self.parts:
                mine, to = self.piece(y, q), self.place(r, q)
                across = self.piece(1 - y, q)
                near = remote(self.s1[q] + 1, self.r1[q] + r, mine, to, core_dev)
                own = pltpu.make_async_copy(mine, to, ls.at[self.l1[q]])
                direct = remote(self.s1[q], self.r1[q] + r, across, to, y_dev)
                staged = remote(self.s1[q], self.r1[q] + r, across, self.stages[q], y_dev)

                @pl.when(jnp.logical_not(is_agg))
                def _():
                    near.start()
                    staged.start()

                @pl.when(is_agg)
                def _():
                    own.start()
                    direct.start()

                later(near, jnp.logical_not(is_agg))
                later(direct)
                self.own.append(own)

        def relay(self):
            @pl.when(jnp.logical_not(is_agg))
            def _():
                for q in self.parts:
                    self.staged[q].wait_recv()
                    self.relay_copies[q].start()

            for copy in self.relay_copies:
                later(copy, jnp.logical_not(is_agg))

        def lead(self, n):
            @pl.when(is_agg)
            def _():
                for m in (0, 1):
                    row = chip_rows[n][m]
                    for q in self.parts:
                        if (n, m) == (0, 0):
                            self.own[q].wait()
                        else:
                            place = self.place(row, q)
                            remote(
                                self.s1[q], self.r1[q] + row, place, place, core_dev
                            ).wait_recv()
                    self.far_copy[n, m].start()
                    self.near_copy[n, m][0].start()

            for m in (0, 1):
                later(self.far_copy[n, m], is_agg)
                later(self.near_copy[n, m][0], is_agg)

        def follow(self, n):
            other = jnp.logical_not(is_agg)

            @pl.when(other)
            def _():
                for m in (0, 1):
                    self.far_copy[n, m].wait_recv()
                    self.near_copy[n, m][0].start()
                    self.pair_far[n, m][0].start()

            for m in (0, 1):
                later(self.near_copy[n, m][0], other)
                later(self.pair_far[n, m][0], other)

        def pair(self, n, spreading):
            mine = is_agg if spreading else jnp.logical_not(is_agg)

            @pl.when(mine)
            def _():
                for m in (0, 1):
                    self.near_copy[n, m][1].wait_recv()
                    self.pair_near[n, m][0].start()

            for m in (0, 1):
                later(self.pair_near[n, m][0], mine)

        def ready(self):
            for key in ((0, 0), (0, 1), (1, 0), (1, 1)):

                @pl.when(jnp.logical_not(is_agg))
                def _():
                    self.pair_far[key][1].wait_recv()

                self.pair_near[key][1].wait_recv()

    w_qkv = Weight(wq, qkv_piece, qkv_place, qkv_row, [stage_q.at[q] for q in (0, 1, 2)])
    w_out = Weight(wo, out_piece, out_place, out_row, [stage_o])
    w_up = Weight(wu, up_piece, up_place, up_row, [stage_u])
    w_down = Weight(wd, down_piece, down_place, down_row, [stage_d])

    def rows_of(ref, s, row):
        return ref.at[s, pl.ds(al(row, ROWS), ROWS), :]

    def slab_of(ref, s, row):
        return ref.at[s, :, pl.ds(al(row, 256), 256)]

    class Gather:
        def __init__(self, full, at, s, source=None):
            self.full, self.at, self.s = full, at, s
            self.source = source
            self.si, self.ri = [new("s"), new("s"), new("s")], new("r", 3)

        def send(self):
            mine = self.source if self.source is not None else self.at(self.full, self.s, r)
            place = self.at(self.full, self.s, r)
            for n, dev in ((0, y_dev), (1, core_dev)):
                copy = remote(self.si[n], self.ri + n, mine, place, dev)
                copy.start()
                later(copy)

        def forward(self):
            place = self.at(self.full, self.s, r2)
            remote(self.si[0], self.ri, place, place, y_dev).wait_recv()
            copy = remote(self.si[2], self.ri + 2, place, place, core_dev)
            copy.start()
            later(copy)

        def wait(self):
            near = self.at(self.full, self.s, r1)
            remote(self.si[1], self.ri + 1, near, near, core_dev).wait_recv()
            far = self.at(self.full, self.s, r3)
            remote(self.si[2], self.ri + 2, far, far, core_dev).wait_recv()

    class Scatter:
        def __init__(self, source, at, core_recv, y_send, y_recv, s):
            self.source, self.at = source, at
            self.core_recv, self.y_send, self.y_recv, self.s = core_recv, y_send, y_recv, s
            si, ri = [new("s"), new("s"), new("s")], new("r", 3)
            self.far = remote(si[0], ri, at(source, s, r3), core_recv.at[s, 1], core_dev)
            self.near = remote(si[1], ri + 1, at(source, s, r1), core_recv.at[s, 0], core_dev)
            self.cross = remote(si[2], ri + 2, y_send.at[s], y_recv.at[s], y_dev)

        def to_core(self):
            self.far.start()
            self.near.start()

        def to_y(self):
            self.far.wait_recv()
            total = self.at(self.source, self.s, r2)[...].astype(F32)
            self.y_send[self.s] = (total + self.core_recv[self.s, 1].astype(F32)).astype(BF)
            self.cross.start()

        def result(self):
            self.near.wait_recv()
            total = self.at(self.source, self.s, r)[...].astype(F32)
            total = total + self.core_recv[self.s, 0].astype(F32)
            self.cross.wait_recv()
            return total + self.y_recv[self.s].astype(F32)

        def sent(self):
            self.far.wait_send()
            self.near.wait_send()
            self.cross.wait_send()

    w_qkv.spread_rows()
    x_gather = [Gather(xf, slab_of, s, x_in.at[s]) for s in (0, 1)]
    x_own = [
        pltpu.make_async_copy(x_in.at[s], slab_of(xf, s, r), ls.at[new("l")]) for s in (0, 1)
    ]
    seg_s, seg_r, seg_l = new("s"), new("r"), new("l")
    seg_copy = remote(seg_s, seg_r, seg_in, seg, (d, c, r))
    seg_own = pltpu.make_async_copy(seg_in, seg, ls.at[seg_l])

    @pl.when(r != c)
    def _():
        seg_copy.start()

    @pl.when(r == c)
    def _():
        seg_own.start()

    bias_s, bias_r = new("s", 3), new("r", 4)
    bias_own[...] = jnp.zeros_like(bias_own)
    bias_own[0:1, :] = up_bias_in[...]
    bias_own[1:2, 0:256] = qv_bias_in[0:1, :]
    bias_own[1:2, 256:512] = qv_bias_in[1:2, :]
    for j in (1, 2, 3):
        copy = remote(bias_s + j - 1, bias_r + c, bias_own, biases.at[c], (d, r, (c + j) % 4))
        copy.start()
        later(copy)
    biases[c] = bias_own[...]
    w_out.spread_rows()
    for s in (0, 1):
        x_gather[s].send()
        x_own[s].start()

    w_up.spread_rows()
    w_down.spread_rows()
    og_s, og_r, og_l = new("s", 4), new("r", 5), new("l")

    def og_place(row):
        return og.at[:, :, pl.ds(al(row, 256), 256)]

    def og_rows(row):
        return og_in.at[:, pl.ds(al(row, ROWS), ROWS), :]

    og_own = pltpu.make_async_copy(og_rows(r), og_place(r), ls.at[og_l])
    og_own.start()
    og_copies = [
        remote(og_s, og_r + r, og_rows(r1), og_place(r), core_dev),
        remote(og_s + 1, og_r + r, og_rows(r2), og_place(r), y_dev),
        remote(og_s + 2, og_r + 4, og_rows(r3), og_stage, y_dev),
    ]
    for copy in og_copies:
        copy.start()
        later(copy)
    og_relay = remote(og_s + 3, og_r + r2, og_stage, og_place(r2), core_dev)

    def relay_og():
        remote(og_s + 2, og_r + 4, og_stage, og_stage, y_dev).wait_recv()
        og_relay.start()
        later(og_relay)

    def wait_og():
        og_own.wait()
        for j in (1, 2, 3):
            place = og_place((r + j) % 4)
            remote(og_s, og_r + (r + j) % 4, place, place, core_dev).wait_recv()

    w_qkv.lead(0)
    w_qkv.relay()
    w_out.relay()
    w_qkv.follow(0)
    w_qkv.lead(1)
    w_out.lead(0)
    w_out.lead(1)
    w_up.lead(0)
    w_qkv.pair(0, True)
    w_qkv.pair(0, False)
    w_qkv.follow(1)
    x_gather[0].forward()
    w_out.follow(0)
    w_qkv.pair(1, True)
    w_qkv.pair(1, False)
    w_out.follow(1)
    x_gather[1].forward()
    w_out.pair(0, True)
    w_out.pair(0, False)
    w_out.pair(1, True)
    w_out.pair(1, False)
    w_up.relay()

    for j in (1, 2, 3):
        source = (c + j) % 4
        remote(bias_s, bias_r + source, biases.at[source], biases.at[source], core_dev).wait_recv()

    @pl.when(r != c)
    def _():
        seg_copy.wait_recv()

    @pl.when(r == c)
    def _():
        seg_own.wait()

    later(seg_copy, r != c)
    w_qkv.ready()

    vec_sum[...] = jnp.zeros_like(vec_sum)

    def project(s):
        rows = xf[s]

        def half(ci, carry):
            weight = wq[:, :, :, pl.ds(al(ci, 384), 384)].reshape(D, 384)
            q_bias = biases[2 * k + ci, 1:2, pl.ds(al(y, 128), 128)]
            v_bias = biases[2 * k + ci, 1:2, pl.ds(pl.multiple_of(256 + y * 128, 128), 128)]
            bias = jnp.concatenate([q_bias, jnp.zeros_like(q_bias), v_bias], 1)
            proj[s, :, pl.ds(al(ci, 384), 384)] = (dot(rows, weight, 1, 0) + bias).astype(BF)
            return carry

        lax.fori_loop(0, 2, half, 0)

    def columns(ci, n):
        return pl.ds(pl.multiple_of(ci * 384 + n * 128, 128), 128)

    def attend(s):
        labels = seg[s : s + 1, :].astype(F32)
        down = jnp.transpose(jnp.broadcast_to(labels, (128, SEQ)))[:, 0:1]
        mask[...] = jnp.where(down == labels, 0.0, -1e30)
        lane = lax.broadcasted_iota(jnp.int32, (SEQ, 128), 1)
        row = lax.broadcasted_iota(jnp.int32, (128, SEQ), 0)

        def pair(ci, carry):
            queries = proj[s, :, columns(ci, 0)]
            keys_in = proj[s, :, columns(ci, 1)]
            values_in = proj[s, :, columns(ci, 2)]
            parts = []
            for h in (0, 1):
                chosen = (lane < HEAD) if h == 0 else (lane >= HEAD)
                masked = jnp.where(chosen, queries, jnp.zeros_like(queries))
                scores = dot(keys_in, masked, 1, 1) * (float(HEAD) ** (-0.5)) + mask[...]
                weights = jnp.exp(scores - jnp.max(scores, 0, keepdims=True))
                totals = jnp.sum(weights, 0, keepdims=True)
                share = (weights * (1.0 / totals)).astype(BF)
                probs[s, ci * 2 + h] = share
                parts.append(dot(values_in, share, 0, 0))
            both = jnp.where(row < HEAD, parts[0], parts[1])
            ctx[s, :, pl.ds(al(ci, 128), 128)] = jnp.transpose(both).astype(BF)
            return carry

        lax.fori_loop(0, 2, pair, 0)

    def out_partial(s):
        part[s] = dot(ctx[s], wo[...].reshape(256, D), 1, 0).astype(BF)

    def norm_stats(summed):
        center = jnp.sum(summed, 1, keepdims=True) * (1.0 / D)
        spread = jnp.sum(summed * summed, 1, keepdims=True) * (1.0 / D) - center * center
        inverse = lax.rsqrt(spread + EPS)
        return (summed - center) * inverse, inverse

    def norm_pull(grad, normed, inverse, gain):
        scaled = grad * gain
        first = jnp.sum(scaled, 1, keepdims=True) * (1.0 / D)
        second = jnp.sum(scaled * normed, 1, keepdims=True) * (1.0 / D)
        return inverse * (scaled - first - normed * second)

    out_bias, gain1, offset1 = out_bias_in[...], gain1_in[...], offset1_in[...]
    down_bias, gain2, offset2 = down_bias_in[...], gain2_in[...], offset2_in[...]
    own_rows = pl.ds(al(r, ROWS), ROWS)

    def scatters():
        return [Scatter(part, rows_of, rsc, ysend, rsy, s) for s in (0, 1)]

    rs1 = scatters()
    ag1 = [Gather(hf, rows_of, s) for s in (0, 1)]

    def first_norm(s):
        first_sum = rs1[s].result() + out_bias + xf[s, own_rows, :].astype(F32)
        normed, inverse = norm_stats(first_sum)
        normed1[s] = normed
        inv1[s] = jnp.broadcast_to(inverse, (ROWS, 128))
        hf[s, own_rows, :] = (normed * gain1 + offset1).astype(BF)
        ag1[s].send()

    x_own[0].wait()
    x_gather[0].wait()
    project(0)
    w_up.lead(1)
    w_up.follow(0)
    w_up.pair(0, True)
    attend(0)
    w_out.ready()
    out_partial(0)
    rs1[0].to_core()
    w_down.relay()
    w_down.lead(0)
    rs1[0].to_y()
    x_own[1].wait()
    x_gather[1].wait()
    project(1)
    w_down.lead(1)
    w_up.follow(1)
    attend(1)
    w_up.pair(1, True)
    out_partial(1)
    rs1[1].to_core()
    rs1[1].to_y()
    w_up.pair(0, False)
    w_down.pair(0, True)
    w_down.follow(0)
    first_norm(0)
    w_up.pair(1, False)
    w_down.follow(1)
    w_down.pair(0, False)
    first_norm(1)
    w_down.pair(1, True)
    w_down.pair(1, False)
    ag1[0].forward()
    w_up.ready()
    ag1[0].wait()

    def up_bias_of(ci):
        return biases[2 * k + ci, 0:1, pl.ds(al(y, 512), 512)]

    def mlp_up(s):
        rows = hf[s]

        def tile(n, carry):
            cols = pl.ds(al(n, 256), 256)
            weight = wu[:, :, :, cols].reshape(D, 256)
            ci = n // 2
            bias = biases[2 * k + ci, 0:1, pl.ds(pl.multiple_of(y * 512 + (n % 2) * 256, 256), 256)]
            upward = dot(rows, weight, 1, 0) + bias
            share = 0.5 + 0.5 * lax.erf(upward * 0.7071067811865476)
            act[s, :, cols] = (upward * share).astype(BF)
            density = jnp.exp(-0.5 * upward * upward) * 0.3989422804014327
            gelup[s, :, cols] = (share + upward * density).astype(BF)
            return carry

        lax.fori_loop(0, 4, tile, 0)

    def mlp_down(s):
        rows = act[s]

        def tile(n, carry):
            cols = pl.ds(al(n, 256), 256)
            weight = wd[:, :, :, cols].reshape(D, 256)
            part[s, :, cols] = dot(rows, weight, 1, 0).astype(BF)
            return carry

        lax.fori_loop(0, 4, tile, 0)

    rs2 = scatters()
    ag2 = [Gather(gdf, rows_of, s) for s in (0, 1)]
    lo_s, lo_r, lo_l = new("s", 6), new("r", 8), new("l", 2)

    def second_norm(s):
        hidden = normed1[s] * gain1 + offset1
        second_sum = rs2[s].result() + down_bias + hidden
        normed, inverse = norm_stats(second_sum)
        lo[s] = (normed * gain2 + offset2).astype(BF)
        grad = og[s].astype(F32)
        vec_sum[0:1, :] += col_sum(grad * normed)
        vec_sum[1:2, :] += col_sum(grad)
        grad_second = norm_pull(grad, normed, inverse, gain2)
        gsec[s] = grad_second
        rounded = grad_second.astype(BF)
        vec_sum[4:5, :] += col_sum(rounded.astype(F32))
        gdf[s, own_rows, :] = rounded
        ag2[s].send()

    def lo_place(s, row):
        return lo_out.at[s, pl.ds(al(row, ROWS), ROWS), :]

    def lo_part(s, row):
        return lo.at[s, :, pl.ds(al(row, 256), 256)]

    lo_own = [
        pltpu.make_async_copy(lo_part(s, r), lo_place(s, r), ls.at[lo_l + s]) for s in (0, 1)
    ]

    def send_lo(s):
        lo_own[s].start()
        for j in (1, 2, 3):
            row = (r + j) % 4
            copy = remote(
                lo_s + 3 * s + j - 1, lo_r + 4 * s + r, lo_part(s, row), lo_place(s, r), (d, row, c)
            )
            copy.start()
            later(copy)

    mlp_up(0)
    ag1[1].forward()
    relay_og()
    ag1[1].wait()
    mlp_up(1)
    w_down.ready()
    rs1[0].sent()
    mlp_down(0)
    rs2[0].to_core()
    rs1[1].sent()
    rs2[0].to_y()
    mlp_down(1)
    rs2[1].to_core()
    rs2[1].to_y()
    wait_og()
    second_norm(0)
    second_norm(1)
    ag2[0].forward()
    ag2[0].wait()

    class Grad:
        def __init__(
            self, buffer, chunk, both, by_ci, pair_recv, col_recv, place, pair_first, by_row=False
        ):
            self.buffer, self.place, self.pair_first = buffer, place, pair_first
            pair_recvs, col_recvs = pair_recv, col_recv
            self.by_row = by_row
            self.rows = (r, r1, r2, r3)
            self.near_copy, self.far_copy, self.pair_copy = {}, {}, {}
            self.near_add, self.far_add, self.pair_add = {}, {}, {}
            self.own, self.rows_copies = None, {}
            self.chunk = chunk
            self.s3, self.r3, self.l3 = new("s", 7), new("r", 4), new("l")
            for n in range(len(pair_recv)):
                chip = self.rows[n] if by_row else (y if n == 0 else 1 - y)
                pair_recv, col_recv = pair_recvs[n], col_recvs[n]
                if pair_first[n]:
                    pair_src, pair_dst = both(buffer, 1 - p, chip), both(buffer, p, chip)
                    near_src, held = chunk(buffer, p, 1 - ic, chip), chunk(buffer, p, ic, chip)
                else:
                    pair_src, pair_dst = chunk(buffer, 1 - p, ic, chip), chunk(buffer, p, ic, chip)
                    near_src, held = by_ci(buffer, 1 - ic, chip), by_ci(buffer, ic, chip)
                self.pair_copy[n] = remote(new("s"), new("r"), pair_src, pair_recv, x_dev)
                self.near_copy[n] = remote(new("s"), new("r"), near_src, col_recv.at[0], near_dev)
                self.far_copy[n] = remote(new("s"), new("r"), held, col_recv.at[1], far_dev)
                self.pair_add[n] = (pair_dst, pair_recv)
                self.near_add[n] = (held, col_recv.at[0])
                self.far_add[n] = (held, col_recv.at[1])

        def add(self, refs):
            mine, other = refs
            mine[...] = (mine[...].astype(F32) + other[...].astype(F32)).astype(BF)

        def arrival(self, half, yp):
            return self.r3 + 2 * half + yp

        def rows_of_chunk(self, n):
            copies = []
            here, there = d, d + 1 - 2 * p
            if n == 0:
                self.own = pltpu.make_async_copy(self.piece(r), self.place(p, y), ls.at[self.l3])
            if self.by_row:
                targets = [(here, self.rows[n]), (there, self.rows[n])]
                at = 2 * n - 1
                if n == 0:
                    targets, at = targets[1:], 0
            elif n == 0:
                targets = [(here, r1), (there, r), (there, r1)]
                at = 0
            else:
                targets = [(here, r2), (there, r2), (here, r3), (there, r3)]
                at = 3
            for plane, row in targets:
                copies.append(
                    remote(
                        self.s3 + at,
                        self.arrival(p, y),
                        self.piece(row),
                        self.place(p, y),
                        (plane, row, c),
                    )
                )
                at += 1
            return copies

        def begin(self, n):
            first = self.pair_copy[n] if self.pair_first[n] else self.near_copy[n]
            first.start()
            later(first)

        def second(self, n):
            if self.pair_first[n]:
                self.pair_copy[n].wait_recv()
                self.add(self.pair_add[n])
                self.near_copy[n].start()
                later(self.near_copy[n])
            else:
                self.near_copy[n].wait_recv()
                self.add(self.near_add[n])

                @pl.when(jnp.logical_not(is_agg))
                def _():
                    self.far_copy[n].start()

                later(self.far_copy[n], jnp.logical_not(is_agg))

        def third(self, n):
            if self.pair_first[n]:
                self.near_copy[n].wait_recv()
                self.add(self.near_add[n])

                @pl.when(jnp.logical_not(is_agg))
                def _():
                    self.far_copy[n].start()

                later(self.far_copy[n], jnp.logical_not(is_agg))
            else:

                @pl.when(is_agg)
                def _():
                    self.far_copy[n].wait_recv()
                    self.add(self.far_add[n])
                    self.pair_copy[n].start()

                later(self.pair_copy[n], is_agg)

        def to_rows(self, n):
            copies = self.rows_of_chunk(n)

            @pl.when(is_agg)
            def _():
                if self.pair_first[n]:
                    self.far_copy[n].wait_recv()
                    self.add(self.far_add[n])
                else:
                    self.pair_copy[n].wait_recv()
                    self.add(self.pair_add[n])
                if n == 0:
                    self.own.start()
                for copy in copies:
                    copy.start()

            for copy in copies:
                later(copy, is_agg)

        def done(self):
            @pl.when(is_agg)
            def _():
                self.own.wait()

            @pl.when(jnp.logical_not(is_agg))
            def _():
                place = self.place(p, y)
                remote(self.s3, self.arrival(p, y), place, place, core_dev).wait_recv()

            for half, yp in ((p, 1 - y), (1 - p, y), (1 - p, 1 - y)):
                place = self.place(half, yp)
                remote(self.s3, self.arrival(half, yp), place, place, core_dev).wait_recv()

    def rows_both(ref, half, chip):
        return ref.at[pl.ds(2 * chip, 2), half]

    def cols_both(ref, half, chip):
        return ref.at[:, half, :, pl.ds(al(chip, 512), 512)]

    def cols_of_ci(ref, ci, chip):
        return ref.at[ci, :, :, pl.ds(al(chip, 512), 512)]

    def two(ref):
        return [ref.at[0], ref.at[1]]

    def qkv_row_both(ref, half, row):
        return ref.at[row, half]

    g_qkv = Grad(
        gq,
        qkv_row,
        qkv_row_both,
        None,
        [xq.at[n] for n in range(4)],
        [zq.at[n] for n in range(4)],
        lambda half, yp: fin_q.at[half, :, pl.ds(al(yp, 384), 384)],
        (True,) * 4,
        by_row=True,
    )
    g_qkv.piece = lambda row: gq.at[row, p, :, pl.ds(al(ic, 384), 384)]
    g_out = Grad(
        go, out_chunk, cols_both, None, two(xo), two(zo), lambda half, yp: fin_o.at[yp, half], (True, True)
    )
    g_out.piece = lambda row: go.at[ic, p, :, pl.ds(al(row, 256), 256)]
    g_up = Grad(
        gup,
        up_chunk,
        rows_both,
        None,
        two(xu),
        two(zu),
        lambda half, yp: fin_u.at[half, :, pl.ds(al(yp, 512), 512)],
        (True, True),
    )
    g_up.piece = lambda row: gup.at[row, p, :, pl.ds(al(ic, 512), 512)]
    g_down = Grad(
        gd,
        down_chunk,
        cols_both,
        cols_of_ci,
        [xd, xd1],
        [zd, zd1],
        lambda half, yp: fin_d.at[yp, half],
        (True, False),
    )
    g_down.piece = lambda row: gd.at[ic, p, :, pl.ds(al(row, 256), 256)]

    def tokens_by(ref, cols):
        return ref[:, :, cols].reshape(2 * SEQ, cols.size)

    def down_grad(m):
        cols = pl.ds(al(y if m == 0 else 1 - y, 512), 512)

        def tile(n, carry):
            left = tokens_by(act, pl.ds(al(n, 256), 256))
            right = gdf[:, :, cols].reshape(2 * SEQ, 512)
            gd[n // 2, n % 2, :, cols] = dot(left, right, 0, 0).astype(BF)
            return carry

        lax.fori_loop(0, 4, tile, 0)

    def up_grad():
        def tile(n, carry):
            left = tokens_by(hf, pl.ds(al(n, 256), 256))
            gup[n] = (
                dot(left, gu[...].reshape(2 * SEQ, D), 0, 0).astype(BF).reshape(2, 128, D)
            )
            return carry

        lax.fori_loop(0, 4, tile, 0)

    def out_grad():
        left = ctx[...].reshape(2 * SEQ, 256)
        go[...] = dot(left, gaf[...].reshape(2 * SEQ, D), 0, 0).astype(BF).reshape(2, 2, 64, D)

    def qkv_grad():
        def tile(n, carry):
            left = tokens_by(xf, pl.ds(al(n, 256), 256))
            gq[n] = (
                dot(left, gproj[...].reshape(2 * SEQ, 768), 0, 0).astype(BF).reshape(2, 128, 768)
            )
            return carry

        lax.fori_loop(0, 4, tile, 0)

    def pull_act(s):
        rows = gdf[s]

        def tile(n, carry):
            cols = pl.ds(al(n, 256), 256)
            grad = dot(rows, wd[n // 2, n % 2], 1, 1) * gelup[s, :, cols].astype(F32)
            rounded = grad.astype(BF)
            gu[s, :, cols] = rounded
            vec_sum[6:7, cols] += col_sum(rounded.astype(F32))
            return carry

        lax.fori_loop(0, 4, tile, 0)

    def pull_hidden(s):
        rows = gu[s]

        def tile(n, carry):
            weight = wu[n].reshape(256, D)
            part[s, :, pl.ds(al(n, 256), 256)] = dot(rows, weight, 1, 1).astype(BF)
            return carry

        lax.fori_loop(0, 4, tile, 0)

    rs3 = scatters()
    ag3 = [Gather(gaf, rows_of, s) for s in (0, 1)]

    def first_norm_pull(s):
        grad = gsec[s] + rs3[s].result()
        normed = normed1[s]
        vec_sum[2:3, :] += col_sum(grad * normed)
        vec_sum[3:4, :] += col_sum(grad)
        rounded = norm_pull(grad, normed, inv1[s][:, 0:1], gain1).astype(BF)
        vec_sum[5:6, :] += col_sum(rounded.astype(F32))
        gaf[s, own_rows, :] = rounded
        ag3[s].send()

    pull_act(0)
    rs2[0].sent()
    pull_hidden(0)
    rs3[0].to_core()
    ag2[1].forward()
    rs3[0].to_y()
    ag2[1].wait()
    down_grad(0)
    g_down.begin(0)
    down_grad(1)
    g_down.begin(1)
    pull_act(1)
    rs2[1].sent()
    pull_hidden(1)
    rs3[1].to_core()
    rs3[1].to_y()
    first_norm_pull(0)
    up_grad()
    g_up.begin(1)
    g_up.begin(0)
    g_down.second(1)
    g_down.second(0)
    first_norm_pull(1)
    ag3[0].forward()
    ag3[0].wait()

    def pull_attend(s):
        gctx[...] = dot(gaf[s], wo[...].reshape(256, D), 1, 1).astype(BF)
        lane = lax.broadcasted_iota(jnp.int32, (SEQ, 128), 1)
        row = lax.broadcasted_iota(jnp.int32, (128, SEQ), 0)
        scale_factor = float(HEAD) ** (-0.5)

        def pair(ci, carry):
            queries = proj[s, :, columns(ci, 0)]
            keys_in = proj[s, :, columns(ci, 1)]
            values_in = proj[s, :, columns(ci, 2)]
            grad = gctx[:, pl.ds(al(ci, 128), 128)]
            grads_q, grads_k, grads_v = [], [], []
            for h in (0, 1):
                chosen = (lane < HEAD) if h == 0 else (lane >= HEAD)
                masked = jnp.where(chosen, grad, jnp.zeros_like(grad))
                share = probs[s, ci * 2 + h]
                wide = share.astype(F32)
                weighted = wide * dot(values_in, masked, 1, 1)
                total = jnp.sum(weighted, 0, keepdims=True)
                grad_scores = (weighted - wide * total).astype(BF)
                grads_v.append(dot(share, grad, 1, 0))
                grads_k.append(dot(grad_scores, queries, 1, 0))
                grads_q.append(dot(keys_in, grad_scores, 0, 0))
            both_q = jnp.transpose(jnp.where(row < HEAD, grads_q[0], grads_q[1]) * scale_factor)
            both_q = both_q.astype(BF)
            both_v = jnp.where(lane < HEAD, grads_v[0], grads_v[1]).astype(BF)
            both_k = jnp.where(lane < HEAD, grads_k[0], grads_k[1]) * scale_factor
            gproj[s, :, columns(ci, 0)] = both_q
            gproj[s, :, columns(ci, 1)] = both_k.astype(BF)
            gproj[s, :, columns(ci, 2)] = both_v
            at = pl.ds(al(ci, 128), 128)
            vec_sum[7:8, at] += col_sum(both_q.astype(F32))
            at = pl.ds(pl.multiple_of(256 + ci * 128, 128), 128)
            vec_sum[7:8, at] += col_sum(both_v.astype(F32))
            return carry

        lax.fori_loop(0, 2, pair, 0)

    def pull_tokens(s):
        rows = gproj[s]

        def tile(n, carry):
            partf[s, n] = dot(rows, wq[n].reshape(256, 768), 1, 1).astype(BF)
            return carry

        lax.fori_loop(0, 4, tile, 0)

    rs4 = [Scatter(partf, lambda ref, s, row: ref.at[s, row], rscf, ysendf, rsyf, s) for s in (0, 1)]
    tg_l = new("l", 2)
    tg_copy = [pltpu.make_async_copy(tg.at[s], tg_out.at[s], ls.at[tg_l + s]) for s in (0, 1)]

    def tokens_done(s):
        tg[s] = rs4[s].result() + slab_of(gaf, s, r)[...].astype(F32)
        tg_copy[s].start()

    class Sums:
        def __init__(self):
            self.si, self.ri = new("s", 7), new("r", 9)
            self.pair = remote(self.si + 6, self.ri + 8, vec_part, vec_pair, x_dev)

        def to_rows(self):
            vec_rows[r] = vec_sum[...]
            for j in (1, 2, 3):
                copy = remote(
                    self.si + j - 1, self.ri + r, vec_sum, vec_rows.at[r], (d, (r + j) % 4, c)
                )
                copy.start()
                later(copy)

        def to_cols(self):
            for j in (1, 2, 3):
                place = vec_rows.at[(r + j) % 4]
                remote(self.si, self.ri + (r + j) % 4, place, place, core_dev).wait_recv()
            mine = pl.ds(al(r, 256), 256)
            features = vec_rows[0, 0:6, mine] + vec_rows[1, 0:6, mine]
            features = features + vec_rows[2, 0:6, mine] + vec_rows[3, 0:6, mine]
            for j in (0, 1, 2, 3):
                to = (c + j) % 4
                slot = vec_out_parts.at[j]
                slot[0:6, :] = features
                for yp in (0, 1):
                    row = 2 * yp + to // 2
                    ci = to % 2
                    for n in (0, 1):
                        at = pl.ds(pl.multiple_of(ci * 512 + n * 256, 256), 256)
                        slot[6 + 2 * yp + n : 7 + 2 * yp + n, :] = vec_rows[row, 6:7, at]
                        at = pl.ds(pl.multiple_of(n * 256 + ci * 128, 128), 128)
                        slot[10 + n : 11 + n, yp * 128 : yp * 128 + 128] = vec_rows[row, 7:8, at]
                slot[12:16, :] = jnp.zeros((4, 256), F32)
                if j > 0:
                    copy = remote(
                        self.si + 2 + j,
                        self.ri + 4 + c,
                        slot,
                        vec_cols.at[c],
                        (d, r, to),
                    )
                    copy.start()
                    later(copy)

        def to_pair(self):
            total = vec_out_parts[0]
            for j in (1, 2, 3):
                source = (c + j) % 4
                place = vec_cols.at[source]
                remote(self.si, self.ri + 4 + source, place, place, core_dev).wait_recv()
                total = total + vec_cols[source]
            vec_part[...] = total
            self.pair.start()
            later(self.pair)

        def done(self):
            self.pair.wait_recv()
            vec_out[...] = vec_part[...] + vec_pair[...]

    pull_attend(0)
    ag3[1].forward()
    g_up.second(1)
    pull_tokens(0)
    rs4[0].to_core()
    g_down.third(1)
    rs4[0].to_y()
    g_down.third(0)
    ag3[1].wait()
    pull_attend(1)
    sums = Sums()
    sums.to_rows()
    qkv_grad()
    g_qkv.begin(3)
    g_qkv.begin(2)
    g_qkv.begin(1)
    g_up.second(0)
    out_grad()
    g_out.begin(1)
    g_out.begin(0)
    g_qkv.begin(0)
    g_up.third(1)
    pull_tokens(1)
    rs4[1].to_core()
    g_down.to_rows(0)
    rs4[1].to_y()
    send_lo(0)
    send_lo(1)
    g_down.to_rows(1)
    tokens_done(0)
    g_qkv.second(3)
    sums.to_cols()
    g_up.to_rows(1)
    g_qkv.second(2)
    g_up.third(0)
    tokens_done(1)
    g_qkv.third(3)
    g_qkv.second(1)
    g_qkv.third(2)
    g_qkv.to_rows(3)
    g_up.to_rows(0)
    g_out.second(1)
    sums.to_pair()
    g_qkv.third(1)
    g_qkv.to_rows(2)
    g_out.second(0)
    g_qkv.second(0)
    g_out.third(1)
    g_qkv.to_rows(1)
    g_out.third(0)
    g_qkv.third(0)
    g_out.to_rows(1)
    g_out.to_rows(0)
    g_qkv.to_rows(0)
    sums.done()
    g_down.done()
    g_up.done()
    g_out.done()
    g_qkv.done()

    for s in (0, 1):
        rs3[s].sent()
        rs4[s].sent()
        tg_copy[s].wait()
        lo_own[s].wait()
        for j in (1, 2, 3):
            source = (r + j) % 4
            place = lo_place(s, source)
            remote(lo_s, lo_r + 4 * s + source, place, place, core_dev).wait_recv()
    for condition, copy in late:
        if condition is None:
            copy.wait_send()
        else:
            pl.when(condition)(copy.wait_send)


S_SEMS = 320
R_SEMS = 320
L_SEMS = 32


def run_layer(seg, x, og, wq, wo, wu, wd, *vecs):
    any_spec = pl.BlockSpec(memory_space=pl.ANY)
    vmem = pl.BlockSpec(memory_space=pltpu.VMEM)
    out = jax.ShapeDtypeStruct
    outs = [
        (out((2, SEQ, 256), BF), any_spec),
        (out((2, SEQ, 256), F32), any_spec),
        (out((2, 128, 768), BF), any_spec),
        (out((2, 2, 64, 256), BF), any_spec),
        (out((2, 128, D), BF), any_spec),
        (out((2, 2, 256, 256), BF), any_spec),
        (out((16, 256), F32), vmem),
    ]
    full = ((2, SEQ, D), BF)
    scratch = [
        ((2, SEQ), jnp.int32),
        ((8, D), F32),
        ((4, 8, D), F32),
        full,
        ((4, 2, 128, 768), BF),
        ((2, 2, 64, D), BF),
        ((4, 2, 128, D), BF),
        ((2, 2, 256, D), BF),
        ((3, 2, 128, 128), BF),
        ((2, 64, 256), BF),
        ((2, 128, 512), BF),
        ((2, 256, 256), BF),
        ((2, SEQ, 768), BF),
        ((2, 4, SEQ, SEQ), BF),
        ((2, SEQ, 256), BF),
        ((SEQ, SEQ), F32),
        full,
        ((2, 2, ROWS, D), BF),
        ((2, ROWS, D), BF),
        ((2, ROWS, D), BF),
        ((2, ROWS, D), F32),
        ((2, ROWS, 128), F32),
        full,
        full,
        full,
        ((2, ROWS, D), BF),
        ((2, ROWS, 256), BF),
        ((2, ROWS, D), BF),
        ((2, ROWS, D), F32),
        full,
        full,
        full,
        ((SEQ, 256), BF),
        ((2, SEQ, 768), BF),
        ((2, 4, SEQ, 256), BF),
        ((2, 2, SEQ, 256), BF),
        ((2, SEQ, 256), BF),
        ((2, SEQ, 256), BF),
        ((2, SEQ, 256), F32),
        ((4, 2, 128, 768), BF),
        ((2, 2, 64, D), BF),
        ((4, 2, 128, D), BF),
        ((2, 2, 256, D), BF),
        ((4, 128, 768), BF),
        ((2, 2, 64, 512), BF),
        ((2, 2, 128, D), BF),
        ((2, 256, 512), BF),
        ((256, 512), BF),
        ((4, 2, 128, 384), BF),
        ((2, 2, 64, 512), BF),
        ((2, 2, 2, 128, 512), BF),
        ((2, 256, 512), BF),
        ((2, 2, 256, 512), BF),
        ((8, D), F32),
        ((4, 8, D), F32),
        ((4, 16, 256), F32),
        ((4, 16, 256), F32),
        ((16, 256), F32),
        ((16, 256), F32),
    ]
    return pl.pallas_call(
        layer_kernel,
        out_shape=[o[0] for o in outs],
        in_specs=[any_spec] * 7 + [vmem] * len(vecs),
        out_specs=[o[1] for o in outs],
        scratch_shapes=[pltpu.VMEM(shape, dtype) for shape, dtype in scratch]
        + [
            pltpu.SemaphoreType.DMA((S_SEMS,)),
            pltpu.SemaphoreType.DMA((R_SEMS,)),
            pltpu.SemaphoreType.DMA((L_SEMS,)),
        ],
        compiler_params=pltpu.CompilerParams(
            collective_id=0, has_side_effects=True, vmem_limit_bytes=62 * 1024 * 1024
        ),
        name="layer",
    )(seg, x, og, wq, wo, wu, wd, *vecs)


def finish_kernel(lo, tg, fq, fo, fu, fd, vec, lo_out, tg_out, q_out, o_out, u_out, d_out, *vectors):
    lo_out[...] = lo[...]
    tg_out[...] = tg[...]
    for yp in (0, 1):
        for n in (0, 1, 2):
            at = yp * 384 + n * 128
            q_out[n, :, yp * 128 : yp * 128 + 128] = fq[:, at : at + 128].astype(F32)
    o_out[...] = fo[...].astype(F32)
    u_out[...] = fu[...].astype(F32)
    d_out[...] = fd[...].astype(F32)
    for n in range(6):
        vectors[n][...] = vec[n : n + 1, :]
    for n in range(4):
        vectors[6][:, n * 256 : n * 256 + 256] = vec[6 + n : 7 + n, :]
    vectors[7][...] = vec[10:12, :]


def finish(*arrays):
    steps = 2
    out = jax.ShapeDtypeStruct

    def rows_spec(shape):
        return pl.BlockSpec((shape[0] // steps, shape[1]), lambda i: (i, 0))

    def whole(shape):
        return pl.BlockSpec(shape, lambda i: (0, 0))

    shapes = [out(arrays[0].shape, BF)] + [out(a.shape, F32) for a in arrays[1:6]]
    vectors = [out((1, 256), F32)] * 6 + [out((1, D), F32), out((2, 256), F32)]
    shapes[2] = out((3, 256, 256), F32)
    out_specs = [rows_spec(a.shape) for a in shapes] + [whole(v.shape) for v in vectors]
    out_specs[2] = pl.BlockSpec((3, 256 // steps, 256), lambda i: (0, i, 0))
    return pl.pallas_call(
        finish_kernel,
        grid=(steps,),
        in_specs=[rows_spec(a.shape) for a in arrays[:6]] + [whole(arrays[6].shape)],
        out_specs=out_specs,
        out_shape=shapes + vectors,
        name="finish",
    )(*arrays)


def shards(
    pairs,
    tokens,
    segments,
    qkv_weight,
    qv_bias,
    out_weight,
    out_bias,
    norm1_gain,
    norm1_bias,
    up_weight,
    up_bias,
    down_weight,
    down_bias,
    norm2_gain,
    norm2_bias,
    out_grad,
):
    lo, tg, fin_q, fin_o, fin_u, fin_d, vec = run_layer(
        segments,
        tokens.reshape(2, SEQ, 256),
        out_grad.reshape(2, SEQ, 256),
        qkv_weight.transpose(1, 0, 2).reshape(3, 2, 128, 256),
        out_weight.reshape(2, 2, 64, 256),
        up_weight.reshape(2, 128, D),
        down_weight.reshape(2, 2, 256, 256),
        up_bias.reshape(1, D),
        qv_bias,
        out_bias.reshape(1, D),
        norm1_gain.reshape(1, D),
        norm1_bias.reshape(1, D),
        down_bias.reshape(1, D),
        norm2_gain.reshape(1, D),
        norm2_bias.reshape(1, D),
    )
    grads = (fin_q, fin_o, fin_u, fin_d, vec)
    if pairs is not None:
        grads = lax.psum(grads, "dp", axis_index_groups=pairs)
    fin_q, fin_o, fin_u, fin_d, vec = grads
    results = finish(
        lo.reshape(2 * SEQ, 256),
        tg.reshape(2 * SEQ, 256),
        fin_q.reshape(256, 768),
        fin_o.reshape(256, 256),
        fin_u.reshape(256, D),
        fin_d.reshape(D, 256),
        vec,
    )
    layer_out, tokens_grad, qkv_grad, out_grad_w, up_grad, down_grad = results[:6]
    n2_gain, n2_bias, n1_gain, n1_bias, down_b, out_b, up_b, qv_b = results[6:]
    return (
        layer_out,
        tokens_grad,
        qkv_grad.transpose(1, 0, 2),
        qv_b,
        out_grad_w,
        out_b.reshape(256),
        n1_gain.reshape(256),
        n1_bias.reshape(256),
        up_grad,
        up_b.reshape(D),
        down_grad,
        down_b.reshape(256),
        n2_gain.reshape(256),
        n2_bias.reshape(256),
    )


def solution(mesh):
    placed = (
        P(("dp", "col"), "row"),
        P(("dp", "row"), None),
        P("row", None, "col"),
        P(None, "col"),
        P("col", "row"),
        P(),
        P(),
        P(),
        P("row", "col"),
        P("col"),
        P("col", "row"),
        P(),
        P(),
        P(),
        P(("dp", "col"), "row"),
    )
    dp = mesh.shape["dp"]
    pairs = None
    if dp > 2:
        pairs = [list(range(0, dp, 2)), list(range(1, dp, 2))]
    return jax.shard_map(
        functools.partial(shards, pairs),
        mesh=mesh,
        in_specs=placed,
        out_specs=(
            P(("dp", "col"), "row"),
            P(("dp", "col"), "row"),
            P("row", None, "col"),
            P(None, "col"),
            P("col", "row"),
            P("row"),
            P("row"),
            P("row"),
            P("row", "col"),
            P("col"),
            P("col", "row"),
            P("row"),
            P("row"),
            P("row"),
        ),
        check_vma=False,
    )
```
